32 devices in a mesh: grp: 2 (over y), space: 4 (over z), tm: 2 (over x), sub: 2 (over core).
Axes of the slice: x: 2, y: 2, z: 4, core: 2. Of those that a mesh axis runs over, the one named last changes fastest.
Arguments:
- sink_modes: bfloat16 [8, 128, 2, 12, 1024], P(('grp', 'tm'), None, None, None, ('space', 'sub')), parts along dimension 0, may hold values from -6 to 6
- source_modes: bfloat16 [8, 128, 2, 12, 1024], P(('grp', 'tm'), None, None, None, ('space', 'sub')), parts along dimension 0, may hold values from -6 to 6
- gamma_index: int32 [8], replicated, may hold values from 0 to 15
- momenta: int32 [8, 3], replicated, may hold values from -2 to 2
- pattern: int32 [4, 1024], P('tm', ('space', 'sub')), may hold values from 0 to 3
- time_pairs: int32 [4, 2], P('tm'), may hold values from 0 to 3
Outputs:
- meson: float32 [8, 8, 2, 128, 128], P(('grp', 'tm'), None, None, ('space', 'sub')), parts along dimension 0
- products: float32 [8, 8, 2, 128, 128], P(('grp', 'tm'), None, None, ('space', 'sub')), parts along dimension 0
The draws below stay inside these ranges and needn't reach their ends.
There are 2 independent parts, one for each index of `grp`. The reference program is written for one: setup_inputs(seed, part) draws one part's arguments, and reference() takes and returns one part's arrays. A program takes and returns all parts, laid end to end along the dimension named above; an argument that names none is the same for every part. Nothing has to cross between parts.
All inputs are finite; a program needn't handle non-finite values.
Results may differ from the reference program's by a relative error of at most 0.0039.
Values sent between devices are 32-bit elements; how exact they have to be, the bound alone decides.
No kernel may reach another device: no remote copies, remote signals or barrier semaphores. Data moves between devices by JAX's collectives and lax.ppermute only.
A program may use at most 128 MiB of HBM per device.

```python
import math
import jax
import jax.numpy as jnp
import numpy as np
from jax import lax

NMODE = 128
SC = 12
LAT = 96
NINS = 8
SITES = 1024
TS = 4
PAIRS = 4


def place_ends(values, stream_key, low, top_value):
    longest = values.shape.index(max(values.shape))
    spots = []
    for shift in (0, 1):
        where = [jax.random.randint(jax.random.fold_in(stream_key, axis), (), 0, length) for axis, length in enumerate(values.shape)]
        where[longest] = (where[longest] + shift) % values.shape[longest]
        spots.append(tuple(where))
    return values.at[spots[0]].set(low).at[spots[1]].set(top_value)


def shard_levels(stream_key, dims, shards, low, top_value):
    level, own = 1.0, jax.random.fold_in(stream_key, 6)
    for position, shards_of in shards:
        heights = jnp.exp(jax.random.uniform(jax.random.fold_in(own, position), (shards_of,), jnp.float32, low / len(shards), top_value / len(shards)))
        level = level * jnp.repeat(heights, dims[position] // shards_of).reshape([-1 if axis == position else 1 for axis in range(len(dims))])
    return level


def centred(key, extent, width, reach, cuts=(), kind=jnp.bfloat16):
    values = width * jax.random.normal(key, extent, jnp.float32)
    if cuts:
        values = values * shard_levels(key, extent, cuts, -0.22, 0.18)
    return jnp.clip(values, -reach, reach).astype(kind)


def setup_inputs(seed: int = 0, part: int = 0) -> dict:
    keys = jax.random.split(jax.random.key(seed), 7)
    part_keys = jax.random.split(jax.random.fold_in(keys[6], part), 7)
    sink_modes = centred(part_keys[0], (TS, NMODE, 2, SC, SITES), 1.0, 6.0, ((0, 2), (4, 8)))
    source_modes = centred(part_keys[1], (TS, NMODE, 2, SC, SITES), 1.0, 6.0, ((0, 2), (4, 8)))
    gamma_index = place_ends(jax.random.randint(keys[2], (NINS,), 0, 16), jax.random.fold_in(keys[2], 1), 0, 15).astype(jnp.int32)
    momenta = place_ends(jax.random.randint(keys[3], (NINS, 3), -2, 3), jax.random.fold_in(keys[3], 1), -2, 2).astype(jnp.int32)
    pattern = place_ends(jax.random.randint(keys[4], (TS, SITES), 0, 4), jax.random.fold_in(keys[4], 1), 0, 3).astype(jnp.int32)
    time_pairs = place_ends(jax.random.randint(keys[5], (PAIRS, 2), 0, TS), jax.random.fold_in(keys[5], 1), 0, TS - 1).astype(jnp.int32)
    return {"sink_modes": sink_modes, "source_modes": source_modes, "gamma_index": gamma_index, "momenta": momenta, "pattern": pattern, "time_pairs": time_pairs}


def block_matrix(upper_left, upper_right, lower_left, lower_right):
    upper_rows = np.concatenate([upper_left, upper_right], axis=1)
    lower_rows = np.concatenate([lower_left, lower_right], axis=1)
    return np.concatenate([upper_rows, lower_rows], axis=0)

def build_gammas():
    sigmas = [np.array([[0, 1], [1, 0]], dtype=complex), np.array([[0, -1j], [1j, 0]], dtype=complex), np.array([[1, 0], [0, -1]], dtype=complex)]
    zero_block = np.zeros((2, 2), dtype=complex)
    identity_two = np.eye(2, dtype=complex)
    gammas = [block_matrix(zero_block, 1j * sigma_one, -1j * sigma_one, zero_block) for sigma_one in sigmas]
    gammas.append(block_matrix(zero_block, identity_two, identity_two, zero_block))
    tables = []
    for subset in range(16):
        product = np.eye(4, dtype=complex)
        for factor_index in range(4):
            if subset >> factor_index & 1:
                product = product @ gammas[factor_index]
        tables.append(product)
    tables = np.stack(tables)
    return np.stack([tables.real, tables.imag]).astype(np.float32)

def site_coords(site_index):
    coord_x = jnp.zeros_like(site_index)
    coord_y = jnp.zeros_like(site_index)
    coord_z = jnp.zeros_like(site_index)
    for level in range(6):
        weight = 2 ** level
        coord_x = coord_x + site_index // 8 ** level % 2 * weight
        coord_y = coord_y + site_index // (2 * 8 ** level) % 2 * weight
        coord_z = coord_z + site_index // (4 * 8 ** level) % 2 * weight
    return (coord_x, coord_y, coord_z)

def insert_field(mode_field, gamma_choice, momentum_row, pattern_row, slot, first_site):
    highest = lax.Precision.HIGHEST
    nmode, site_count = (mode_field.shape[0], mode_field.shape[-1])
    selector = (jnp.arange(16, dtype=jnp.int32) == gamma_choice).astype(jnp.float32)
    gamma_pair = jnp.tensordot(selector, jnp.asarray(build_gammas(), dtype=jnp.float32), axes=([0], [1]), precision=highest)
    spinor = mode_field.astype(jnp.float32).reshape(nmode, 2, 4, mode_field.shape[2] // 4, site_count)
    real_in, imag_in = (spinor[:, 0], spinor[:, 1])
    real_out = jnp.einsum('ab,nbcx->nacx', gamma_pair[0], real_in, precision=highest) - jnp.einsum('ab,nbcx->nacx', gamma_pair[1], imag_in, precision=highest)
    imag_out = jnp.einsum('ab,nbcx->nacx', gamma_pair[0], imag_in, precision=highest) + jnp.einsum('ab,nbcx->nacx', gamma_pair[1], real_in, precision=highest)
    site_index = first_site + jnp.arange(site_count, dtype=jnp.int32)
    coord_x, coord_y, coord_z = site_coords(site_index)
    wave_number = (momentum_row[0] * coord_x + momentum_row[1] * coord_y + momentum_row[2] * coord_z) % LAT
    phase_angle = wave_number.astype(jnp.float32) * (2.0 * math.pi / LAT)
    keep_mask = (pattern_row == slot).astype(jnp.float32)
    cos_part = jnp.cos(phase_angle) * keep_mask
    sine_part = jnp.sin(phase_angle) * keep_mask
    rot_real = (real_out * cos_part - imag_out * sine_part).astype(jnp.bfloat16)
    rot_imag = (real_out * sine_part + imag_out * cos_part).astype(jnp.bfloat16)
    return (rot_real.reshape(nmode, -1), rot_imag.reshape(nmode, -1))

def stack_rhs(rot_real, rot_imag):
    upper_rows = jnp.concatenate([rot_real, rot_imag], axis=1)
    lower_rows = jnp.concatenate([rot_imag, -rot_real], axis=1)
    return jnp.concatenate([upper_rows, lower_rows], axis=0)

def meson_block(sink_flat, rot_real, rot_imag):
    nmode = sink_flat.shape[0]
    result = lax.dot_general(sink_flat, stack_rhs(rot_real, rot_imag), (((1,), (1,)), ((), ())), preferred_element_type=jnp.float32)
    return jnp.stack([result[:, :nmode], result[:, nmode:]])

def two_time(left_factor, right_factor):
    highest = lax.Precision.HIGHEST
    real_part = jnp.einsum('qgik,qgkj->qgij', left_factor[:, :, 0], right_factor[:, :, 0], precision=highest) - jnp.einsum('qgik,qgkj->qgij', left_factor[:, :, 1], right_factor[:, :, 1], precision=highest)
    imag_part = jnp.einsum('qgik,qgkj->qgij', left_factor[:, :, 0], right_factor[:, :, 1], precision=highest) + jnp.einsum('qgik,qgkj->qgij', left_factor[:, :, 1], right_factor[:, :, 0], precision=highest)
    return jnp.stack([real_part, imag_part], axis=2) / math.sqrt(right_factor.shape[-1])

def reference(sink_modes, source_modes, gamma_index, momenta, pattern, time_pairs):
    norm_scale = 1.0 / math.sqrt(3 * SITES)
    blocks = []
    for slice_index in range(TS):
        sink_flat = sink_modes[slice_index].reshape(NMODE, -1)
        row_blocks = []
        for insertion in range(NINS):
            rot_real, rot_imag = insert_field(source_modes[slice_index], gamma_index[insertion], momenta[insertion], pattern[slice_index], insertion % 4, 0)
            row_blocks.append(norm_scale * meson_block(sink_flat, rot_real, rot_imag))
        blocks.append(jnp.stack(row_blocks))
    meson = jnp.stack(blocks)
    products = two_time(meson[time_pairs[:, 0]], meson[time_pairs[:, 1]])
    return (meson, products)
```

```python
import functools
import math

import jax
import jax.numpy as jnp
import numpy as np
from jax import lax
from jax.experimental import pallas as pl
from jax.experimental.pallas import tpu as pltpu
from jax.sharding import PartitionSpec as P

LAT = 96
F32 = jnp.float32
BF16 = jnp.bfloat16
VMEM_LIMIT = 48 * 2**20


def build_gammas():
    sigmas = [
        np.array([[0, 1], [1, 0]], dtype=complex),
        np.array([[0, -1j], [1j, 0]], dtype=complex),
        np.array([[1, 0], [0, -1]], dtype=complex),
    ]
    zero, one = np.zeros((2, 2), dtype=complex), np.eye(2, dtype=complex)
    gammas = [np.block([[zero, 1j * s], [-1j * s, zero]]) for s in sigmas]
    gammas.append(np.block([[zero, one], [one, zero]]))
    tables = []
    for subset in range(16):
        product = np.eye(4, dtype=complex)
        for factor in range(4):
            if subset >> factor & 1:
                product = product @ gammas[factor]
        tables.append(product)
    return tables


def gamma_codes():
    words = [0, 0, 0, 0]
    for index, table in enumerate(build_gammas()):
        flip = gamma_flip(index)
        for row in range(4):
            entry = table[row, row ^ flip]
            power = [k for k in range(4) if abs(entry - 1j**k) < 1e-6]
            assert len(power) == 1 and np.count_nonzero(table[row]) == 1
            words[index // 4] |= power[0] << (8 * (index % 4) + 2 * row)
    return [word - 2**32 if word >= 2**31 else word for word in words]


def gamma_flip(index):
    b1, b2, b3, b4 = (index & 1, (index >> 1) & 1, (index >> 2) & 1, (index >> 3) & 1)
    return (b1 ^ b2) | ((b1 ^ b2 ^ b3 ^ b4) << 1)


def column(values):
    row = lax.broadcasted_iota(jnp.int32, (len(values), 1), 0)
    out = jnp.zeros((len(values), 1), jnp.int32)
    for index, value in enumerate(values):
        out = jnp.where(row == index, value, out)
    return out


def site_coords(site):
    coords = []
    for axis in range(3):
        total = jnp.zeros_like(site)
        for level in range(6):
            total = total + (((site >> (3 * level + axis)) & 1) << level)
        coords.append(total)
    return coords


def meson_kernel(
    order, batch, sink_ref, source_ref, gamma_ref, momenta_ref, pattern_ref, *refs, time
):
    outs, (sink_mat, source_rows, stage, phases, rotated) = refs[:-5], refs[-5:]
    rows, sites = sink_ref.shape
    nmode = outs[0].shape[1]
    per_mode = rows // nmode
    comps = per_mode // 2
    colours = comps // 4
    insertions = order()
    slots = len(insertions)

    first_site = (
        lax.axis_index("space") * lax.axis_size("sub") + lax.axis_index("sub")
    ) * sites
    site = lax.broadcasted_iota(jnp.int32, (slots, sites), 1) + first_site
    coords = site_coords(site)
    wave = jnp.zeros_like(site)
    for axis in range(3):
        wave = wave + coords[axis] * column([momenta_ref[axis, g] for g in insertions])
    laps = jnp.floor((wave.astype(F32) + 0.5) * (1.0 / LAT)).astype(jnp.int32)
    wave = wave - LAT * laps
    angle = wave.astype(F32) * (2.0 * math.pi / LAT)
    keep = jnp.where(
        pattern_ref[time : time + 1, :] == column([lax.rem(g, 4) for g in insertions]), 1.0, 0.0
    )
    phases[0] = jnp.cos(angle) * keep
    phases[1] = jnp.sin(angle) * keep

    stage[...] = sink_ref[...].astype(F32)
    for comp in range(comps):
        at = comp * 2 * sites
        real = stage[pl.ds(2 * comp, nmode, stride=per_mode), :].astype(BF16)
        imag = stage[pl.ds(2 * comp + 1, nmode, stride=per_mode), :].astype(BF16)
        sink_mat[0:nmode, at : at + sites] = real
        sink_mat[0:nmode, at + sites : at + 2 * sites] = imag
        sink_mat[nmode:, at : at + sites] = -imag
        sink_mat[nmode:, at + sites : at + 2 * sites] = real
    stage[...] = source_ref[...].astype(F32)
    for comp in range(comps):
        for part in range(2):
            source_rows[comp, part] = stage[pl.ds(2 * comp + part, nmode, stride=per_mode), :]

    words = gamma_codes()
    for slot, g in enumerate(insertions):
        index = gamma_ref[g]
        word = jnp.int32(words[3])
        for k in (2, 1, 0):
            word = jnp.where(index < 4 * (k + 1), jnp.int32(words[k]), word)
        code = word >> (8 * (index & 3))
        flip = gamma_flip(index)
        buffer = slot // batch % 2
        base = slot % batch * nmode
        cos_row, sin_row = phases[0, slot : slot + 1, :], phases[1, slot : slot + 1, :]
        for spin in range(4):
            power = (code >> (2 * spin)) & 3
            real_unit = jnp.where(power == 0, 1.0, jnp.where(power == 2, -1.0, 0.0))
            imag_unit = jnp.where(power == 1, 1.0, jnp.where(power == 3, -1.0, 0.0))
            cos_now = real_unit * cos_row - imag_unit * sin_row
            sin_now = real_unit * sin_row + imag_unit * cos_row
            taken = (flip ^ spin) * colours
            for colour in range(colours):
                real = source_rows[taken + colour, 0]
                imag = source_rows[taken + colour, 1]
                at = (spin * colours + colour) * 2 * sites
                rotated[buffer, base : base + nmode, at : at + sites] = (
                    real * cos_now - imag * sin_now
                ).astype(BF16)
                rotated[buffer, base : base + nmode, at + sites : at + 2 * sites] = (
                    real * sin_now + imag * cos_now
                ).astype(BF16)
        if slot % batch == batch - 1:
            block = lax.dot_general(
                rotated[buffer],
                sink_mat[...],
                (((1,), (1,)), ((), ())),
                preferred_element_type=F32,
            )
            for k in range(batch):
                where = slot - batch + 1 + k
                per_out = slots // len(outs)
                outs[where // per_out][where % per_out] = block[k * nmode : (k + 1) * nmode]


def meson_partial(sink, source, gamma_index, momenta, pattern, time, nmode, order, slots, outs):
    _, rows, sites = sink.shape
    batch = slots // 2 if slots % 2 == 0 else slots
    comps = rows // nmode // 2
    field = pl.BlockSpec((None, rows, sites), lambda i: (time, 0, 0))
    smem = pl.BlockSpec(memory_space=pltpu.SMEM)
    whole = pl.BlockSpec(pattern.shape, lambda i: (0, 0))
    shape = (slots // outs, nmode, 2 * nmode)
    flops = 2 * slots * nmode * 2 * nmode * rows // nmode * sites
    return pl.pallas_call(
        functools.partial(meson_kernel, order, batch, time=time),
        grid=(1,),
        in_specs=[field, field, smem, smem, whole],
        out_specs=[pl.BlockSpec(shape, lambda i: (0, 0, 0))] * outs,
        out_shape=[jax.ShapeDtypeStruct(shape, F32)] * outs,
        scratch_shapes=[
            pltpu.VMEM((2 * nmode, comps * 2 * sites), BF16),
            pltpu.VMEM((comps, 2, nmode, sites), F32),
            pltpu.VMEM((rows, sites), F32),
            pltpu.VMEM((2, slots, sites), F32),
            pltpu.VMEM((2, batch * nmode, comps * 2 * sites), BF16),
        ],
        compiler_params=pltpu.CompilerParams(vmem_limit_bytes=VMEM_LIMIT),
        cost_estimate=pl.CostEstimate(
            flops=flops, bytes_accessed=4 * rows * sites + 8 * slots * nmode * nmode, transcendentals=0
        ),
        name="meson_blocks",
    )(sink, source, gamma_index, momenta, pattern)


def add_kernel(keep_ref, got_ref, *outs):
    for slot, out in enumerate(outs):
        out[...] = keep_ref[slot] + got_ref[slot]


def add_units(keep, got):
    units = keep.shape[0]
    return pl.pallas_call(
        add_kernel,
        out_shape=[jax.ShapeDtypeStruct(keep.shape[1:], F32)] * units,
        compiler_params=pltpu.CompilerParams(vmem_limit_bytes=VMEM_LIMIT),
        cost_estimate=pl.CostEstimate(
            flops=keep.size, bytes_accessed=12 * keep.size, transcendentals=0
        ),
        name="add_cores",
    )(keep, got)


def sum_kernel(scale, first_ref, *refs):
    terms, out = refs[:-1], refs[-1]
    total = first_ref[...]
    for term in terms:
        total = total + term[...]
    out[...] = total * scale


def sum_units(terms, scale):
    size = terms[0].size
    return pl.pallas_call(
        functools.partial(sum_kernel, scale),
        out_shape=jax.ShapeDtypeStruct(terms[0].shape, F32),
        cost_estimate=pl.CostEstimate(
            flops=4 * size, bytes_accessed=20 * size, transcendentals=0
        ),
        name="sum_chips",
    )(*terms)


def write_rows(matrix, lane, row_count, spaces, subs, outs, staging):
    nmode = matrix.shape[0]
    z, core = lax.axis_index("space"), lax.axis_index("sub")
    for part in range(2):
        staging[part] = matrix[:, part * nmode : (part + 1) * nmode].T
    for c in range(subs):
        for s in range(spaces):
            start = pl.multiple_of(((z ^ s) * subs + (core ^ c)) * row_count, row_count)
            for part in range(2):
                outs[c * spaces + s][lane, part] = staging[part, pl.ds(start, row_count), :]


def split_kernel(spaces, subs, times, *refs):
    fields, outs, staging = refs[:times], refs[times:-1], refs[-1]
    row_count = outs[0].shape[2]
    for time in range(times):
        write_rows(fields[time][...], time, row_count, spaces, subs, outs, staging.at[time])


def split_rows(fields, spaces, subs):
    nmode, times = fields[0].shape[0], len(fields)
    groups = spaces * subs
    shape = (times, 2, nmode // groups, nmode)
    return pl.pallas_call(
        functools.partial(split_kernel, spaces, subs, times),
        out_shape=[jax.ShapeDtypeStruct(shape, F32)] * groups,
        scratch_shapes=[pltpu.VMEM((times, 2, nmode, nmode), F32)],
        cost_estimate=pl.CostEstimate(
            flops=0, bytes_accessed=16 * times * nmode * nmode, transcendentals=0
        ),
        name="split_rows",
    )(*fields)


def product_kernel(spaces, subs, times, tms, pairs_ref, *refs):
    fields, outs, (held, staging) = refs[: times * tms], refs[times * tms : -2], refs[-2:]
    nmode = fields[0].shape[0]
    row_count = outs[0].shape[2]
    mine = lax.axis_index("tm")
    for other in range(tms):
        for time in range(times):
            held[(mine ^ other) * times + time] = fields[other * times + time][...]
    for pair in range(pairs_ref.shape[0]):
        left, right = held[pairs_ref[pair, 0]], held[pairs_ref[pair, 1]]
        swapped = jnp.concatenate([-left[:, nmode:], left[:, :nmode]], axis=1)
        result = lax.dot_general(
            right,
            jnp.concatenate([left, swapped], axis=0),
            (((1,), (0,)), ((), ())),
            preferred_element_type=F32,
            precision=lax.Precision.HIGHEST,
        ) * (1.0 / math.sqrt(nmode))
        write_rows(result, pair, row_count, spaces, subs, outs, staging.at[pair])


def product_rows(time_pairs, fields, spaces, subs, tms):
    nmode, times, pairs = fields[0].shape[0], len(fields) // tms, time_pairs.shape[0]
    groups = spaces * subs
    shape = (pairs, 2, nmode // groups, nmode)
    return pl.pallas_call(
        functools.partial(product_kernel, spaces, subs, times, tms),
        in_specs=[pl.BlockSpec(memory_space=pltpu.SMEM)]
        + [pl.BlockSpec(memory_space=pltpu.VMEM)] * len(fields),
        out_shape=[jax.ShapeDtypeStruct(shape, F32)] * groups,
        scratch_shapes=[
            pltpu.VMEM((times * tms, nmode, 2 * nmode), F32),
            pltpu.VMEM((pairs, 2, nmode, nmode), F32),
        ],
        compiler_params=pltpu.CompilerParams(vmem_limit_bytes=VMEM_LIMIT),
        cost_estimate=pl.CostEstimate(
            flops=8 * pairs * nmode**3, bytes_accessed=32 * nmode * nmode * times, transcendentals=0
        ),
        name="products",
    )(time_pairs, *fields)


def join_kernel(spaces, subs, *refs):
    blocks, out = refs[:-1], refs[-1]
    z, core = lax.axis_index("space"), lax.axis_index("sub")
    for c in range(subs):
        for s in range(spaces):
            out[:, (z ^ s) * subs + (core ^ c)] = blocks[c * spaces + s][...]


def join_blocks(blocks, spaces, subs):
    shape = blocks[0].shape
    return pl.pallas_call(
        functools.partial(join_kernel, spaces, subs),
        out_shape=jax.ShapeDtypeStruct((shape[0], len(blocks)) + shape[1:], F32),
        cost_estimate=pl.CostEstimate(
            flops=0, bytes_accessed=8 * len(blocks) * blocks[0].size, transcendentals=0
        ),
        name="join_blocks",
    )(*blocks)


def swap(value, axis, distance):
    size = lax.axis_size(axis)
    return lax.ppermute(value, axis, [(i, i ^ distance) for i in range(size)])


def spread(blocks, spaces, subs):
    got = list(blocks)
    for s in reversed(range(spaces)):
        for c in reversed(range(subs)):
            if s or c:
                got[c * spaces + s] = swap(blocks[c * spaces + s], ("space", "sub"), s * subs + c)
    return got


def own_insertions(spaces, subs):
    z, core = lax.axis_index("space"), lax.axis_index("sub")
    return [
        (z ^ s) * subs + (core ^ c) for c in reversed(range(subs)) for s in range(spaces)
    ]


def by_owner(sink, source, gamma_index, momenta, pattern, time_pairs, nmode, times, scale):
    spaces, subs, tms = (lax.axis_size(name) for name in ("space", "sub", "tm"))
    order = functools.partial(own_insertions, spaces, subs)
    units = []
    for time in range(times):
        away, keep = meson_partial(
            sink, source, gamma_index, momenta, pattern, time, nmode, order, spaces * subs, 2
        )
        units.append((keep, swap(away, "sub", 1)))
    sums = []
    for keep, got in units:
        parts = list(add_units(keep, got))
        sums.append(
            parts[:1] + [swap(parts[s], "space", s) for s in reversed(range(1, spaces))]
        )
    fields, others = [], []
    for terms in sums:
        fields.append(sum_units(terms, scale))
        others.append(swap(fields[-1], "tm", 1))
    meson_blocks = spread(split_rows(fields, spaces, subs), spaces, subs)
    product_blocks = spread(
        product_rows(time_pairs, fields + others, spaces, subs, tms), spaces, subs
    )
    meson = join_blocks(meson_blocks, spaces, subs)
    products = join_blocks(product_blocks, spaces, subs)
    return meson, products


def by_rows(sink, source, gamma_index, momenta, pattern, time_pairs, nmode, times, scale):
    axes = ("space", "sub")
    highest = lax.Precision.HIGHEST
    insertions = gamma_index.shape[0]
    partial = jnp.stack(
        [
            meson_partial(
                sink,
                source,
                gamma_index,
                momenta,
                pattern,
                time,
                nmode,
                lambda: list(range(insertions)),
                insertions,
                1,
            )[0]
            for time in range(times)
        ]
    )
    partial = partial.reshape(times, insertions, nmode, 2, nmode).transpose(0, 1, 3, 4, 2)
    meson = lax.psum_scatter(partial * scale, axes, scatter_dimension=3, tiled=True)
    rows = lax.all_gather(meson, "tm", axis=0, tiled=True)
    whole = lax.all_gather(rows, axes, axis=3, tiled=True)
    left, right = rows[time_pairs[:, 0]], whole[time_pairs[:, 1]]

    def multiply(a, b):
        return jnp.einsum("qgik,qgkj->qgij", a, b, precision=highest)

    real = multiply(left[:, :, 0], right[:, :, 0]) - multiply(left[:, :, 1], right[:, :, 1])
    imag = multiply(left[:, :, 0], right[:, :, 1]) + multiply(left[:, :, 1], right[:, :, 0])
    return meson, jnp.stack([real, imag], axis=2) / math.sqrt(nmode)


def local(sink_modes, source_modes, gamma_index, momenta, pattern, time_pairs):
    times, nmode, _, comps, sites = sink_modes.shape
    spaces, subs, tms = (lax.axis_size(name) for name in ("space", "sub", "tm"))

    def as_rows(modes):
        return modes.transpose(0, 1, 3, 2, 4).reshape(times, nmode * comps * 2, sites)

    owners = (
        spaces * subs == gamma_index.shape[0]
        and spaces & (spaces - 1) == 0
        and subs == 2
        and tms == 2
    )
    plan = by_owner if owners else by_rows
    scale = 1.0 / math.sqrt(3 * sites * spaces * subs)
    return plan(
        as_rows(sink_modes),
        as_rows(source_modes),
        gamma_index,
        momenta.T,
        pattern,
        time_pairs,
        nmode,
        times,
        scale,
    )


def solution(mesh):
    rows = P(("grp", "tm"), None, None, None, ("space", "sub"))
    in_specs = (rows, rows, P(), P(), P("tm", ("space", "sub")), P("tm", None))
    out_specs = (P(("grp", "tm"), None, None, ("space", "sub"), None),) * 2
    return jax.shard_map(local, mesh=mesh, in_specs=in_specs, out_specs=out_specs, check_vma=False)
```

```python
import functools
import math

import jax
import jax.numpy as jnp
import numpy as np
from jax import lax
from jax.experimental import pallas as pl
from jax.experimental.pallas import tpu as pltpu
from jax.sharding import PartitionSpec as P

LAT = 96
CLASSES = 4
F32 = jnp.float32
BF16 = jnp.bfloat16
VMEM_LIMIT = 16 * 2**20
SMALL_LIMIT = 4 * 2**20


def build_gammas():
    sigmas = [
        np.array([[0, 1], [1, 0]], dtype=complex),
        np.array([[0, -1j], [1j, 0]], dtype=complex),
        np.array([[1, 0], [0, -1]], dtype=complex),
    ]
    zero, one = np.zeros((2, 2), dtype=complex), np.eye(2, dtype=complex)
    gammas = [np.block([[zero, 1j * s], [-1j * s, zero]]) for s in sigmas]
    gammas.append(np.block([[zero, one], [one, zero]]))
    tables = []
    for subset in range(16):
        product = np.eye(4, dtype=complex)
        for factor in range(4):
            if subset >> factor & 1:
                product = product @ gammas[factor]
        tables.append(product)
    return tables


def gamma_codes():
    words = [0, 0, 0, 0]
    for index, table in enumerate(build_gammas()):
        flip = gamma_flip(index)
        for row in range(4):
            entry = table[row, row ^ flip]
            power = [k for k in range(4) if abs(entry - 1j**k) < 1e-6]
            assert len(power) == 1 and np.count_nonzero(table[row]) == 1
            words[index // 4] |= power[0] << (8 * (index % 4) + 2 * row)
    return [word - 2**32 if word >= 2**31 else word for word in words]


def gamma_flip(index):
    b1, b2, b3, b4 = (index & 1, (index >> 1) & 1, (index >> 2) & 1, (index >> 3) & 1)
    return (b1 ^ b2) | ((b1 ^ b2 ^ b3 ^ b4) << 1)


def site_coords(site):
    coords = []
    for axis in range(3):
        total = jnp.zeros_like(site)
        for level in range(6):
            total = total + (((site >> (3 * level + axis)) & 1) << level)
        coords.append(total)
    return coords


def wave_phases(insertions, momenta_ref, pattern_row):
    sites = pattern_row.shape[1]
    fours = insertions // CLASSES
    first_site = (
        lax.axis_index("space") * lax.axis_size("sub") + lax.axis_index("sub")
    ) * sites
    site = lax.broadcasted_iota(jnp.int32, (1, sites), 1) + first_site
    coords = site_coords(site)
    rows = []
    for four in range(fours):
        wave = jnp.zeros_like(site)
        for axis in range(3):
            chosen = jnp.zeros_like(site)
            for kind in range(CLASSES):
                chosen = jnp.where(
                    pattern_row == kind, momenta_ref[axis, four * CLASSES + kind], chosen
                )
            wave = wave + coords[axis] * chosen
        laps = jnp.floor((wave.astype(F32) + 0.5) * (1.0 / LAT)).astype(jnp.int32)
        rows.append((wave - LAT * laps).astype(F32) * (2.0 * math.pi / LAT))
    angle = jnp.concatenate(rows, axis=0)
    return jnp.cos(angle), jnp.sin(angle)


def multiply_slots(
    insertions, slots, gamma_ref, pattern_row, sink_mat, turned, buffers, out
):
    _, comps, _, nmode, sites = turned.shape
    colours = comps // 4
    words = gamma_codes()
    parts = len(buffers)
    per_part = comps // parts
    plan = []
    for slot in slots:
        g = insertions[slot]
        index = gamma_ref[g]
        word = jnp.int32(words[3])
        for step in (2, 1, 0):
            word = jnp.where(index < 4 * (step + 1), jnp.int32(words[step]), word)
        code = word >> (8 * (index & 3))
        mask = jnp.where(pattern_row == lax.rem(g, CLASSES), 1.0, 0.0)
        rows = []
        for spin in range(4):
            power = (code >> (2 * spin)) & 3
            real_sign = jnp.where((power == 0) | (power == 3), 1.0, -1.0)
            imag_sign = jnp.where(power < 2, 1.0, -1.0)
            rows.append(
                (
                    power & 1,
                    (gamma_flip(index) ^ spin) * colours,
                    (mask * real_sign).astype(BF16),
                    (mask * imag_sign).astype(BF16),
                )
            )
        plan.append((g // CLASSES, rows))
    for part in range(parts):
        buffer = buffers[part]
        for k, (four, rows) in enumerate(plan):
            base = k * nmode
            for step in range(per_part):
                comp = part * per_part + step
                odd, taken, real_row, imag_row = rows[comp // colours]
                source = taken + comp % colours
                at = step * 2 * sites
                buffer[base : base + nmode, at : at + sites] = (
                    turned[four, source, odd] * real_row
                )
                buffer[base : base + nmode, at + sites : at + 2 * sites] = (
                    turned[four, source, 1 - odd] * imag_row
                )
        width = per_part * 2 * sites
        block = lax.dot_general(
            buffer[...],
            sink_mat[:, part * width : (part + 1) * width],
            (((1,), (1,)), ((), ())),
            preferred_element_type=F32,
        ).reshape(out.shape)
        out[...] = block if part == 0 else out[...] + block


def first_kernel(
    order,
    time,
    slots,
    chunks,
    sink_hbm,
    source_hbm,
    gamma_hbm,
    momenta_hbm,
    pattern_hbm,
    out,
    sink_mat,
    turned,
    sink_raw,
    source_raw,
    sink_stage,
    source_stage,
    gamma_ref,
    momenta_ref,
    pattern_ref,
    small_sems,
    big_sems,
    *buffers,
):
    rows, sites = sink_raw.shape
    fours, _, _, nmode, _ = turned.shape
    per_mode = rows // nmode
    comps = per_mode // 2
    insertions = order()
    small = [
        pltpu.make_async_copy(src, dst, small_sems.at[k])
        for k, (src, dst) in enumerate(
            [(momenta_hbm, momenta_ref), (pattern_hbm, pattern_ref), (gamma_hbm, gamma_ref)]
        )
    ]
    for copy in small:
        copy.start()
    height = rows // chunks
    big = []
    for which, (src, dst) in enumerate([(sink_hbm, sink_raw), (source_hbm, source_raw)]):
        for k in range(chunks):
            part = pl.ds(k * height, height)
            copy = pltpu.make_async_copy(
                src.at[time, part], dst.at[part], big_sems.at[which * chunks + k]
            )
            copy.start()
            big.append(copy)
    for copy in small:
        copy.wait()
    pattern_row = pattern_ref[time : time + 1, :]
    cosine, sine = wave_phases(fours * CLASSES, momenta_ref, pattern_row)

    for k in range(chunks):
        part = slice(k * height, (k + 1) * height)
        big[k].wait()
        sink_stage[part] = sink_raw[part].astype(F32)
    for comp in range(comps):
        at = comp * 2 * sites
        real = sink_stage[pl.ds(2 * comp, nmode, stride=per_mode), :].astype(BF16)
        imag = sink_stage[pl.ds(2 * comp + 1, nmode, stride=per_mode), :].astype(BF16)
        sink_mat[0:nmode, at : at + sites] = real
        sink_mat[0:nmode, at + sites : at + 2 * sites] = imag
        sink_mat[nmode:, at : at + sites] = -imag
        sink_mat[nmode:, at + sites : at + 2 * sites] = real
    for k in range(chunks):
        part = slice(k * height, (k + 1) * height)
        big[chunks + k].wait()
        source_stage[part] = source_raw[part].astype(F32)
    for comp in range(comps):
        real = source_stage[pl.ds(2 * comp, nmode, stride=per_mode), :]
        imag = source_stage[pl.ds(2 * comp + 1, nmode, stride=per_mode), :]
        for four in range(fours):
            cos_row, sin_row = cosine[four : four + 1], sine[four : four + 1]
            turned[four, comp, 0] = (real * cos_row - imag * sin_row).astype(BF16)
            turned[four, comp, 1] = (real * sin_row + imag * cos_row).astype(BF16)
    multiply_slots(insertions, slots, gamma_ref, pattern_row, sink_mat, turned, buffers, out)


def block_cost(slots, nmode, depth):
    return pl.CostEstimate(
        flops=4 * slots * nmode * nmode * depth,
        bytes_accessed=8 * nmode * depth,
        transcendentals=0,
    )


def product_buffers(slots, nmode, depth):
    parts = 2
    return [pltpu.VMEM((slots * nmode, depth // parts), BF16)] * parts


def first_blocks(sink, source, gamma_index, momenta, pattern, time, nmode, order, slots):
    _, rows, sites = sink.shape
    comps = rows // nmode // 2
    depth = comps * 2 * sites
    chunks = 4 if rows % 64 == 0 else 1
    fours = gamma_index.shape[0] // CLASSES
    return pl.pallas_call(
        functools.partial(first_kernel, order, time, slots, chunks),
        in_specs=[pl.BlockSpec(memory_space=pltpu.HBM)] * 5,
        out_shape=[
            jax.ShapeDtypeStruct((len(slots), nmode, 2 * nmode), F32),
            jax.ShapeDtypeStruct((2 * nmode, depth), BF16),
            jax.ShapeDtypeStruct((fours, comps, 2, nmode, sites), BF16),
        ],
        scratch_shapes=[
            pltpu.VMEM((rows, sites), BF16),
            pltpu.VMEM((rows, sites), BF16),
            pltpu.VMEM((rows, sites), F32),
            pltpu.VMEM((rows, sites), F32),
            pltpu.SMEM(gamma_index.shape, jnp.int32),
            pltpu.SMEM(momenta.shape, jnp.int32),
            pltpu.VMEM(pattern.shape, jnp.int32),
            pltpu.SemaphoreType.DMA((3,)),
            pltpu.SemaphoreType.DMA((2 * chunks,)),
        ]
        + product_buffers(len(slots), nmode, depth),
        compiler_params=pltpu.CompilerParams(vmem_limit_bytes=VMEM_LIMIT),
        cost_estimate=block_cost(len(slots), nmode, depth),
        name="first_blocks",
    )(sink, source, gamma_index, momenta, pattern)


def later_kernel(
    order,
    time,
    slots,
    gamma_hbm,
    pattern_hbm,
    sink_mat,
    turned,
    out,
    gamma_ref,
    pattern_ref,
    sems,
    *buffers,
):
    copies = [
        pltpu.make_async_copy(gamma_hbm, gamma_ref, sems.at[0]),
        pltpu.make_async_copy(pattern_hbm, pattern_ref, sems.at[1]),
    ]
    for copy in copies:
        copy.start()
    for copy in copies:
        copy.wait()
    pattern_row = pattern_ref[time : time + 1, :]
    multiply_slots(order(), slots, gamma_ref, pattern_row, sink_mat, turned, buffers, out)


def later_blocks(gamma_index, pattern, sink_mat, turned, time, order, slots):
    nmode, depth = turned.shape[3], sink_mat.shape[1]
    return pl.pallas_call(
        functools.partial(later_kernel, order, time, slots),
        in_specs=[pl.BlockSpec(memory_space=pltpu.HBM)] * 2
        + [pl.BlockSpec(memory_space=pltpu.VMEM)] * 2,
        out_shape=jax.ShapeDtypeStruct((len(slots), nmode, 2 * nmode), F32),
        scratch_shapes=[
            pltpu.SMEM(gamma_index.shape, jnp.int32),
            pltpu.VMEM(pattern.shape, jnp.int32),
            pltpu.SemaphoreType.DMA((2,)),
        ]
        + product_buffers(len(slots), nmode, depth),
        compiler_params=pltpu.CompilerParams(vmem_limit_bytes=VMEM_LIMIT),
        cost_estimate=block_cost(len(slots), nmode, depth),
        name="later_blocks",
    )(gamma_index, pattern, sink_mat, turned)


def add_kernel(keep_ref, got_ref, *outs):
    for slot, out in enumerate(outs):
        out[...] = keep_ref[slot] + got_ref[slot]


def add_units(keep, got):
    units = keep.shape[0]
    return pl.pallas_call(
        add_kernel,
        out_shape=[jax.ShapeDtypeStruct(keep.shape[1:], F32)] * units,
        compiler_params=pltpu.CompilerParams(vmem_limit_bytes=SMALL_LIMIT),
        cost_estimate=pl.CostEstimate(
            flops=keep.size, bytes_accessed=12 * keep.size, transcendentals=0
        ),
        name="add_cores",
    )(keep, got)


def sum_kernel(scale, first_ref, *refs):
    terms, out = refs[:-1], refs[-1]
    total = first_ref[...]
    for term in terms:
        total = total + term[...]
    out[...] = total * scale


def sum_units(terms, scale):
    size = terms[0].size
    return pl.pallas_call(
        functools.partial(sum_kernel, scale),
        out_shape=jax.ShapeDtypeStruct(terms[0].shape, F32),
        cost_estimate=pl.CostEstimate(
            flops=4 * size, bytes_accessed=20 * size, transcendentals=0
        ),
        compiler_params=pltpu.CompilerParams(vmem_limit_bytes=SMALL_LIMIT),
        name="sum_chips",
    )(*terms)


def write_rows(matrix, lane, spaces, subs, outs, staging):
    nmode, row_count = matrix.shape[0], outs[0].shape[3]
    z, core = lax.axis_index("space"), lax.axis_index("sub")
    for part in range(2):
        staging[part] = matrix[:, part * nmode : (part + 1) * nmode].T
    for c in range(subs):
        for s in range(spaces):
            start = pl.multiple_of(((z ^ s) * subs + (core ^ c)) * row_count, row_count)
            for part in range(2):
                outs[c][s, lane, part] = staging[part, pl.ds(start, row_count), :]


def split_kernel(spaces, subs, times, *refs):
    fields, outs, staging = refs[:times], refs[times:-1], refs[-1]
    for time in range(times):
        write_rows(fields[time][...], time, spaces, subs, outs, staging.at[time])


def split_rows(fields, spaces, subs):
    nmode, times = fields[0].shape[0], len(fields)
    groups = spaces * subs
    shape = (spaces, times, 2, nmode // groups, nmode)
    return pl.pallas_call(
        functools.partial(split_kernel, spaces, subs, times),
        out_shape=[jax.ShapeDtypeStruct(shape, F32)] * subs,
        scratch_shapes=[pltpu.VMEM((times, 2, nmode, nmode), F32)],
        cost_estimate=pl.CostEstimate(
            flops=0, bytes_accessed=16 * times * nmode * nmode, transcendentals=0
        ),
        compiler_params=pltpu.CompilerParams(vmem_limit_bytes=SMALL_LIMIT),
        name="split_rows",
    )(*fields)


def product_kernel(spaces, subs, times, tms, pairs_ref, *refs):
    fields, outs, (held, staging) = refs[: times * tms], refs[times * tms : -2], refs[-2:]
    nmode = fields[0].shape[0]
    mine = lax.axis_index("tm")
    for other in range(tms):
        for time in range(times):
            held[(mine ^ other) * times + time] = fields[other * times + time][...]
    for pair in range(pairs_ref.shape[0]):
        left, right = held[pairs_ref[pair, 0]], held[pairs_ref[pair, 1]]
        swapped = jnp.concatenate([-left[:, nmode:], left[:, :nmode]], axis=1)
        result = lax.dot_general(
            right,
            jnp.concatenate([left, swapped], axis=0),
            (((1,), (0,)), ((), ())),
            preferred_element_type=F32,
            precision=lax.Precision.HIGHEST,
        ) * (1.0 / math.sqrt(nmode))
        write_rows(result, pair, spaces, subs, outs, staging.at[pair])


def product_rows(time_pairs, fields, spaces, subs, tms):
    nmode, times, pairs = fields[0].shape[0], len(fields) // tms, time_pairs.shape[0]
    groups = spaces * subs
    shape = (spaces, pairs, 2, nmode // groups, nmode)
    return pl.pallas_call(
        functools.partial(product_kernel, spaces, subs, times, tms),
        in_specs=[pl.BlockSpec(memory_space=pltpu.SMEM)]
        + [pl.BlockSpec(memory_space=pltpu.VMEM)] * len(fields),
        out_shape=[jax.ShapeDtypeStruct(shape, F32)] * subs,
        scratch_shapes=[
            pltpu.VMEM((times * tms, nmode, 2 * nmode), F32),
            pltpu.VMEM((pairs, 2, nmode, nmode), F32),
        ],
        compiler_params=pltpu.CompilerParams(vmem_limit_bytes=SMALL_LIMIT),
        cost_estimate=pl.CostEstimate(
            flops=8 * pairs * nmode**3, bytes_accessed=32 * nmode * nmode * times, transcendentals=0
        ),
        name="products",
    )(time_pairs, *fields)


def pair_kernel(keep_ref, got_ref, *outs):
    for s, out in enumerate(outs):
        out[0] = keep_ref[s]
        out[1] = got_ref[s]


def pair_cores(keep, got):
    shape = keep.shape
    return pl.pallas_call(
        pair_kernel,
        out_shape=[jax.ShapeDtypeStruct((2,) + shape[1:], F32)] * shape[0],
        compiler_params=pltpu.CompilerParams(vmem_limit_bytes=SMALL_LIMIT),
        cost_estimate=pl.CostEstimate(
            flops=0, bytes_accessed=16 * keep.size, transcendentals=0
        ),
        name="pair_cores",
    )(keep, got)


def join_kernel(spaces, subs, *refs):
    blocks, out = refs[:-1], refs[-1]
    z, core = lax.axis_index("space"), lax.axis_index("sub")
    for s in range(spaces):
        for c in range(subs):
            out[:, (z ^ s) * subs + (core ^ c)] = blocks[s][c]


def join_blocks(blocks, spaces, subs):
    shape = blocks[0].shape
    return pl.pallas_call(
        functools.partial(join_kernel, spaces, subs),
        out_shape=jax.ShapeDtypeStruct((shape[1], spaces * subs) + shape[2:], F32),
        compiler_params=pltpu.CompilerParams(vmem_limit_bytes=SMALL_LIMIT),
        cost_estimate=pl.CostEstimate(
            flops=0, bytes_accessed=8 * len(blocks) * blocks[0].size, transcendentals=0
        ),
        name="join_blocks",
    )(*blocks)


def swap(value, axis, distance):
    size = lax.axis_size(axis)
    return lax.ppermute(value, axis, [(i, i ^ distance) for i in range(size)])


def chip_order(spaces):
    return sorted(range(1, spaces), key=lambda s: (s & (s - 1) != 0, s == 1, -s))


def swap_chips(parts, spaces):
    got = list(parts)
    for s in chip_order(spaces):
        got[s] = swap(parts[s], "space", s)
    return got


def spread(keep, away, spaces, subs):
    parts = pair_cores(keep, swap(away, "sub", 1))
    return join_blocks(swap_chips(parts, spaces), spaces, subs)


def own_insertions(spaces, subs):
    z, core = lax.axis_index("space"), lax.axis_index("sub")
    return [(z ^ s) * subs + (core ^ c) for c in range(subs) for s in range(spaces)]


def by_owner(sink, source, gamma_index, momenta, pattern, time_pairs, nmode, times, scale):
    spaces, subs, tms = (lax.axis_size(name) for name in ("space", "sub", "tm"))
    order = functools.partial(own_insertions, spaces, subs)
    mine, other = list(range(spaces)), list(range(spaces, 2 * spaces))
    fields, others = [], []
    sums = []
    for time in range(times):
        if sums:
            gamma_index, sums[-1] = lax.optimization_barrier((gamma_index, sums[-1]))
        away, *laid = first_blocks(
            sink, source, gamma_index, momenta, pattern, time, nmode, order, other
        )
        got = swap(away, "sub", 1)
        keep = later_blocks(gamma_index, pattern, *laid, time, order, mine)
        sums.append(add_units(keep, got))
    for parts in sums:
        fields.append(sum_units(swap_chips(parts, spaces), scale))
        others.append(swap(fields[-1], "tm", 1))
    keep, away = split_rows(fields, spaces, subs)
    meson = spread(keep, away, spaces, subs)
    keep, away = product_rows(time_pairs, fields + others, spaces, subs, tms)
    products = spread(keep, away, spaces, subs)
    return meson, products


def by_rows(sink, source, gamma_index, momenta, pattern, time_pairs, nmode, times, scale):
    axes = ("space", "sub")
    highest = lax.Precision.HIGHEST
    insertions = gamma_index.shape[0]
    partial = jnp.stack(
        [
            first_blocks(
                sink,
                source,
                gamma_index,
                momenta,
                pattern,
                time,
                nmode,
                lambda: list(range(insertions)),
                list(range(insertions)),
            )[0]
            for time in range(times)
        ]
    )
    partial = partial.reshape(times, insertions, nmode, 2, nmode).transpose(0, 1, 3, 4, 2)
    meson = lax.psum_scatter(partial * scale, axes, scatter_dimension=3, tiled=True)
    rows = lax.all_gather(meson, "tm", axis=0, tiled=True)
    whole = lax.all_gather(rows, axes, axis=3, tiled=True)
    left, right = rows[time_pairs[:, 0]], whole[time_pairs[:, 1]]

    def multiply(a, b):
        return jnp.einsum("qgik,qgkj->qgij", a, b, precision=highest)

    real = multiply(left[:, :, 0], right[:, :, 0]) - multiply(left[:, :, 1], right[:, :, 1])
    imag = multiply(left[:, :, 0], right[:, :, 1]) + multiply(left[:, :, 1], right[:, :, 0])
    return meson, jnp.stack([real, imag], axis=2) / math.sqrt(nmode)


def local(sink_modes, source_modes, gamma_index, momenta, pattern, time_pairs):
    times, nmode, _, comps, sites = sink_modes.shape
    spaces, subs, tms = (lax.axis_size(name) for name in ("space", "sub", "tm"))

    def as_rows(modes):
        return modes.transpose(0, 1, 3, 2, 4).reshape(times, nmode * comps * 2, sites)

    owners = (
        spaces * subs == gamma_index.shape[0]
        and spaces & (spaces - 1) == 0
        and subs == 2
        and tms == 2
    )
    plan = by_owner if owners else by_rows
    arrays = (as_rows(sink_modes), as_rows(source_modes), gamma_index, momenta.T, pattern)
    arrays = [pltpu.with_memory_space_constraint(a, pltpu.HBM) for a in arrays]
    scale = 1.0 / math.sqrt(3 * sites * spaces * subs)
    return plan(*arrays, time_pairs, nmode, times, scale)


def solution(mesh):
    rows = P(("grp", "tm"), None, None, None, ("space", "sub"))
    in_specs = (rows, rows, P(), P(), P("tm", ("space", "sub")), P("tm", None))
    out_specs = (P(("grp", "tm"), None, None, ("space", "sub"), None),) * 2
    return jax.shard_map(local, mesh=mesh, in_specs=in_specs, out_specs=out_specs, check_vma=False)
```

```python
import functools
import math

import jax
import jax.numpy as jnp
import numpy as np
from jax import lax
from jax.experimental import pallas as pl
from jax.experimental.pallas import tpu as pltpu
from jax.sharding import PartitionSpec as P

LAT = 96
CLASSES = 4
F32 = jnp.float32
BF16 = jnp.bfloat16
VMEM_LIMIT = 16 * 2**20
SMALL_LIMIT = 4 * 2**20
LARGE = 10**11


def build_gammas():
    sigmas = [
        np.array([[0, 1], [1, 0]], dtype=complex),
        np.array([[0, -1j], [1j, 0]], dtype=complex),
        np.array([[1, 0], [0, -1]], dtype=complex),
    ]
    zero, one = np.zeros((2, 2), dtype=complex), np.eye(2, dtype=complex)
    gammas = [np.block([[zero, 1j * s], [-1j * s, zero]]) for s in sigmas]
    gammas.append(np.block([[zero, one], [one, zero]]))
    tables = []
    for subset in range(16):
        product = np.eye(4, dtype=complex)
        for factor in range(4):
            if subset >> factor & 1:
                product = product @ gammas[factor]
        tables.append(product)
    return tables


def gamma_codes():
    words = [0, 0, 0, 0]
    for index, table in enumerate(build_gammas()):
        flip = gamma_flip(index)
        for row in range(4):
            entry = table[row, row ^ flip]
            power = [k for k in range(4) if abs(entry - 1j**k) < 1e-6]
            assert len(power) == 1 and np.count_nonzero(table[row]) == 1
            words[index // 4] |= power[0] << (8 * (index % 4) + 2 * row)
    return [word - 2**32 if word >= 2**31 else word for word in words]


def gamma_flip(index):
    b1, b2, b3, b4 = (index & 1, (index >> 1) & 1, (index >> 2) & 1, (index >> 3) & 1)
    return (b1 ^ b2) | ((b1 ^ b2 ^ b3 ^ b4) << 1)


def site_coords(site):
    coords = []
    for axis in range(3):
        total = jnp.zeros_like(site)
        for level in range(6):
            total = total + (((site >> (3 * level + axis)) & 1) << level)
        coords.append(total)
    return coords


def wave_phases(insertions, momenta_ref, pattern_row):
    sites = pattern_row.shape[1]
    fours = insertions // CLASSES
    first_site = (
        lax.axis_index("space") * lax.axis_size("sub") + lax.axis_index("sub")
    ) * sites
    site = lax.broadcasted_iota(jnp.int32, (1, sites), 1) + first_site
    coords = site_coords(site)
    rows = []
    for four in range(fours):
        wave = jnp.zeros_like(site)
        for axis in range(3):
            chosen = jnp.zeros_like(site)
            for kind in range(CLASSES):
                chosen = jnp.where(
                    pattern_row == kind, momenta_ref[axis, four * CLASSES + kind], chosen
                )
            wave = wave + coords[axis] * chosen
        laps = jnp.floor((wave.astype(F32) + 0.5) * (1.0 / LAT)).astype(jnp.int32)
        rows.append((wave - LAT * laps).astype(F32) * (2.0 * math.pi / LAT))
    angle = jnp.concatenate(rows, axis=0)
    return jnp.cos(angle), jnp.sin(angle)


def multiply_slots(
    insertions, slots, gamma_ref, pattern_row, sink_mat, turned, buffers, out
):
    _, comps, _, nmode, sites = turned.shape
    colours = comps // 4
    words = gamma_codes()
    parts = len(buffers)
    per_part = comps // parts
    plan = []
    for slot in slots:
        g = insertions[slot]
        index = gamma_ref[g]
        word = jnp.int32(words[3])
        for step in (2, 1, 0):
            word = jnp.where(index < 4 * (step + 1), jnp.int32(words[step]), word)
        code = word >> (8 * (index & 3))
        mask = jnp.where(pattern_row == lax.rem(g, CLASSES), 1.0, 0.0)
        rows = []
        for spin in range(4):
            power = (code >> (2 * spin)) & 3
            real_sign = jnp.where((power == 0) | (power == 3), 1.0, -1.0)
            imag_sign = jnp.where(power < 2, 1.0, -1.0)
            rows.append(
                (
                    power & 1,
                    (gamma_flip(index) ^ spin) * colours,
                    (mask * real_sign).astype(BF16),
                    (mask * imag_sign).astype(BF16),
                )
            )
        plan.append((g // CLASSES, rows))
    for part in range(parts):
        buffer = buffers[part]
        for k, (four, rows) in enumerate(plan):
            base = k * nmode
            for step in range(per_part):
                comp = part * per_part + step
                odd, taken, real_row, imag_row = rows[comp // colours]
                source = taken + comp % colours
                at = step * 2 * sites
                buffer[base : base + nmode, at : at + sites] = (
                    turned[four, source, odd] * real_row
                )
                buffer[base : base + nmode, at + sites : at + 2 * sites] = (
                    turned[four, source, 1 - odd] * imag_row
                )
        width = per_part * 2 * sites
        block = lax.dot_general(
            buffer[...],
            sink_mat[:, part * width : (part + 1) * width],
            (((1,), (1,)), ((), ())),
            preferred_element_type=F32,
        ).reshape(out.shape)
        out[...] = block if part == 0 else out[...] + block


def first_kernel(
    order,
    time,
    slots,
    chunks,
    sink_hbm,
    source_hbm,
    gamma_hbm,
    momenta_hbm,
    pattern_hbm,
    out,
    sink_mat,
    turned,
    sink_raw,
    source_raw,
    sink_stage,
    source_stage,
    gamma_ref,
    momenta_ref,
    pattern_ref,
    small_sems,
    big_sems,
    *buffers,
):
    rows, sites = sink_raw.shape
    fours, _, _, nmode, _ = turned.shape
    per_mode = rows // nmode
    comps = per_mode // 2
    insertions = order()
    small = [
        pltpu.make_async_copy(src, dst, small_sems.at[k])
        for k, (src, dst) in enumerate(
            [(momenta_hbm, momenta_ref), (pattern_hbm, pattern_ref), (gamma_hbm, gamma_ref)]
        )
    ]
    for copy in small:
        copy.start()
    height = rows // chunks
    big = []
    for which, (src, dst) in enumerate([(sink_hbm, sink_raw), (source_hbm, source_raw)]):
        for k in range(chunks):
            part = pl.ds(k * height, height)
            copy = pltpu.make_async_copy(
                src.at[time, part], dst.at[part], big_sems.at[which * chunks + k]
            )
            copy.start()
            big.append(copy)
    for copy in small:
        copy.wait()
    pattern_row = pattern_ref[time : time + 1, :]
    cosine, sine = wave_phases(fours * CLASSES, momenta_ref, pattern_row)

    for k in range(chunks):
        part = slice(k * height, (k + 1) * height)
        big[k].wait()
        sink_stage[part] = sink_raw[part].astype(F32)
    for comp in range(comps):
        at = comp * 2 * sites
        real = sink_stage[pl.ds(2 * comp, nmode, stride=per_mode), :].astype(BF16)
        imag = sink_stage[pl.ds(2 * comp + 1, nmode, stride=per_mode), :].astype(BF16)
        sink_mat[0:nmode, at : at + sites] = real
        sink_mat[0:nmode, at + sites : at + 2 * sites] = imag
        sink_mat[nmode:, at : at + sites] = -imag
        sink_mat[nmode:, at + sites : at + 2 * sites] = real
    for k in range(chunks):
        part = slice(k * height, (k + 1) * height)
        big[chunks + k].wait()
        source_stage[part] = source_raw[part].astype(F32)
    for comp in range(comps):
        real = source_stage[pl.ds(2 * comp, nmode, stride=per_mode), :]
        imag = source_stage[pl.ds(2 * comp + 1, nmode, stride=per_mode), :]
        for four in range(fours):
            cos_row, sin_row = cosine[four : four + 1], sine[four : four + 1]
            turned[four, comp, 0] = (real * cos_row - imag * sin_row).astype(BF16)
            turned[four, comp, 1] = (real * sin_row + imag * cos_row).astype(BF16)
    multiply_slots(insertions, slots, gamma_ref, pattern_row, sink_mat, turned, buffers, out)


def block_cost(slots, nmode, depth):
    return pl.CostEstimate(
        flops=400 * slots * nmode * nmode * depth,
        bytes_accessed=8 * nmode * depth,
        transcendentals=0,
    )


def product_buffers(slots, nmode, depth):
    parts = 2
    return [pltpu.VMEM((slots * nmode, depth // parts), BF16)] * parts


def first_blocks(sink, source, gamma_index, momenta, pattern, time, nmode, order, slots):
    _, rows, sites = sink.shape
    comps = rows // nmode // 2
    depth = comps * 2 * sites
    chunks = 4 if rows % 64 == 0 else 1
    fours = gamma_index.shape[0] // CLASSES
    return pl.pallas_call(
        functools.partial(first_kernel, order, time, slots, chunks),
        in_specs=[pl.BlockSpec(memory_space=pltpu.HBM)] * 5,
        out_shape=[
            pltpu.VMEM((len(slots), nmode, 2 * nmode), F32),
            pltpu.VMEM((2 * nmode, depth), BF16),
            pltpu.VMEM((fours, comps, 2, nmode, sites), BF16),
        ],
        scratch_shapes=[
            pltpu.VMEM((rows, sites), BF16),
            pltpu.VMEM((rows, sites), BF16),
            pltpu.VMEM((rows, sites), F32),
            pltpu.VMEM((rows, sites), F32),
            pltpu.SMEM(gamma_index.shape, jnp.int32),
            pltpu.SMEM(momenta.shape, jnp.int32),
            pltpu.VMEM(pattern.shape, jnp.int32),
            pltpu.SemaphoreType.DMA((3,)),
            pltpu.SemaphoreType.DMA((2 * chunks,)),
        ]
        + product_buffers(len(slots), nmode, depth),
        compiler_params=pltpu.CompilerParams(vmem_limit_bytes=VMEM_LIMIT),
        cost_estimate=block_cost(len(slots), nmode, depth),
        name="first_blocks",
    )(sink, source, gamma_index, momenta, pattern)


def later_kernel(
    order,
    time,
    slots,
    gamma_hbm,
    pattern_hbm,
    sink_mat,
    turned,
    out,
    gamma_ref,
    pattern_ref,
    sems,
    *buffers,
):
    copies = [
        pltpu.make_async_copy(gamma_hbm, gamma_ref, sems.at[0]),
        pltpu.make_async_copy(pattern_hbm, pattern_ref, sems.at[1]),
    ]
    for copy in copies:
        copy.start()
    for copy in copies:
        copy.wait()
    pattern_row = pattern_ref[time : time + 1, :]
    multiply_slots(order(), slots, gamma_ref, pattern_row, sink_mat, turned, buffers, out)


def later_blocks(gamma_index, pattern, sink_mat, turned, time, order, slots):
    nmode, depth = turned.shape[3], sink_mat.shape[1]
    return pl.pallas_call(
        functools.partial(later_kernel, order, time, slots),
        in_specs=[pl.BlockSpec(memory_space=pltpu.HBM)] * 2
        + [pl.BlockSpec(memory_space=pltpu.VMEM)] * 2,
        out_shape=pltpu.VMEM((len(slots), nmode, 2 * nmode), F32),
        scratch_shapes=[
            pltpu.SMEM(gamma_index.shape, jnp.int32),
            pltpu.VMEM(pattern.shape, jnp.int32),
            pltpu.SemaphoreType.DMA((2,)),
        ]
        + product_buffers(len(slots), nmode, depth),
        compiler_params=pltpu.CompilerParams(vmem_limit_bytes=VMEM_LIMIT),
        cost_estimate=block_cost(len(slots), nmode, depth),
        name="later_blocks",
    )(gamma_index, pattern, sink_mat, turned)


def small_call(kernel, outs, name, *args, flops=1, after=(), scratch=()):
    return pl.pallas_call(
        kernel,
        in_specs=[pl.BlockSpec(memory_space=pltpu.VMEM)] * len(args)
        + [pl.BlockSpec(memory_space=pl.ANY)] * len(after),
        out_shape=outs,
        scratch_shapes=scratch,
        compiler_params=pltpu.CompilerParams(vmem_limit_bytes=SMALL_LIMIT),
        cost_estimate=pl.CostEstimate(flops=flops, bytes_accessed=1, transcendentals=0),
        name=name,
    )(*args, *after)


def add_units(keep, got):
    def kernel(keep_ref, got_ref, *outs):
        for slot, out in enumerate(outs):
            out[...] = keep_ref[slot] + got_ref[slot]

    units, rows, columns = keep.shape
    outs = [pltpu.VMEM((rows, columns), F32)] * units
    return small_call(kernel, outs, "add_cores", keep, got)


def sum_units(terms, scale, after=()):
    def kernel(*refs):
        total = refs[0][...]
        for ref in refs[1 : len(terms)]:
            total = total + ref[...]
        refs[-1][...] = total * scale

    out = pltpu.VMEM(terms[0].shape, F32)
    return small_call(kernel, out, "sum_chips", *terms, after=after)


def write_rows(whole, lane, spaces, subs, cores, outs):
    row_count = outs[0].shape[3]
    z, core = lax.axis_index("space"), lax.axis_index("sub")
    for c, out in zip(cores, outs, strict=True):
        for s in range(spaces):
            start = pl.multiple_of(((z ^ s) * subs + (core ^ c)) * row_count, row_count)
            for part in range(2):
                out[s, lane, part] = whole[part, pl.ds(start, row_count), :]


def turn(matrix, whole):
    nmode = matrix.shape[1] // 2
    for part in range(2):
        whole[part] = matrix[:, part * nmode : (part + 1) * nmode].T


def turn_field(field, after):
    def kernel(field_ref, *refs):
        turn(field_ref[...], refs[-1])

    nmode = field.shape[0]
    out = pltpu.VMEM((2, nmode, nmode), F32)
    return small_call(kernel, out, "turn_field", field, flops=LARGE, after=after)


def split_rows(whole, field, spaces, subs):
    nmode = whole.shape[1]

    def kernel(whole_ref, field_ref, away, keep, staging):
        turn(field_ref[...], staging)
        for lane, source in enumerate((whole_ref, staging)):
            write_rows(source, lane, spaces, subs, [1, 0], [away, keep])

    outs = [pltpu.VMEM((spaces, 2, 2, nmode // (spaces * subs), nmode), F32)] * 2
    scratch = [pltpu.VMEM((2, nmode, nmode), F32)]
    return small_call(kernel, outs, "split_rows", whole, field, scratch=scratch)


def product_kernel(spaces, subs, tms, pairs_ref, *refs):
    fields, (away, whole, held) = refs[:-3], refs[-3:]
    nmode = fields[0].shape[0]
    times = len(fields) // tms
    mine = lax.axis_index("tm")
    for other in range(tms):
        for time in range(times):
            held[(mine ^ other) * times + time] = fields[other * times + time][...]
    for pair in range(pairs_ref.shape[0]):
        left, right = held[pairs_ref[pair, 0]], held[pairs_ref[pair, 1]]
        swapped = jnp.concatenate([-left[:, nmode:], left[:, :nmode]], axis=1)
        result = lax.dot_general(
            right,
            jnp.concatenate([left, swapped], axis=0),
            (((1,), (0,)), ((), ())),
            preferred_element_type=F32,
            precision=lax.Precision.HIGHEST,
        ) * (1.0 / math.sqrt(nmode))
        turn(result, whole.at[pair])
        write_rows(whole.at[pair], pair, spaces, subs, [1], [away])


def product_rows(time_pairs, fields, spaces, subs, tms):
    nmode, pairs = fields[0].shape[0], time_pairs.shape[0]
    shape = (spaces, pairs, 2, nmode // (spaces * subs), nmode)
    return pl.pallas_call(
        functools.partial(product_kernel, spaces, subs, tms),
        in_specs=[pl.BlockSpec(memory_space=pltpu.SMEM)]
        + [pl.BlockSpec(memory_space=pltpu.VMEM)] * len(fields),
        out_shape=[pltpu.VMEM(shape, F32), pltpu.VMEM((pairs, 2, nmode, nmode), F32)],
        scratch_shapes=[pltpu.VMEM((len(fields), nmode, 2 * nmode), F32)],
        compiler_params=pltpu.CompilerParams(vmem_limit_bytes=SMALL_LIMIT),
        cost_estimate=pl.CostEstimate(
            flops=8 * pairs * nmode**3, bytes_accessed=64 * nmode * nmode, transcendentals=0
        ),
        name="products",
    )(time_pairs, *fields)


def keep_rows(whole, spaces, subs):
    lanes, _, nmode, _ = whole.shape

    def kernel(whole_ref, out):
        for lane in range(lanes):
            write_rows(whole_ref.at[lane], lane, spaces, subs, [0], [out])

    out = pltpu.VMEM((spaces, lanes, 2, nmode // (spaces * subs), nmode), F32)
    return small_call(kernel, out, "keep_rows", whole, flops=LARGE)


def pair_cores(keep, got):
    shape = keep.shape

    def kernel(keep_ref, got_ref, *outs):
        for s, out in enumerate(outs):
            out[0] = keep_ref[s]
            out[1] = got_ref[s]

    outs = [pltpu.VMEM((2,) + shape[1:], F32)] * shape[0]
    return small_call(kernel, outs, "pair_cores", keep, got)


def pair_with(near, keep, got):
    shape = keep.shape

    def kernel(near_ref, keep_ref, got_ref, *outs):
        outs[1][0] = near_ref[...]
        for s, out in enumerate(outs):
            out = out.at[1] if s == 1 else out
            out[0] = keep_ref[s]
            out[1] = got_ref[s]

    outs = [
        pltpu.VMEM(((2,) if s == 1 else ()) + (2,) + shape[1:], F32) for s in range(shape[0])
    ]
    return small_call(kernel, outs, "pair_cores", near, keep, got)


def put_blocks(args, places, arrays, spaces, subs, name, flops):
    lanes, _, row_count, nmode = args[0].shape[-4:]
    count = len(arrays)

    def kernel(*refs):
        outs, sems = refs[-1 - count : -1], refs[-1]
        refs = refs[len(given) :]
        z, core = lax.axis_index("space"), lax.axis_index("sub")
        copies = []
        for out, group in zip(outs, places, strict=True):
            for s, operand, index in group:
                block = refs[operand] if index is None else refs[operand].at[index]
                for c in range(subs):
                    for lane in range(lanes):
                        copy = pltpu.make_async_copy(
                            block.at[c, lane],
                            out.at[lane, (z ^ s) * subs + (core ^ c)],
                            sems.at[len(copies)],
                        )
                        copy.start()
                        copies.append(copy)
        for copy in copies:
            copy.wait()

    out = jax.ShapeDtypeStruct((lanes, spaces * subs, 2, row_count, nmode), F32)
    given = [(k, array) for k, array in enumerate(arrays) if array is not None]
    return pl.pallas_call(
        kernel,
        in_specs=[pl.BlockSpec(memory_space=pltpu.HBM)] * len(given)
        + [pl.BlockSpec(memory_space=pltpu.VMEM)] * len(args),
        out_specs=[pl.BlockSpec(memory_space=pltpu.HBM)] * count,
        out_shape=[out] * count,
        input_output_aliases={n: k for n, (k, _) in enumerate(given)},
        scratch_shapes=[pltpu.SemaphoreType.DMA((sum(map(len, places)) * subs * lanes,))],
        compiler_params=pltpu.CompilerParams(vmem_limit_bytes=SMALL_LIMIT),
        cost_estimate=pl.CostEstimate(flops=flops, bytes_accessed=1, transcendentals=0),
        name=name,
    )(*(array for _, array in given), *args)


def swap(value, axis, distance):
    size = lax.axis_size(axis)
    return lax.ppermute(value, axis, [(i, i ^ distance) for i in range(size)])


def own_insertions(spaces, subs):
    z, core = lax.axis_index("space"), lax.axis_index("sub")
    return [(z ^ s) * subs + (core ^ c) for c in range(subs) for s in range(spaces)]


def by_owner(sink, source, gamma_index, momenta, pattern, time_pairs, nmode, times, scale):
    spaces, subs, tms = (lax.axis_size(name) for name in ("space", "sub", "tm"))
    order = functools.partial(own_insertions, spaces, subs)
    mine, other = list(range(spaces)), list(range(spaces, 2 * spaces))

    def blocks(gamma_index, time):
        away, *laid = first_blocks(
            sink, source, gamma_index, momenta, pattern, time, nmode, order, other
        )
        got = swap(away, "sub", 1)
        return later_blocks(gamma_index, pattern, *laid, time, order, mine), got

    def send(own, one, two, three):
        two, three, one = (swap(v, "space", s) for v, s in ((two, 2), (three, 3), (one, 1)))
        return own, one, two, three

    parts = add_units(*blocks(gamma_index, 0))
    gamma_index, parts = lax.optimization_barrier((gamma_index, parts))
    first = send(*parts)
    second = send(*add_units(*blocks(gamma_index, 1)))
    first = sum_units(first, scale)
    first_other = swap(first, "tm", 1)
    whole = turn_field(first, second[1:])
    second = sum_units(second, scale, [first_other, whole])
    second_other = swap(second, "tm", 1)

    away, keep = split_rows(whole, second, spaces, subs)
    meson = pair_cores(keep, swap(away, "sub", 1))
    own, meson_near, two, three = meson
    two, three = swap(two, "space", 2), swap(three, "space", 3)
    fields = [first, second, first_other, second_other]
    away, whole = product_rows(time_pairs, fields, spaces, subs, tms)
    got = swap(away, "sub", 1)
    products = pair_with(meson_near, keep_rows(whole, spaces, subs), got)
    places = [[(0, 0, None), (2, 1, None), (3, 2, None)]]
    (meson,) = put_blocks(
        [own, two, three], places, [None], spaces, subs, "put_early", LARGE
    )
    own, near, two, three = products
    two, three, near = (swap(v, "space", s) for v, s in ((two, 2), (three, 3), (near, 1)))
    places = [[(1, 1, 0)], [(0, 0, None), (1, 1, 1), (2, 2, None), (3, 3, None)]]
    return put_blocks(
        [own, near, two, three], places, [meson, None], spaces, subs, "put_late", 1
    )


def by_rows(sink, source, gamma_index, momenta, pattern, time_pairs, nmode, times, scale):
    axes = ("space", "sub")
    highest = lax.Precision.HIGHEST
    insertions = gamma_index.shape[0]
    partial = jnp.stack(
        [
            first_blocks(
                sink,
                source,
                gamma_index,
                momenta,
                pattern,
                time,
                nmode,
                lambda: list(range(insertions)),
                list(range(insertions)),
            )[0]
            for time in range(times)
        ]
    )
    partial = partial.reshape(times, insertions, nmode, 2, nmode).transpose(0, 1, 3, 4, 2)
    meson = lax.psum_scatter(partial * scale, axes, scatter_dimension=3, tiled=True)
    rows = lax.all_gather(meson, "tm", axis=0, tiled=True)
    whole = lax.all_gather(rows, axes, axis=3, tiled=True)
    left, right = rows[time_pairs[:, 0]], whole[time_pairs[:, 1]]

    def multiply(a, b):
        return jnp.einsum("qgik,qgkj->qgij", a, b, precision=highest)

    real = multiply(left[:, :, 0], right[:, :, 0]) - multiply(left[:, :, 1], right[:, :, 1])
    imag = multiply(left[:, :, 0], right[:, :, 1]) + multiply(left[:, :, 1], right[:, :, 0])
    return meson, jnp.stack([real, imag], axis=2) / math.sqrt(nmode)


def local(sink_modes, source_modes, gamma_index, momenta, pattern, time_pairs):
    times, nmode, _, comps, sites = sink_modes.shape
    spaces, subs, tms = (lax.axis_size(name) for name in ("space", "sub", "tm"))

    def as_rows(modes):
        return modes.transpose(0, 1, 3, 2, 4).reshape(times, nmode * comps * 2, sites)

    owners = (
        (spaces, subs, tms, times) == (4, 2, 2, 2)
        and gamma_index.shape[0] == spaces * subs
        and time_pairs.shape[0] == times
    )
    plan = by_owner if owners else by_rows
    arrays = (as_rows(sink_modes), as_rows(source_modes), gamma_index, momenta.T, pattern)
    arrays = [pltpu.with_memory_space_constraint(a, pltpu.HBM) for a in arrays]
    scale = 1.0 / math.sqrt(3 * sites * spaces * subs)
    return plan(*arrays, time_pairs, nmode, times, scale)


def solution(mesh):
    rows = P(("grp", "tm"), None, None, None, ("space", "sub"))
    in_specs = (rows, rows, P(), P(), P("tm", ("space", "sub")), P("tm", None))
    out_specs = (P(("grp", "tm"), None, None, ("space", "sub"), None),) * 2
    return jax.shard_map(local, mesh=mesh, in_specs=in_specs, out_specs=out_specs, check_vma=False)
```

```python
import functools
import math

import jax
import jax.numpy as jnp
import numpy as np
from jax import lax
from jax.experimental import pallas as pl
from jax.experimental.pallas import tpu as pltpu
from jax.sharding import PartitionSpec as P

LAT = 96
CLASSES = 4
F32 = jnp.float32
BF16 = jnp.bfloat16
VMEM_LIMIT = 16 * 2**20
SMALL_LIMIT = 4 * 2**20
ROUND = ((2, 1, 3), (2, 1, 3))
LARGE = 10**11


def build_gammas():
    sigmas = [
        np.array([[0, 1], [1, 0]], dtype=complex),
        np.array([[0, -1j], [1j, 0]], dtype=complex),
        np.array([[1, 0], [0, -1]], dtype=complex),
    ]
    zero, one = np.zeros((2, 2), dtype=complex), np.eye(2, dtype=complex)
    gammas = [np.block([[zero, 1j * s], [-1j * s, zero]]) for s in sigmas]
    gammas.append(np.block([[zero, one], [one, zero]]))
    tables = []
    for subset in range(16):
        product = np.eye(4, dtype=complex)
        for factor in range(4):
            if subset >> factor & 1:
                product = product @ gammas[factor]
        tables.append(product)
    return tables


def gamma_codes():
    words = [0, 0, 0, 0]
    for index, table in enumerate(build_gammas()):
        flip = gamma_flip(index)
        for row in range(4):
            entry = table[row, row ^ flip]
            power = [k for k in range(4) if abs(entry - 1j**k) < 1e-6]
            assert len(power) == 1 and np.count_nonzero(table[row]) == 1
            words[index // 4] |= power[0] << (8 * (index % 4) + 2 * row)
    return [word - 2**32 if word >= 2**31 else word for word in words]


def gamma_flip(index):
    b1, b2, b3, b4 = (index & 1, (index >> 1) & 1, (index >> 2) & 1, (index >> 3) & 1)
    return (b1 ^ b2) | ((b1 ^ b2 ^ b3 ^ b4) << 1)


def site_coords(site):
    coords = []
    for axis in range(3):
        total = jnp.zeros_like(site)
        for level in range(6):
            total = total + (((site >> (3 * level + axis)) & 1) << level)
        coords.append(total)
    return coords


def wave_phases(insertions, momenta_ref, pattern_row):
    sites = pattern_row.shape[1]
    fours = insertions // CLASSES
    first_site = (
        lax.axis_index("space") * lax.axis_size("sub") + lax.axis_index("sub")
    ) * sites
    site = lax.broadcasted_iota(jnp.int32, (1, sites), 1) + first_site
    coords = site_coords(site)
    rows = []
    for four in range(fours):
        wave = jnp.zeros_like(site)
        for axis in range(3):
            chosen = jnp.zeros_like(site)
            for kind in range(CLASSES):
                chosen = jnp.where(
                    pattern_row == kind, momenta_ref[axis, four * CLASSES + kind], chosen
                )
            wave = wave + coords[axis] * chosen
        laps = jnp.floor((wave.astype(F32) + 0.5) * (1.0 / LAT)).astype(jnp.int32)
        rows.append((wave - LAT * laps).astype(F32) * (2.0 * math.pi / LAT))
    angle = jnp.concatenate(rows, axis=0)
    return jnp.cos(angle), jnp.sin(angle)


def multiply_slots(
    insertions, slots, gamma_ref, pattern_row, sink_mat, turned, buffers, out
):
    _, comps, _, nmode, sites = turned.shape
    colours = comps // 4
    words = gamma_codes()
    parts = len(buffers)
    per_part = comps // parts
    plan = []
    for slot in slots:
        g = insertions[slot]
        index = gamma_ref[g]
        word = jnp.int32(words[3])
        for step in (2, 1, 0):
            word = jnp.where(index < 4 * (step + 1), jnp.int32(words[step]), word)
        code = word >> (8 * (index & 3))
        mask = jnp.where(pattern_row == lax.rem(g, CLASSES), 1.0, 0.0)
        rows = []
        for spin in range(4):
            power = (code >> (2 * spin)) & 3
            real_sign = jnp.where((power == 0) | (power == 3), 1.0, -1.0)
            imag_sign = jnp.where(power < 2, 1.0, -1.0)
            rows.append(
                (
                    power & 1,
                    (gamma_flip(index) ^ spin) * colours,
                    (mask * real_sign).astype(BF16),
                    (mask * imag_sign).astype(BF16),
                )
            )
        plan.append((g // CLASSES, rows))
    for part in range(parts):
        buffer = buffers[part]
        for k, (four, rows) in enumerate(plan):
            base = k * nmode
            for step in range(per_part):
                comp = part * per_part + step
                odd, taken, real_row, imag_row = rows[comp // colours]
                source = taken + comp % colours
                at = step * 2 * sites
                buffer[base : base + nmode, at : at + sites] = (
                    turned[four, source, odd] * real_row
                )
                buffer[base : base + nmode, at + sites : at + 2 * sites] = (
                    turned[four, source, 1 - odd] * imag_row
                )
        width = per_part * 2 * sites
        block = lax.dot_general(
            buffer[...],
            sink_mat[:, part * width : (part + 1) * width],
            (((1,), (1,)), ((), ())),
            preferred_element_type=F32,
        ).reshape(out.shape)
        out[...] = block if part == 0 else out[...] + block


def first_kernel(order, time, slots, chunks, ahead, loaded, waits, *refs):
    sink_src, source_src, gamma_hbm, momenta_hbm, pattern_hbm, *refs = refs
    out, sink_mat, turned, *refs = refs[waits:]
    nexts, refs = (refs[:2], refs[2:]) if ahead else ([], refs)
    sink_stage, source_stage, gamma_ref, momenta_ref, pattern_ref, *refs = refs
    small_sems, big_sems, next_sems, *refs = refs
    raws, buffers = ([sink_src, source_src], refs) if loaded else (refs[:2], refs[2:])
    rows, sites = sink_stage.shape
    fours, _, _, nmode, _ = turned.shape
    per_mode = rows // nmode
    comps = per_mode // 2
    insertions = order()
    height = rows // chunks

    small = [
        pltpu.make_async_copy(src, dst, small_sems.at[k])
        for k, (src, dst) in enumerate(
            [(momenta_hbm, momenta_ref), (pattern_hbm, pattern_ref), (gamma_hbm, gamma_ref)]
        )
    ]
    big, later = [], []
    if not loaded:
        for which, (src, dst) in enumerate(zip((sink_src, source_src), raws)):
            for k in range(chunks):
                part = pl.ds(k * height, height)
                sem = big_sems.at[which * chunks + k]
                big.append(pltpu.make_async_copy(src.at[time, part], dst.at[part], sem))
    for k, (src, dst) in enumerate(zip((sink_src, source_src), nexts)):
        later.append(pltpu.make_async_copy(src.at[time + 1], dst, next_sems.at[k]))
    for copy in small + big + later:
        copy.start()

    def stage(which, dst):
        for k in range(chunks):
            part = slice(k * height, (k + 1) * height)
            if not loaded:
                big[which * chunks + k].wait()
            dst[part] = raws[which][part].astype(F32)

    stage(0, sink_stage)
    for comp in range(comps):
        at = comp * 2 * sites
        real = sink_stage[pl.ds(2 * comp, nmode, stride=per_mode), :].astype(BF16)
        imag = sink_stage[pl.ds(2 * comp + 1, nmode, stride=per_mode), :].astype(BF16)
        sink_mat[0:nmode, at : at + sites] = real
        sink_mat[0:nmode, at + sites : at + 2 * sites] = imag
        sink_mat[nmode:, at : at + sites] = -imag
        sink_mat[nmode:, at + sites : at + 2 * sites] = real
    for copy in small:
        copy.wait()
    pattern_row = pattern_ref[time : time + 1, :]
    cosine, sine = wave_phases(fours * CLASSES, momenta_ref, pattern_row)
    stage(1, source_stage)
    for comp in range(comps):
        real = source_stage[pl.ds(2 * comp, nmode, stride=per_mode), :]
        imag = source_stage[pl.ds(2 * comp + 1, nmode, stride=per_mode), :]
        for four in range(fours):
            cos_row, sin_row = cosine[four : four + 1], sine[four : four + 1]
            turned[four, comp, 0] = (real * cos_row - imag * sin_row).astype(BF16)
            turned[four, comp, 1] = (real * sin_row + imag * cos_row).astype(BF16)
    multiply_slots(insertions, slots, gamma_ref, pattern_row, sink_mat, turned, buffers, out)
    for copy in later:
        copy.wait()


def block_cost(slots, nmode, depth):
    return pl.CostEstimate(
        flops=400 * slots * nmode * nmode * depth,
        bytes_accessed=8 * nmode * depth,
        transcendentals=0,
    )


def product_buffers(slots, nmode, depth):
    parts = 2
    return [pltpu.VMEM((slots * nmode, depth // parts), BF16)] * parts


def first_blocks(modes, small, time, nmode, order, slots, ahead=False, after=()):
    rows, sites = modes[0].shape[-2:]
    loaded = modes[0].ndim == 2
    comps = rows // nmode // 2
    depth = comps * 2 * sites
    chunks = 4 if rows % 64 == 0 else 1
    gamma_index, momenta, pattern = small
    fours = gamma_index.shape[0] // CLASSES
    raw = [pltpu.VMEM((rows, sites), BF16)] * 2
    where = pltpu.VMEM if loaded else pltpu.HBM
    if not loaded:
        modes = in_hbm(modes)
    return pl.pallas_call(
        functools.partial(first_kernel, order, time, slots, chunks, ahead, loaded, len(after)),
        in_specs=[pl.BlockSpec(memory_space=where)] * 2
        + [pl.BlockSpec(memory_space=pltpu.HBM)] * 3
        + [pl.BlockSpec(memory_space=pl.ANY)] * len(after),
        out_shape=[
            pltpu.VMEM((len(slots), nmode, 2 * nmode), F32),
            pltpu.VMEM((2 * nmode, depth), BF16),
            pltpu.VMEM((fours, comps, 2, nmode, sites), BF16),
        ]
        + (raw if ahead else []),
        scratch_shapes=[
            pltpu.VMEM((rows, sites), F32),
            pltpu.VMEM((rows, sites), F32),
            pltpu.SMEM(gamma_index.shape, jnp.int32),
            pltpu.SMEM(momenta.shape, jnp.int32),
            pltpu.VMEM(pattern.shape, jnp.int32),
            pltpu.SemaphoreType.DMA((3,)),
            pltpu.SemaphoreType.DMA((2 * chunks,)),
            pltpu.SemaphoreType.DMA((2,)),
        ]
        + ([] if loaded else raw)
        + product_buffers(len(slots), nmode, depth),
        compiler_params=pltpu.CompilerParams(vmem_limit_bytes=VMEM_LIMIT),
        cost_estimate=block_cost(len(slots), nmode, depth),
        name="first_blocks",
    )(*modes, *in_hbm(small), *after)


def in_hbm(arrays):
    return [pltpu.with_memory_space_constraint(a, pltpu.HBM) for a in arrays]


def later_kernel(order, time, slots, gamma_ref, pattern_ref, sink_mat, turned, out, *buffers):
    pattern_row = pattern_ref[time : time + 1, :]
    multiply_slots(order(), slots, gamma_ref, pattern_row, sink_mat, turned, buffers, out)


def later_blocks(gamma_index, pattern, sink_mat, turned, time, order, slots):
    nmode, depth = turned.shape[3], sink_mat.shape[1]
    return pl.pallas_call(
        functools.partial(later_kernel, order, time, slots),
        in_specs=[pl.BlockSpec(memory_space=pltpu.SMEM)]
        + [pl.BlockSpec(memory_space=pltpu.VMEM)] * 3,
        out_shape=pltpu.VMEM((len(slots), nmode, 2 * nmode), F32),
        scratch_shapes=product_buffers(len(slots), nmode, depth),
        compiler_params=pltpu.CompilerParams(vmem_limit_bytes=VMEM_LIMIT),
        cost_estimate=block_cost(len(slots), nmode, depth),
        name="later_blocks",
    )(gamma_index, pattern, sink_mat, turned)


def small_call(kernel, outs, name, *args, flops=1, after=(), scratch=()):
    return pl.pallas_call(
        kernel,
        in_specs=[pl.BlockSpec(memory_space=pltpu.VMEM)] * len(args)
        + [pl.BlockSpec(memory_space=pl.ANY)] * len(after),
        out_shape=outs,
        scratch_shapes=scratch,
        compiler_params=pltpu.CompilerParams(vmem_limit_bytes=SMALL_LIMIT),
        cost_estimate=pl.CostEstimate(flops=flops, bytes_accessed=1, transcendentals=0),
        name=name,
    )(*args, *after)


def add_units(keep, got):
    def kernel(keep_ref, got_ref, *outs):
        for slot, out in enumerate(outs):
            out[...] = keep_ref[slot] + got_ref[slot]

    units, rows, columns = keep.shape
    outs = [pltpu.VMEM((rows, columns), F32)] * units
    return small_call(kernel, outs, "add_cores", keep, got)


def sum_units(terms, scale, after=()):
    def kernel(*refs):
        total = refs[0][...]
        for ref in refs[1 : len(terms)]:
            total = total + ref[...]
        refs[-1][...] = total * scale

    out = pltpu.VMEM(terms[0].shape, F32)
    return small_call(kernel, out, "sum_chips", *terms, after=after)


def write_rows(whole, lane, spaces, subs, cores, outs):
    row_count = outs[0].shape[3]
    z, core = lax.axis_index("space"), lax.axis_index("sub")
    for c, out in zip(cores, outs, strict=True):
        for s in range(spaces):
            start = pl.multiple_of(((z ^ s) * subs + (core ^ c)) * row_count, row_count)
            for part in range(2):
                out[s, lane, part] = whole[part, pl.ds(start, row_count), :]


def turn(matrix, whole):
    nmode = matrix.shape[1] // 2
    for part in range(2):
        whole[part] = matrix[:, part * nmode : (part + 1) * nmode].T


def turn_field(field, after):
    def kernel(field_ref, *refs):
        turn(field_ref[...], refs[-1])

    nmode = field.shape[0]
    out = pltpu.VMEM((2, nmode, nmode), F32)
    return small_call(kernel, out, "turn_field", field, flops=LARGE, after=after)


def split_rows(whole, field, spaces, subs):
    nmode = whole.shape[1]

    def kernel(whole_ref, field_ref, away, keep, staging):
        turn(field_ref[...], staging)
        for lane, source in enumerate((whole_ref, staging)):
            write_rows(source, lane, spaces, subs, [1, 0], [away, keep])

    outs = [pltpu.VMEM((spaces, 2, 2, nmode // (spaces * subs), nmode), F32)] * 2
    scratch = [pltpu.VMEM((2, nmode, nmode), F32)]
    return small_call(kernel, outs, "split_rows", whole, field, scratch=scratch)


def product_kernel(spaces, subs, tms, pairs_ref, *refs):
    fields, (away, whole, held) = refs[:-3], refs[-3:]
    nmode = fields[0].shape[0]
    times = len(fields) // tms
    mine = lax.axis_index("tm")
    for other in range(tms):
        for time in range(times):
            held[(mine ^ other) * times + time] = fields[other * times + time][...]
    for pair in range(pairs_ref.shape[0]):
        left, right = held[pairs_ref[pair, 0]], held[pairs_ref[pair, 1]]
        swapped = jnp.concatenate([-left[:, nmode:], left[:, :nmode]], axis=1)
        result = lax.dot_general(
            right,
            jnp.concatenate([left, swapped], axis=0),
            (((1,), (0,)), ((), ())),
            preferred_element_type=F32,
            precision=lax.Precision.HIGHEST,
        ) * (1.0 / math.sqrt(nmode))
        turn(result, whole.at[pair])
        write_rows(whole.at[pair], pair, spaces, subs, [1], [away])


def product_rows(time_pairs, fields, spaces, subs, tms):
    nmode, pairs = fields[0].shape[0], time_pairs.shape[0]
    shape = (spaces, pairs, 2, nmode // (spaces * subs), nmode)
    return pl.pallas_call(
        functools.partial(product_kernel, spaces, subs, tms),
        in_specs=[pl.BlockSpec(memory_space=pltpu.SMEM)]
        + [pl.BlockSpec(memory_space=pltpu.VMEM)] * len(fields),
        out_shape=[pltpu.VMEM(shape, F32), pltpu.VMEM((pairs, 2, nmode, nmode), F32)],
        scratch_shapes=[pltpu.VMEM((len(fields), nmode, 2 * nmode), F32)],
        compiler_params=pltpu.CompilerParams(vmem_limit_bytes=SMALL_LIMIT),
        cost_estimate=pl.CostEstimate(
            flops=8 * pairs * nmode**3, bytes_accessed=64 * nmode * nmode, transcendentals=0
        ),
        name="products",
    )(time_pairs, *fields)


def keep_rows(whole, spaces, subs):
    lanes, _, nmode, _ = whole.shape

    def kernel(whole_ref, out):
        for lane in range(lanes):
            write_rows(whole_ref.at[lane], lane, spaces, subs, [0], [out])

    out = pltpu.VMEM((spaces, lanes, 2, nmode // (spaces * subs), nmode), F32)
    return small_call(kernel, out, "keep_rows", whole, flops=LARGE)


def pair_cores(keep, got):
    shape = keep.shape

    def kernel(keep_ref, got_ref, *outs):
        for s, out in enumerate(outs):
            out[0] = keep_ref[s]
            out[1] = got_ref[s]

    outs = [pltpu.VMEM((2,) + shape[1:], F32)] * shape[0]
    return small_call(kernel, outs, "pair_cores", keep, got)


def pair_with(near, keep, got):
    shape = keep.shape

    def kernel(near_ref, keep_ref, got_ref, *outs):
        outs[1][0] = near_ref[...]
        for s, out in enumerate(outs):
            out = out.at[1] if s == 1 else out
            out[0] = keep_ref[s]
            out[1] = got_ref[s]

    outs = [
        pltpu.VMEM(((2,) if s == 1 else ()) + (2,) + shape[1:], F32) for s in range(shape[0])
    ]
    return small_call(kernel, outs, "pair_cores", near, keep, got)


def put_blocks(args, places, arrays, spaces, subs, name, flops):
    lanes, _, row_count, nmode = args[0].shape[-4:]
    count = len(arrays)

    def kernel(*refs):
        outs, sems = refs[-1 - count : -1], refs[-1]
        refs = refs[len(given) :]
        z, core = lax.axis_index("space"), lax.axis_index("sub")
        copies = []
        for out, group in zip(outs, places, strict=True):
            for s, operand, index in group:
                block = refs[operand] if index is None else refs[operand].at[index]
                for c in range(subs):
                    for lane in range(lanes):
                        copy = pltpu.make_async_copy(
                            block.at[c, lane],
                            out.at[lane, (z ^ s) * subs + (core ^ c)],
                            sems.at[len(copies)],
                        )
                        copy.start()
                        copies.append(copy)
        for copy in copies:
            copy.wait()

    out = jax.ShapeDtypeStruct((lanes, spaces * subs, 2, row_count, nmode), F32)
    given = [(k, array) for k, array in enumerate(arrays) if array is not None]
    return pl.pallas_call(
        kernel,
        in_specs=[pl.BlockSpec(memory_space=pltpu.HBM)] * len(given)
        + [pl.BlockSpec(memory_space=pltpu.VMEM)] * len(args),
        out_specs=[pl.BlockSpec(memory_space=pltpu.HBM)] * count,
        out_shape=[out] * count,
        input_output_aliases={n: k for n, (k, _) in enumerate(given)},
        scratch_shapes=[pltpu.SemaphoreType.DMA((sum(map(len, places)) * subs * lanes,))],
        compiler_params=pltpu.CompilerParams(vmem_limit_bytes=SMALL_LIMIT),
        cost_estimate=pl.CostEstimate(flops=flops, bytes_accessed=1, transcendentals=0),
        name=name,
    )(*(array for _, array in given), *args)


def swap(value, axis, distance):
    size = lax.axis_size(axis)
    return lax.ppermute(value, axis, [(i, i ^ distance) for i in range(size)])


def own_insertions(spaces, subs):
    z, core = lax.axis_index("space"), lax.axis_index("sub")
    return [(z ^ s) * subs + (core ^ c) for c in range(subs) for s in range(spaces)]


def by_owner(sink, source, gamma_index, momenta, pattern, time_pairs, nmode, times, scale):
    spaces, subs, tms = (lax.axis_size(name) for name in ("space", "sub", "tm"))
    order = functools.partial(own_insertions, spaces, subs)
    mine, other = list(range(spaces)), list(range(spaces, 2 * spaces))
    small = (gamma_index, momenta, pattern)

    def send(away, laid, time):
        got = swap(away, "sub", 1)
        keep = later_blocks(gamma_index, pattern, *laid, time, order, mine)
        parts = add_units(keep, got)
        return [parts[0]] + [swap(parts[s], "space", s) for s in ROUND[time]]

    away, sink_mat, turned, *modes = first_blocks(
        (sink, source), small, 0, nmode, order, other, ahead=True
    )
    first = send(away, (sink_mat, turned), 0)
    away, sink_mat, turned = first_blocks(modes, small, 1, nmode, order, other, after=first[:1])
    second = send(away, (sink_mat, turned), 1)
    first = sum_units(first, scale)
    first_other = swap(first, "tm", 1)
    whole = turn_field(first, second[1:])
    second = sum_units(second, scale, [first_other, whole])
    second_other = swap(second, "tm", 1)

    away, keep = split_rows(whole, second, spaces, subs)
    meson = pair_cores(keep, swap(away, "sub", 1))
    own, meson_near, two, three = meson
    two, three = swap(two, "space", 2), swap(three, "space", 3)
    fields = [first, second, first_other, second_other]
    away, whole = product_rows(time_pairs, fields, spaces, subs, tms)
    got = swap(away, "sub", 1)
    products = pair_with(meson_near, keep_rows(whole, spaces, subs), got)
    places = [[(0, 0, None), (2, 1, None), (3, 2, None)]]
    (meson,) = put_blocks(
        [own, two, three], places, [None], spaces, subs, "put_early", LARGE
    )
    own, near, two, three = products
    two, three, near = (swap(v, "space", s) for v, s in ((two, 2), (three, 3), (near, 1)))
    places = [[(1, 3, 0)], [(0, 0, None), (1, 3, 1), (2, 2, None), (3, 1, None)]]
    return put_blocks(
        [own, three, two, near], places, [meson, None], spaces, subs, "put_late", 1
    )


def by_rows(sink, source, gamma_index, momenta, pattern, time_pairs, nmode, times, scale):
    axes = ("space", "sub")
    highest = lax.Precision.HIGHEST
    insertions = gamma_index.shape[0]
    partial = jnp.stack(
        [
            first_blocks(
                (sink, source),
                (gamma_index, momenta, pattern),
                time,
                nmode,
                lambda: list(range(insertions)),
                list(range(insertions)),
            )[0]
            for time in range(times)
        ]
    )
    partial = partial.reshape(times, insertions, nmode, 2, nmode).transpose(0, 1, 3, 4, 2)
    meson = lax.psum_scatter(partial * scale, axes, scatter_dimension=3, tiled=True)
    rows = lax.all_gather(meson, "tm", axis=0, tiled=True)
    whole = lax.all_gather(rows, axes, axis=3, tiled=True)
    left, right = rows[time_pairs[:, 0]], whole[time_pairs[:, 1]]

    def multiply(a, b):
        return jnp.einsum("qgik,qgkj->qgij", a, b, precision=highest)

    real = multiply(left[:, :, 0], right[:, :, 0]) - multiply(left[:, :, 1], right[:, :, 1])
    imag = multiply(left[:, :, 0], right[:, :, 1]) + multiply(left[:, :, 1], right[:, :, 0])
    return meson, jnp.stack([real, imag], axis=2) / math.sqrt(nmode)


def local(sink_modes, source_modes, gamma_index, momenta, pattern, time_pairs):
    times, nmode, _, comps, sites = sink_modes.shape
    spaces, subs, tms = (lax.axis_size(name) for name in ("space", "sub", "tm"))

    def as_rows(modes):
        return modes.transpose(0, 1, 3, 2, 4).reshape(times, nmode * comps * 2, sites)

    owners = (
        (spaces, subs, tms, times) == (4, 2, 2, 2)
        and gamma_index.shape[0] == spaces * subs
        and time_pairs.shape[0] == times
    )
    plan = by_owner if owners else by_rows
    arrays = (as_rows(sink_modes), as_rows(source_modes), gamma_index, momenta.T, pattern)
    scale = 1.0 / math.sqrt(3 * sites * spaces * subs)
    return plan(*arrays, time_pairs, nmode, times, scale)


def solution(mesh):
    rows = P(("grp", "tm"), None, None, None, ("space", "sub"))
    in_specs = (rows, rows, P(), P(), P("tm", ("space", "sub")), P("tm", None))
    out_specs = (P(("grp", "tm"), None, None, ("space", "sub"), None),) * 2
    return jax.shard_map(local, mesh=mesh, in_specs=in_specs, out_specs=out_specs, check_vma=False)
```

```python
import functools
import math

import jax
import jax.numpy as jnp
import numpy as np
from jax import lax
from jax.experimental import pallas as pl
from jax.experimental.pallas import tpu as pltpu
from jax.sharding import PartitionSpec as P

LAT = 96
CLASSES = 4
F32 = jnp.float32
BF16 = jnp.bfloat16
VMEM_LIMIT = 16 * 2**20
SMALL_LIMIT = 4 * 2**20
ROUND = ((2, 1, 3), (2, 1, 3))
LARGE = 10**11


def build_gammas():
    sigmas = [
        np.array([[0, 1], [1, 0]], dtype=complex),
        np.array([[0, -1j], [1j, 0]], dtype=complex),
        np.array([[1, 0], [0, -1]], dtype=complex),
    ]
    zero, one = np.zeros((2, 2), dtype=complex), np.eye(2, dtype=complex)
    gammas = [np.block([[zero, 1j * s], [-1j * s, zero]]) for s in sigmas]
    gammas.append(np.block([[zero, one], [one, zero]]))
    tables = []
    for subset in range(16):
        product = np.eye(4, dtype=complex)
        for factor in range(4):
            if subset >> factor & 1:
                product = product @ gammas[factor]
        tables.append(product)
    return tables


def gamma_codes():
    words = [0, 0, 0, 0]
    for index, table in enumerate(build_gammas()):
        flip = gamma_flip(index)
        for row in range(4):
            entry = table[row, row ^ flip]
            power = [k for k in range(4) if abs(entry - 1j**k) < 1e-6]
            assert len(power) == 1 and np.count_nonzero(table[row]) == 1
            words[index // 4] |= power[0] << (8 * (index % 4) + 2 * row)
    return [word - 2**32 if word >= 2**31 else word for word in words]


def gamma_flip(index):
    b1, b2, b3, b4 = (index & 1, (index >> 1) & 1, (index >> 2) & 1, (index >> 3) & 1)
    return (b1 ^ b2) | ((b1 ^ b2 ^ b3 ^ b4) << 1)


def site_coords(site):
    coords = []
    for axis in range(3):
        total = jnp.zeros_like(site)
        for level in range(6):
            total = total + (((site >> (3 * level + axis)) & 1) << level)
        coords.append(total)
    return coords


def wave_phases(insertions, momenta_ref, pattern_row):
    sites = pattern_row.shape[1]
    fours = insertions // CLASSES
    first_site = (
        lax.axis_index("space") * lax.axis_size("sub") + lax.axis_index("sub")
    ) * sites
    site = lax.broadcasted_iota(jnp.int32, (1, sites), 1) + first_site
    coords = site_coords(site)
    rows = []
    for four in range(fours):
        wave = jnp.zeros_like(site)
        for axis in range(3):
            chosen = jnp.zeros_like(site)
            for kind in range(CLASSES):
                chosen = jnp.where(
                    pattern_row == kind, momenta_ref[axis, four * CLASSES + kind], chosen
                )
            wave = wave + coords[axis] * chosen
        laps = jnp.floor((wave.astype(F32) + 0.5) * (1.0 / LAT)).astype(jnp.int32)
        rows.append((wave - LAT * laps).astype(F32) * (2.0 * math.pi / LAT))
    angle = jnp.concatenate(rows, axis=0)
    return jnp.cos(angle), jnp.sin(angle)


def multiply_slots(
    insertions, slots, gamma_ref, pattern_row, sink_mat, turned, buffers, out
):
    _, comps, _, nmode, sites = turned.shape
    colours = comps // 4
    words = gamma_codes()
    parts = len(buffers)
    per_part = comps // parts
    plan = []
    for slot in slots:
        g = insertions[slot]
        index = gamma_ref[g]
        word = jnp.int32(words[3])
        for step in (2, 1, 0):
            word = jnp.where(index < 4 * (step + 1), jnp.int32(words[step]), word)
        code = word >> (8 * (index & 3))
        mask = jnp.where(pattern_row == lax.rem(g, CLASSES), 1.0, 0.0)
        rows = []
        for spin in range(4):
            power = (code >> (2 * spin)) & 3
            real_sign = jnp.where((power == 0) | (power == 3), 1.0, -1.0)
            imag_sign = jnp.where(power < 2, 1.0, -1.0)
            rows.append(
                (
                    power & 1,
                    (gamma_flip(index) ^ spin) * colours,
                    (mask * real_sign).astype(BF16),
                    (mask * imag_sign).astype(BF16),
                )
            )
        plan.append((g // CLASSES, rows))
    for part in range(parts):
        buffer = buffers[part]
        for k, (four, rows) in enumerate(plan):
            base = k * nmode
            for step in range(per_part):
                comp = part * per_part + step
                odd, taken, real_row, imag_row = rows[comp // colours]
                source = taken + comp % colours
                at = step * 2 * sites
                buffer[base : base + nmode, at : at + sites] = (
                    turned[four, source, odd] * real_row
                )
                buffer[base : base + nmode, at + sites : at + 2 * sites] = (
                    turned[four, source, 1 - odd] * imag_row
                )
        width = per_part * 2 * sites
        block = lax.dot_general(
            buffer[...],
            sink_mat[:, part * width : (part + 1) * width],
            (((1,), (1,)), ((), ())),
            preferred_element_type=F32,
        ).reshape(out.shape)
        out[...] = block if part == 0 else out[...] + block


def first_kernel(order, time, slots, chunks, ahead, loaded, waits, *refs):
    sink_src, source_src, gamma_hbm, momenta_hbm, pattern_hbm, *refs = refs
    out, sink_mat, turned, *refs = refs[waits:]
    nexts, refs = (refs[:2], refs[2:]) if ahead else ([], refs)
    sink_stage, source_stage, gamma_ref, momenta_ref, pattern_ref, *refs = refs
    small_sems, big_sems, next_sems, *refs = refs
    raws, buffers = ([sink_src, source_src], refs) if loaded else (refs[:2], refs[2:])
    rows, sites = sink_stage.shape
    fours, _, _, nmode, _ = turned.shape
    per_mode = rows // nmode
    comps = per_mode // 2
    insertions = order()
    height = rows // chunks

    small = [
        pltpu.make_async_copy(src, dst, small_sems.at[k])
        for k, (src, dst) in enumerate(
            [(momenta_hbm, momenta_ref), (pattern_hbm, pattern_ref), (gamma_hbm, gamma_ref)]
        )
    ]
    big, later = [], []
    if not loaded:
        for which, (src, dst) in enumerate(zip((sink_src, source_src), raws)):
            for k in range(chunks):
                part = pl.ds(k * height, height)
                sem = big_sems.at[which * chunks + k]
                big.append(pltpu.make_async_copy(src.at[time, part], dst.at[part], sem))
    for k, (src, dst) in enumerate(zip((sink_src, source_src), nexts)):
        later.append(pltpu.make_async_copy(src.at[time + 1], dst, next_sems.at[k]))
    for copy in small + big + later:
        copy.start()

    def stage(which, dst):
        for k in range(chunks):
            part = slice(k * height, (k + 1) * height)
            if not loaded:
                big[which * chunks + k].wait()
            dst[part] = raws[which][part].astype(F32)

    stage(0, sink_stage)
    for comp in range(comps):
        at = comp * 2 * sites
        real = sink_stage[pl.ds(2 * comp, nmode, stride=per_mode), :].astype(BF16)
        imag = sink_stage[pl.ds(2 * comp + 1, nmode, stride=per_mode), :].astype(BF16)
        sink_mat[0:nmode, at : at + sites] = real
        sink_mat[0:nmode, at + sites : at + 2 * sites] = imag
        sink_mat[nmode:, at : at + sites] = -imag
        sink_mat[nmode:, at + sites : at + 2 * sites] = real
    for copy in small:
        copy.wait()
    pattern_row = pattern_ref[time : time + 1, :]
    cosine, sine = wave_phases(fours * CLASSES, momenta_ref, pattern_row)
    stage(1, source_stage)
    for comp in range(comps):
        real = source_stage[pl.ds(2 * comp, nmode, stride=per_mode), :]
        imag = source_stage[pl.ds(2 * comp + 1, nmode, stride=per_mode), :]
        for four in range(fours):
            cos_row, sin_row = cosine[four : four + 1], sine[four : four + 1]
            turned[four, comp, 0] = (real * cos_row - imag * sin_row).astype(BF16)
            turned[four, comp, 1] = (real * sin_row + imag * cos_row).astype(BF16)
    multiply_slots(insertions, slots, gamma_ref, pattern_row, sink_mat, turned, buffers, out)
    for copy in later:
        copy.wait()


def block_cost(slots, nmode, depth):
    return pl.CostEstimate(
        flops=100 * slots * nmode * nmode * depth,
        bytes_accessed=8 * nmode * depth,
        transcendentals=0,
    )


def product_buffers(slots, nmode, depth):
    parts = 2
    return [pltpu.VMEM((slots * nmode, depth // parts), BF16)] * parts


def first_blocks(modes, small, time, nmode, order, slots, ahead=False, after=()):
    rows, sites = modes[0].shape[-2:]
    loaded = modes[0].ndim == 2
    comps = rows // nmode // 2
    depth = comps * 2 * sites
    chunks = 4 if rows % 64 == 0 else 1
    gamma_index, momenta, pattern = small
    fours = gamma_index.shape[0] // CLASSES
    raw = [pltpu.VMEM((rows, sites), BF16)] * 2
    where = pltpu.VMEM if loaded else pltpu.HBM
    if not loaded:
        modes = in_hbm(modes)
    return pl.pallas_call(
        functools.partial(first_kernel, order, time, slots, chunks, ahead, loaded, len(after)),
        in_specs=[pl.BlockSpec(memory_space=where)] * 2
        + [pl.BlockSpec(memory_space=pltpu.HBM)] * 3
        + [pl.BlockSpec(memory_space=pl.ANY)] * len(after),
        out_shape=[
            pltpu.VMEM((len(slots), nmode, 2 * nmode), F32),
            pltpu.VMEM((2 * nmode, depth), BF16),
            pltpu.VMEM((fours, comps, 2, nmode, sites), BF16),
        ]
        + (raw if ahead else []),
        scratch_shapes=[
            pltpu.VMEM((rows, sites), F32),
            pltpu.VMEM((rows, sites), F32),
            pltpu.SMEM(gamma_index.shape, jnp.int32),
            pltpu.SMEM(momenta.shape, jnp.int32),
            pltpu.VMEM(pattern.shape, jnp.int32),
            pltpu.SemaphoreType.DMA((3,)),
            pltpu.SemaphoreType.DMA((2 * chunks,)),
            pltpu.SemaphoreType.DMA((2,)),
        ]
        + ([] if loaded else raw)
        + product_buffers(len(slots), nmode, depth),
        compiler_params=pltpu.CompilerParams(vmem_limit_bytes=VMEM_LIMIT),
        cost_estimate=block_cost(len(slots), nmode, depth),
        name="first_blocks",
    )(*modes, *in_hbm(small), *after)


def in_hbm(arrays):
    return [pltpu.with_memory_space_constraint(a, pltpu.HBM) for a in arrays]


def later_kernel(order, time, slots, gamma_ref, pattern_ref, sink_mat, turned, out, *buffers):
    pattern_row = pattern_ref[time : time + 1, :]
    multiply_slots(order(), slots, gamma_ref, pattern_row, sink_mat, turned, buffers, out)


def later_blocks(gamma_index, pattern, sink_mat, turned, time, order, slots):
    nmode, depth = turned.shape[3], sink_mat.shape[1]
    return pl.pallas_call(
        functools.partial(later_kernel, order, time, slots),
        in_specs=[pl.BlockSpec(memory_space=pltpu.SMEM)]
        + [pl.BlockSpec(memory_space=pltpu.VMEM)] * 3,
        out_shape=pltpu.VMEM((len(slots), nmode, 2 * nmode), F32),
        scratch_shapes=product_buffers(len(slots), nmode, depth),
        compiler_params=pltpu.CompilerParams(vmem_limit_bytes=VMEM_LIMIT),
        cost_estimate=block_cost(len(slots), nmode, depth),
        name="later_blocks",
    )(gamma_index, pattern, sink_mat, turned)


def small_call(kernel, outs, name, *args, flops=1, after=(), scratch=()):
    return pl.pallas_call(
        kernel,
        in_specs=[pl.BlockSpec(memory_space=pltpu.VMEM)] * len(args)
        + [pl.BlockSpec(memory_space=pl.ANY)] * len(after),
        out_shape=outs,
        scratch_shapes=scratch,
        compiler_params=pltpu.CompilerParams(vmem_limit_bytes=SMALL_LIMIT),
        cost_estimate=pl.CostEstimate(flops=flops, bytes_accessed=1, transcendentals=0),
        name=name,
    )(*args, *after)


def add_units(keep, got):
    def kernel(keep_ref, got_ref, *outs):
        for slot, out in enumerate(outs):
            out[...] = keep_ref[slot] + got_ref[slot]

    units, rows, columns = keep.shape
    outs = [pltpu.VMEM((rows, columns), F32)] * units
    return small_call(kernel, outs, "add_cores", keep, got)


def sum_units(terms, scale, after=()):
    def kernel(*refs):
        total = refs[0][...]
        for ref in refs[1 : len(terms)]:
            total = total + ref[...]
        refs[-1][...] = total * scale

    out = pltpu.VMEM(terms[0].shape, F32)
    return small_call(kernel, out, "sum_chips", *terms, after=after)


def write_rows(whole, lane, spaces, subs, cores, outs):
    row_count = outs[0].shape[3]
    z, core = lax.axis_index("space"), lax.axis_index("sub")
    for c, out in zip(cores, outs, strict=True):
        for s in range(spaces):
            start = pl.multiple_of(((z ^ s) * subs + (core ^ c)) * row_count, row_count)
            for part in range(2):
                out[s, lane, part] = whole[part, pl.ds(start, row_count), :]


def turn(matrix, whole):
    nmode = matrix.shape[1] // 2
    for part in range(2):
        whole[part] = matrix[:, part * nmode : (part + 1) * nmode].T


def turn_field(field, after):
    def kernel(field_ref, *refs):
        turn(field_ref[...], refs[-1])

    nmode = field.shape[0]
    out = pltpu.VMEM((2, nmode, nmode), F32)
    return small_call(kernel, out, "turn_field", field, flops=LARGE, after=after)


def split_rows(whole, field, spaces, subs):
    nmode = whole.shape[1]

    def kernel(whole_ref, field_ref, away, keep, staging):
        turn(field_ref[...], staging)
        for lane, source in enumerate((whole_ref, staging)):
            write_rows(source, lane, spaces, subs, [1, 0], [away, keep])

    outs = [pltpu.VMEM((spaces, 2, 2, nmode // (spaces * subs), nmode), F32)] * 2
    scratch = [pltpu.VMEM((2, nmode, nmode), F32)]
    return small_call(kernel, outs, "split_rows", whole, field, scratch=scratch)


def product_kernel(spaces, subs, tms, pairs_ref, *refs):
    fields, (away, whole, held) = refs[:-3], refs[-3:]
    nmode = fields[0].shape[0]
    times = len(fields) // tms
    mine = lax.axis_index("tm")
    for other in range(tms):
        for time in range(times):
            held[(mine ^ other) * times + time] = fields[other * times + time][...]
    for pair in range(pairs_ref.shape[0]):
        left, right = held[pairs_ref[pair, 0]], held[pairs_ref[pair, 1]]
        swapped = jnp.concatenate([-left[:, nmode:], left[:, :nmode]], axis=1)
        result = lax.dot_general(
            right,
            jnp.concatenate([left, swapped], axis=0),
            (((1,), (0,)), ((), ())),
            preferred_element_type=F32,
            precision=lax.Precision.HIGHEST,
        ) * (1.0 / math.sqrt(nmode))
        turn(result, whole.at[pair])
        write_rows(whole.at[pair], pair, spaces, subs, [1], [away])


def product_rows(time_pairs, fields, spaces, subs, tms):
    nmode, pairs = fields[0].shape[0], time_pairs.shape[0]
    shape = (spaces, pairs, 2, nmode // (spaces * subs), nmode)
    return pl.pallas_call(
        functools.partial(product_kernel, spaces, subs, tms),
        in_specs=[pl.BlockSpec(memory_space=pltpu.SMEM)]
        + [pl.BlockSpec(memory_space=pltpu.VMEM)] * len(fields),
        out_shape=[pltpu.VMEM(shape, F32), pltpu.VMEM((pairs, 2, nmode, nmode), F32)],
        scratch_shapes=[pltpu.VMEM((len(fields), nmode, 2 * nmode), F32)],
        compiler_params=pltpu.CompilerParams(vmem_limit_bytes=SMALL_LIMIT),
        cost_estimate=pl.CostEstimate(
            flops=8 * pairs * nmode**3, bytes_accessed=64 * nmode * nmode, transcendentals=0
        ),
        name="products",
    )(time_pairs, *fields)


def keep_rows(whole, spaces, subs):
    lanes, _, nmode, _ = whole.shape

    def kernel(whole_ref, out):
        for lane in range(lanes):
            write_rows(whole_ref.at[lane], lane, spaces, subs, [0], [out])

    out = pltpu.VMEM((spaces, lanes, 2, nmode // (spaces * subs), nmode), F32)
    return small_call(kernel, out, "keep_rows", whole, flops=LARGE)


def pair_cores(keep, got):
    shape = keep.shape

    def kernel(keep_ref, got_ref, *outs):
        for s, out in enumerate(outs):
            out[0] = keep_ref[s]
            out[1] = got_ref[s]

    outs = [pltpu.VMEM((2,) + shape[1:], F32)] * shape[0]
    return small_call(kernel, outs, "pair_cores", keep, got)


def pair_with(near, keep, got):
    shape = keep.shape

    def kernel(near_ref, keep_ref, got_ref, *outs):
        outs[1][0] = near_ref[...]
        for s, out in enumerate(outs):
            out = out.at[1] if s == 1 else out
            out[0] = keep_ref[s]
            out[1] = got_ref[s]

    outs = [
        pltpu.VMEM(((2,) if s == 1 else ()) + (2,) + shape[1:], F32) for s in range(shape[0])
    ]
    return small_call(kernel, outs, "pair_cores", near, keep, got)


def put_blocks(args, places, arrays, spaces, subs, name, flops):
    lanes, _, row_count, nmode = args[0].shape[-4:]
    count = len(arrays)

    def kernel(*refs):
        outs, sems = refs[-1 - count : -1], refs[-1]
        refs = refs[len(given) :]
        z, core = lax.axis_index("space"), lax.axis_index("sub")
        copies = []
        for out, group in zip(outs, places, strict=True):
            for s, operand, index in group:
                block = refs[operand] if index is None else refs[operand].at[index]
                for c in range(subs):
                    copy = pltpu.make_async_copy(
                        block.at[c],
                        out.at[:, (z ^ s) * subs + (core ^ c)],
                        sems.at[len(copies)],
                    )
                    copy.start()
                    copies.append(copy)
        for copy in copies:
            copy.wait()

    out = jax.ShapeDtypeStruct((lanes, spaces * subs, 2, row_count, nmode), F32)
    given = [(k, array) for k, array in enumerate(arrays) if array is not None]
    return pl.pallas_call(
        kernel,
        in_specs=[pl.BlockSpec(memory_space=pltpu.HBM)] * len(given)
        + [pl.BlockSpec(memory_space=pltpu.VMEM)] * len(args),
        out_specs=[pl.BlockSpec(memory_space=pltpu.HBM)] * count,
        out_shape=[out] * count,
        input_output_aliases={n: k for n, (k, _) in enumerate(given)},
        scratch_shapes=[pltpu.SemaphoreType.DMA((sum(map(len, places)) * subs,))],
        compiler_params=pltpu.CompilerParams(vmem_limit_bytes=SMALL_LIMIT),
        cost_estimate=pl.CostEstimate(flops=flops, bytes_accessed=1, transcendentals=0),
        name=name,
    )(*(array for _, array in given), *args)


def swap(value, axis, distance):
    size = lax.axis_size(axis)
    return lax.ppermute(value, axis, [(i, i ^ distance) for i in range(size)])


def own_insertions(spaces, subs):
    z, core = lax.axis_index("space"), lax.axis_index("sub")
    return [(z ^ s) * subs + (core ^ c) for c in range(subs) for s in range(spaces)]


def by_owner(sink, source, gamma_index, momenta, pattern, time_pairs, nmode, times, scale):
    spaces, subs, tms = (lax.axis_size(name) for name in ("space", "sub", "tm"))
    order = functools.partial(own_insertions, spaces, subs)
    mine, other = list(range(spaces)), list(range(spaces, 2 * spaces))
    small = (gamma_index, momenta, pattern)

    def send(away, laid, time):
        got = swap(away, "sub", 1)
        keep = later_blocks(gamma_index, pattern, *laid, time, order, mine)
        parts = add_units(keep, got)
        return [parts[0]] + [swap(parts[s], "space", s) for s in ROUND[time]]

    away, sink_mat, turned, *modes = first_blocks(
        (sink, source), small, 0, nmode, order, other, ahead=True
    )
    first = send(away, (sink_mat, turned), 0)
    away, sink_mat, turned = first_blocks(modes, small, 1, nmode, order, other, after=first[:1])
    second = send(away, (sink_mat, turned), 1)
    first = sum_units(first, scale)
    first_other = swap(first, "tm", 1)
    whole = turn_field(first, second[1:])
    second = sum_units(second, scale, [first_other, whole])
    second_other = swap(second, "tm", 1)

    away, keep = split_rows(whole, second, spaces, subs)
    meson = pair_cores(keep, swap(away, "sub", 1))
    own, meson_near, two, three = meson
    two, three = swap(two, "space", 2), swap(three, "space", 3)
    fields = [first, second, first_other, second_other]
    away, whole = product_rows(time_pairs, fields, spaces, subs, tms)
    got = swap(away, "sub", 1)
    products = pair_with(meson_near, keep_rows(whole, spaces, subs), got)
    places = [[(0, 0, None), (2, 1, None), (3, 2, None)], [(0, 3, None)]]
    meson_parts = [own, two, three]
    own, near, two, three = products
    two, three, near = (swap(v, "space", s) for v, s in ((two, 2), (three, 3), (near, 1)))
    arrays = put_blocks(
        meson_parts + [own], places, [None, None], spaces, subs, "put_early", LARGE
    )
    places = [[(1, 2, 0)], [(1, 2, 1), (2, 1, None), (3, 0, None)]]
    return put_blocks([three, two, near], places, arrays, spaces, subs, "put_late", 1)


def by_rows(sink, source, gamma_index, momenta, pattern, time_pairs, nmode, times, scale):
    axes = ("space", "sub")
    highest = lax.Precision.HIGHEST
    insertions = gamma_index.shape[0]
    partial = jnp.stack(
        [
            first_blocks(
                (sink, source),
                (gamma_index, momenta, pattern),
                time,
                nmode,
                lambda: list(range(insertions)),
                list(range(insertions)),
            )[0]
            for time in range(times)
        ]
    )
    partial = partial.reshape(times, insertions, nmode, 2, nmode).transpose(0, 1, 3, 4, 2)
    meson = lax.psum_scatter(partial * scale, axes, scatter_dimension=3, tiled=True)
    rows = lax.all_gather(meson, "tm", axis=0, tiled=True)
    whole = lax.all_gather(rows, axes, axis=3, tiled=True)
    left, right = rows[time_pairs[:, 0]], whole[time_pairs[:, 1]]

    def multiply(a, b):
        return jnp.einsum("qgik,qgkj->qgij", a, b, precision=highest)

    real = multiply(left[:, :, 0], right[:, :, 0]) - multiply(left[:, :, 1], right[:, :, 1])
    imag = multiply(left[:, :, 0], right[:, :, 1]) + multiply(left[:, :, 1], right[:, :, 0])
    return meson, jnp.stack([real, imag], axis=2) / math.sqrt(nmode)


def local(sink_modes, source_modes, gamma_index, momenta, pattern, time_pairs):
    times, nmode, _, comps, sites = sink_modes.shape
    spaces, subs, tms = (lax.axis_size(name) for name in ("space", "sub", "tm"))

    def as_rows(modes):
        return modes.transpose(0, 1, 3, 2, 4).reshape(times, nmode * comps * 2, sites)

    owners = (
        (spaces, subs, tms, times) == (4, 2, 2, 2)
        and gamma_index.shape[0] == spaces * subs
        and time_pairs.shape[0] == times
    )
    plan = by_owner if owners else by_rows
    arrays = (as_rows(sink_modes), as_rows(source_modes), gamma_index, momenta.T, pattern)
    scale = 1.0 / math.sqrt(3 * sites * spaces * subs)
    return plan(*arrays, time_pairs, nmode, times, scale)


def solution(mesh):
    rows = P(("grp", "tm"), None, None, None, ("space", "sub"))
    in_specs = (rows, rows, P(), P(), P("tm", ("space", "sub")), P("tm", None))
    out_specs = (P(("grp", "tm"), None, None, ("space", "sub"), None),) * 2
    return jax.shard_map(local, mesh=mesh, in_specs=in_specs, out_specs=out_specs, check_vma=False)
```

```python
import functools
import math

import jax
import jax.numpy as jnp
import numpy as np
from jax import lax
from jax.experimental import pallas as pl
from jax.experimental.pallas import tpu as pltpu
from jax.sharding import PartitionSpec as P

LAT = 96
CLASSES = 4
F32 = jnp.float32
BF16 = jnp.bfloat16
VMEM_LIMIT = 16 * 2**20
SMALL_LIMIT = 4 * 2**20
ROUND = ((2, 1, 3), (2, 1, 3))
LARGE = 10**11


def build_gammas():
    sigmas = [
        np.array([[0, 1], [1, 0]], dtype=complex),
        np.array([[0, -1j], [1j, 0]], dtype=complex),
        np.array([[1, 0], [0, -1]], dtype=complex),
    ]
    zero, one = np.zeros((2, 2), dtype=complex), np.eye(2, dtype=complex)
    gammas = [np.block([[zero, 1j * s], [-1j * s, zero]]) for s in sigmas]
    gammas.append(np.block([[zero, one], [one, zero]]))
    tables = []
    for subset in range(16):
        product = np.eye(4, dtype=complex)
        for factor in range(4):
            if subset >> factor & 1:
                product = product @ gammas[factor]
        tables.append(product)
    return tables


def gamma_codes():
    words = [0, 0, 0, 0]
    for index, table in enumerate(build_gammas()):
        flip = gamma_flip(index)
        for row in range(4):
            entry = table[row, row ^ flip]
            power = [k for k in range(4) if abs(entry - 1j**k) < 1e-6]
            assert len(power) == 1 and np.count_nonzero(table[row]) == 1
            words[index // 4] |= power[0] << (8 * (index % 4) + 2 * row)
    return [word - 2**32 if word >= 2**31 else word for word in words]


def gamma_flip(index):
    b1, b2, b3, b4 = (index & 1, (index >> 1) & 1, (index >> 2) & 1, (index >> 3) & 1)
    return (b1 ^ b2) | ((b1 ^ b2 ^ b3 ^ b4) << 1)


def site_coords(site):
    coords = []
    for axis in range(3):
        total = jnp.zeros_like(site)
        for level in range(6):
            total = total + (((site >> (3 * level + axis)) & 1) << level)
        coords.append(total)
    return coords


def wave_phases(insertions, momenta_ref, pattern_row):
    sites = pattern_row.shape[1]
    fours = insertions // CLASSES
    first_site = (
        lax.axis_index("space") * lax.axis_size("sub") + lax.axis_index("sub")
    ) * sites
    site = lax.broadcasted_iota(jnp.int32, (1, sites), 1) + first_site
    coords = site_coords(site)
    rows = []
    for four in range(fours):
        wave = jnp.zeros_like(site)
        for axis in range(3):
            chosen = jnp.zeros_like(site)
            for kind in range(CLASSES):
                chosen = jnp.where(
                    pattern_row == kind, momenta_ref[axis, four * CLASSES + kind], chosen
                )
            wave = wave + coords[axis] * chosen
        laps = jnp.floor((wave.astype(F32) + 0.5) * (1.0 / LAT)).astype(jnp.int32)
        rows.append((wave - LAT * laps).astype(F32) * (2.0 * math.pi / LAT))
    angle = jnp.concatenate(rows, axis=0)
    return jnp.cos(angle), jnp.sin(angle)


def multiply_slots(
    insertions, slots, gamma_ref, pattern_row, sink_mat, turned, buffers, out
):
    _, comps, _, nmode, sites = turned.shape
    colours = comps // 4
    words = gamma_codes()
    parts = len(buffers)
    per_part = comps // parts
    plan = []
    for slot in slots:
        g = insertions[slot]
        index = gamma_ref[g]
        word = jnp.int32(words[3])
        for step in (2, 1, 0):
            word = jnp.where(index < 4 * (step + 1), jnp.int32(words[step]), word)
        code = word >> (8 * (index & 3))
        mask = jnp.where(pattern_row == lax.rem(g, CLASSES), 1.0, 0.0)
        rows = []
        for spin in range(4):
            power = (code >> (2 * spin)) & 3
            real_sign = jnp.where((power == 0) | (power == 3), 1.0, -1.0)
            imag_sign = jnp.where(power < 2, 1.0, -1.0)
            rows.append(
                (
                    power & 1,
                    (gamma_flip(index) ^ spin) * colours,
                    (mask * real_sign).astype(BF16),
                    (mask * imag_sign).astype(BF16),
                )
            )
        plan.append((g // CLASSES, rows))
    for part in range(parts):
        buffer = buffers[part]
        for k, (four, rows) in enumerate(plan):
            base = k * nmode
            for step in range(per_part):
                comp = part * per_part + step
                odd, taken, real_row, imag_row = rows[comp // colours]
                source = taken + comp % colours
                at = step * 2 * sites
                buffer[base : base + nmode, at : at + sites] = (
                    turned[four, source, odd] * real_row
                )
                buffer[base : base + nmode, at + sites : at + 2 * sites] = (
                    turned[four, source, 1 - odd] * imag_row
                )
        width = per_part * 2 * sites
        block = lax.dot_general(
            buffer[...],
            sink_mat[:, part * width : (part + 1) * width],
            (((1,), (1,)), ((), ())),
            preferred_element_type=F32,
        ).reshape(out.shape)
        out[...] = block if part == 0 else out[...] + block


def first_kernel(order, time, slots, chunks, ahead, loaded, waits, *refs):
    sink_src, source_src, gamma_hbm, momenta_hbm, pattern_hbm, *refs = refs
    out, sink_mat, turned, *refs = refs[waits:]
    nexts, refs = (refs[:2], refs[2:]) if ahead else ([], refs)
    sink_stage, source_stage, gamma_ref, momenta_ref, pattern_ref, *refs = refs
    small_sems, big_sems, next_sems, *refs = refs
    raws, buffers = ([sink_src, source_src], refs) if loaded else (refs[:2], refs[2:])
    rows, sites = sink_stage.shape
    fours, _, _, nmode, _ = turned.shape
    per_mode = rows // nmode
    comps = per_mode // 2
    insertions = order()
    height = rows // chunks

    small = [
        pltpu.make_async_copy(src, dst, small_sems.at[k])
        for k, (src, dst) in enumerate(
            [(momenta_hbm, momenta_ref), (pattern_hbm, pattern_ref), (gamma_hbm, gamma_ref)]
        )
    ]
    big, later = [], []
    if not loaded:
        for which, (src, dst) in enumerate(zip((sink_src, source_src), raws)):
            for k in range(chunks):
                part = pl.ds(k * height, height)
                sem = big_sems.at[which * chunks + k]
                big.append(pltpu.make_async_copy(src.at[time, part], dst.at[part], sem))
    for k, (src, dst) in enumerate(zip((sink_src, source_src), nexts)):
        later.append(pltpu.make_async_copy(src.at[time + 1], dst, next_sems.at[k]))
    for copy in small + big + later:
        copy.start()

    def stage(which, dst):
        for k in range(chunks):
            part = slice(k * height, (k + 1) * height)
            if not loaded:
                big[which * chunks + k].wait()
            dst[part] = raws[which][part].astype(F32)

    stage(0, sink_stage)
    for comp in range(comps):
        at = comp * 2 * sites
        real = sink_stage[pl.ds(2 * comp, nmode, stride=per_mode), :].astype(BF16)
        imag = sink_stage[pl.ds(2 * comp + 1, nmode, stride=per_mode), :].astype(BF16)
        sink_mat[0:nmode, at : at + sites] = real
        sink_mat[0:nmode, at + sites : at + 2 * sites] = imag
        sink_mat[nmode:, at : at + sites] = -imag
        sink_mat[nmode:, at + sites : at + 2 * sites] = real
    for copy in small:
        copy.wait()
    pattern_row = pattern_ref[time : time + 1, :]
    cosine, sine = wave_phases(fours * CLASSES, momenta_ref, pattern_row)
    stage(1, source_stage)
    for comp in range(comps):
        real = source_stage[pl.ds(2 * comp, nmode, stride=per_mode), :]
        imag = source_stage[pl.ds(2 * comp + 1, nmode, stride=per_mode), :]
        for four in range(fours):
            cos_row, sin_row = cosine[four : four + 1], sine[four : four + 1]
            turned[four, comp, 0] = (real * cos_row - imag * sin_row).astype(BF16)
            turned[four, comp, 1] = (real * sin_row + imag * cos_row).astype(BF16)
    multiply_slots(insertions, slots, gamma_ref, pattern_row, sink_mat, turned, buffers, out)
    for copy in later:
        copy.wait()


def block_cost(slots, nmode, depth):
    return pl.CostEstimate(
        flops=100 * slots * nmode * nmode * depth,
        bytes_accessed=8 * nmode * depth,
        transcendentals=0,
    )


def product_buffers(slots, nmode, depth):
    parts = 2
    return [pltpu.VMEM((slots * nmode, depth // parts), BF16)] * parts


def first_blocks(modes, small, time, nmode, order, slots, ahead=False, after=()):
    rows, sites = modes[0].shape[-2:]
    loaded = modes[0].ndim == 2
    comps = rows // nmode // 2
    depth = comps * 2 * sites
    chunks = 4 if rows % 64 == 0 else 1
    gamma_index, momenta, pattern = small
    fours = gamma_index.shape[0] // CLASSES
    raw = [pltpu.VMEM((rows, sites), BF16)] * 2
    where = pltpu.VMEM if loaded else pltpu.HBM
    if not loaded:
        modes = in_hbm(modes)
    return pl.pallas_call(
        functools.partial(first_kernel, order, time, slots, chunks, ahead, loaded, len(after)),
        in_specs=[pl.BlockSpec(memory_space=where)] * 2
        + [pl.BlockSpec(memory_space=pltpu.HBM)] * 3
        + [pl.BlockSpec(memory_space=pl.ANY)] * len(after),
        out_shape=[
            pltpu.VMEM((len(slots), nmode, 2 * nmode), F32),
            pltpu.VMEM((2 * nmode, depth), BF16),
            pltpu.VMEM((fours, comps, 2, nmode, sites), BF16),
        ]
        + (raw if ahead else []),
        scratch_shapes=[
            pltpu.VMEM((rows, sites), F32),
            pltpu.VMEM((rows, sites), F32),
            pltpu.SMEM(gamma_index.shape, jnp.int32),
            pltpu.SMEM(momenta.shape, jnp.int32),
            pltpu.VMEM(pattern.shape, jnp.int32),
            pltpu.SemaphoreType.DMA((3,)),
            pltpu.SemaphoreType.DMA((2 * chunks,)),
            pltpu.SemaphoreType.DMA((2,)),
        ]
        + ([] if loaded else raw)
        + product_buffers(len(slots), nmode, depth),
        compiler_params=pltpu.CompilerParams(vmem_limit_bytes=VMEM_LIMIT),
        cost_estimate=block_cost(len(slots), nmode, depth),
        name="first_blocks",
    )(*modes, *in_hbm(small), *after)


def in_hbm(arrays):
    return [pltpu.with_memory_space_constraint(a, pltpu.HBM) for a in arrays]


def later_kernel(order, time, slots, gamma_ref, pattern_ref, sink_mat, turned, out, *buffers):
    pattern_row = pattern_ref[time : time + 1, :]
    multiply_slots(order(), slots, gamma_ref, pattern_row, sink_mat, turned, buffers, out)


def later_blocks(gamma_index, pattern, sink_mat, turned, time, order, slots):
    nmode, depth = turned.shape[3], sink_mat.shape[1]
    return pl.pallas_call(
        functools.partial(later_kernel, order, time, slots),
        in_specs=[pl.BlockSpec(memory_space=pltpu.SMEM)]
        + [pl.BlockSpec(memory_space=pltpu.VMEM)] * 3,
        out_shape=pltpu.VMEM((len(slots), nmode, 2 * nmode), F32),
        scratch_shapes=product_buffers(len(slots), nmode, depth),
        compiler_params=pltpu.CompilerParams(vmem_limit_bytes=VMEM_LIMIT),
        cost_estimate=block_cost(len(slots), nmode, depth),
        name="later_blocks",
    )(gamma_index, pattern, sink_mat, turned)


def small_call(kernel, outs, name, *args, flops=1, after=(), scratch=()):
    return pl.pallas_call(
        kernel,
        in_specs=[pl.BlockSpec(memory_space=pltpu.VMEM)] * len(args)
        + [pl.BlockSpec(memory_space=pl.ANY)] * len(after),
        out_shape=outs,
        scratch_shapes=scratch,
        compiler_params=pltpu.CompilerParams(vmem_limit_bytes=SMALL_LIMIT),
        cost_estimate=pl.CostEstimate(flops=flops, bytes_accessed=1, transcendentals=0),
        name=name,
    )(*args, *after)


def add_units(keep, got):
    def kernel(keep_ref, got_ref, *outs):
        for slot, out in enumerate(outs):
            out[...] = keep_ref[slot] + got_ref[slot]

    units, rows, columns = keep.shape
    outs = [pltpu.VMEM((rows, columns), F32)] * units
    return small_call(kernel, outs, "add_cores", keep, got)


def sum_units(terms, scale, after=()):
    def kernel(*refs):
        total = refs[0][...]
        for ref in refs[1 : len(terms)]:
            total = total + ref[...]
        refs[-1][...] = total * scale

    out = pltpu.VMEM(terms[0].shape, F32)
    return small_call(kernel, out, "sum_chips", *terms, after=after)


def write_rows(whole, lane, spaces, subs, cores, outs):
    row_count = outs[0].shape[3]
    z, core = lax.axis_index("space"), lax.axis_index("sub")
    for c, out in zip(cores, outs, strict=True):
        for s in range(spaces):
            start = pl.multiple_of(((z ^ s) * subs + (core ^ c)) * row_count, row_count)
            for part in range(2):
                out[s, lane, part] = whole[part, pl.ds(start, row_count), :]


def turn(matrix, whole):
    nmode = matrix.shape[1] // 2
    for part in range(2):
        whole[part] = matrix[:, part * nmode : (part + 1) * nmode].T


def turn_field(field, after):
    def kernel(field_ref, *refs):
        turn(field_ref[...], refs[-1])

    nmode = field.shape[0]
    out = pltpu.VMEM((2, nmode, nmode), F32)
    return small_call(kernel, out, "turn_field", field, flops=LARGE, after=after)


def split_rows(whole, field, spaces, subs):
    nmode = whole.shape[1]

    def kernel(whole_ref, field_ref, away, keep, staging):
        turn(field_ref[...], staging)
        for lane, source in enumerate((whole_ref, staging)):
            write_rows(source, lane, spaces, subs, [1, 0], [away, keep])

    outs = [pltpu.VMEM((spaces, 2, 2, nmode // (spaces * subs), nmode), F32)] * 2
    scratch = [pltpu.VMEM((2, nmode, nmode), F32)]
    return small_call(kernel, outs, "split_rows", whole, field, scratch=scratch, flops=LARGE)


def product_kernel(spaces, subs, tms, pairs_ref, *refs):
    fields, (away, whole, held) = refs[:-3], refs[-3:]
    nmode = fields[0].shape[0]
    times = len(fields) // tms
    mine = lax.axis_index("tm")
    for other in range(tms):
        for time in range(times):
            held[(mine ^ other) * times + time] = fields[other * times + time][...]
    for pair in range(pairs_ref.shape[0]):
        left, right = held[pairs_ref[pair, 0]], held[pairs_ref[pair, 1]]
        swapped = jnp.concatenate([-left[:, nmode:], left[:, :nmode]], axis=1)
        result = lax.dot_general(
            right,
            jnp.concatenate([left, swapped], axis=0),
            (((1,), (0,)), ((), ())),
            preferred_element_type=F32,
            precision=lax.Precision.HIGHEST,
        ) * (1.0 / math.sqrt(nmode))
        turn(result, whole.at[pair])
        write_rows(whole.at[pair], pair, spaces, subs, [1], [away])


def product_rows(time_pairs, fields, spaces, subs, tms):
    nmode, pairs = fields[0].shape[0], time_pairs.shape[0]
    shape = (spaces, pairs, 2, nmode // (spaces * subs), nmode)
    return pl.pallas_call(
        functools.partial(product_kernel, spaces, subs, tms),
        in_specs=[pl.BlockSpec(memory_space=pltpu.SMEM)]
        + [pl.BlockSpec(memory_space=pltpu.VMEM)] * len(fields),
        out_shape=[pltpu.VMEM(shape, F32), pltpu.VMEM((pairs, 2, nmode, nmode), F32)],
        scratch_shapes=[pltpu.VMEM((len(fields), nmode, 2 * nmode), F32)],
        compiler_params=pltpu.CompilerParams(vmem_limit_bytes=SMALL_LIMIT),
        cost_estimate=pl.CostEstimate(
            flops=8 * pairs * nmode**3, bytes_accessed=64 * nmode * nmode, transcendentals=0
        ),
        name="products",
    )(time_pairs, *fields)


def keep_rows(whole, spaces, subs):
    lanes, _, nmode, _ = whole.shape

    def kernel(whole_ref, out):
        for lane in range(lanes):
            write_rows(whole_ref.at[lane], lane, spaces, subs, [0], [out])

    out = pltpu.VMEM((spaces, lanes, 2, nmode // (spaces * subs), nmode), F32)
    return small_call(kernel, out, "keep_rows", whole, flops=LARGE)


def pair_cores(keep, got):
    shape = keep.shape

    def kernel(keep_ref, got_ref, *outs):
        for s, out in enumerate(outs):
            out[0] = keep_ref[s]
            out[1] = got_ref[s]

    outs = [pltpu.VMEM((2,) + shape[1:], F32)] * shape[0]
    return small_call(kernel, outs, "pair_cores", keep, got)


def pair_with(near, keep, got):
    shape = keep.shape

    def kernel(near_ref, keep_ref, got_ref, *outs):
        outs[1][0] = near_ref[...]
        for s, out in enumerate(outs):
            out = out.at[1] if s == 1 else out
            out[0] = keep_ref[s]
            out[1] = got_ref[s]

    outs = [
        pltpu.VMEM(((2,) if s == 1 else ()) + (2,) + shape[1:], F32) for s in range(shape[0])
    ]
    return small_call(kernel, outs, "pair_cores", near, keep, got)


def put_blocks(args, places, arrays, spaces, subs, name, flops):
    lanes, _, row_count, nmode = args[0].shape[-4:]
    count = len(arrays)

    def kernel(*refs):
        outs, sems = refs[-1 - count : -1], refs[-1]
        refs = refs[len(given) :]
        z, core = lax.axis_index("space"), lax.axis_index("sub")
        copies = []
        for out, group in zip(outs, places, strict=True):
            for s, operand, index in group:
                block = refs[operand] if index is None else refs[operand].at[index]
                for c in range(subs):
                    copy = pltpu.make_async_copy(
                        block.at[c],
                        out.at[:, (z ^ s) * subs + (core ^ c)],
                        sems.at[len(copies)],
                    )
                    copy.start()
                    copies.append(copy)
        for copy in copies:
            copy.wait()

    out = jax.ShapeDtypeStruct((lanes, spaces * subs, 2, row_count, nmode), F32)
    given = [(k, array) for k, array in enumerate(arrays) if array is not None]
    return pl.pallas_call(
        kernel,
        in_specs=[pl.BlockSpec(memory_space=pltpu.HBM)] * len(given)
        + [pl.BlockSpec(memory_space=pltpu.VMEM)] * len(args),
        out_specs=[pl.BlockSpec(memory_space=pltpu.HBM)] * count,
        out_shape=[out] * count,
        input_output_aliases={n: k for n, (k, _) in enumerate(given)},
        scratch_shapes=[pltpu.SemaphoreType.DMA((sum(map(len, places)) * subs,))],
        compiler_params=pltpu.CompilerParams(vmem_limit_bytes=SMALL_LIMIT),
        cost_estimate=pl.CostEstimate(flops=flops, bytes_accessed=1, transcendentals=0),
        name=name,
    )(*(array for _, array in given), *args)


def swap(value, axis, distance):
    size = lax.axis_size(axis)
    return lax.ppermute(value, axis, [(i, i ^ distance) for i in range(size)])


def own_insertions(spaces, subs):
    z, core = lax.axis_index("space"), lax.axis_index("sub")
    return [(z ^ s) * subs + (core ^ c) for c in range(subs) for s in range(spaces)]


def by_owner(sink, source, gamma_index, momenta, pattern, time_pairs, nmode, times, scale):
    spaces, subs, tms = (lax.axis_size(name) for name in ("space", "sub", "tm"))
    order = functools.partial(own_insertions, spaces, subs)
    mine, other = list(range(spaces)), list(range(spaces, 2 * spaces))
    small = (gamma_index, momenta, pattern)

    def send(away, laid, time):
        got = swap(away, "sub", 1)
        keep = later_blocks(gamma_index, pattern, *laid, time, order, mine)
        parts = add_units(keep, got)
        return [parts[0]] + [swap(parts[s], "space", s) for s in ROUND[time]]

    away, sink_mat, turned, *modes = first_blocks(
        (sink, source), small, 0, nmode, order, other, ahead=True
    )
    first = send(away, (sink_mat, turned), 0)
    away, sink_mat, turned = first_blocks(modes, small, 1, nmode, order, other, after=first[:1])
    second = send(away, (sink_mat, turned), 1)
    first = sum_units(first, scale)
    first_other = swap(first, "tm", 1)
    whole = turn_field(first, second[1:])
    second = sum_units(second, scale, [first_other, whole])
    second_other = swap(second, "tm", 1)

    away, keep = split_rows(whole, second, spaces, subs)
    meson = pair_cores(keep, swap(away, "sub", 1))
    own, near, two, three = meson
    two, three, near = (swap(v, "space", s) for v, s in ((two, 2), (three, 3), (near, 1)))
    fields = [first, second, first_other, second_other]
    away, whole = product_rows(time_pairs, fields, spaces, subs, tms)
    got = swap(away, "sub", 1)
    products = pair_cores(keep_rows(whole, spaces, subs), got)
    places = [
        [(0, 0, None), (1, 3, None), (2, 2, None), (3, 1, None)],
        [(0, 4, None)],
    ]
    meson_parts = [own, three, two, near]
    own, near, two, three = products
    two, three, near = (swap(v, "space", s) for v, s in ((two, 2), (three, 3), (near, 1)))
    meson, products = put_blocks(
        meson_parts + [own], places, [None, None], spaces, subs, "put_early", LARGE
    )
    places = [[(1, 1, None), (2, 0, None), (3, 2, None)]]
    (products,) = put_blocks([two, near, three], places, [products], spaces, subs, "put_late", 1)
    return meson, products


def by_rows(sink, source, gamma_index, momenta, pattern, time_pairs, nmode, times, scale):
    axes = ("space", "sub")
    highest = lax.Precision.HIGHEST
    insertions = gamma_index.shape[0]
    partial = jnp.stack(
        [
            first_blocks(
                (sink, source),
                (gamma_index, momenta, pattern),
                time,
                nmode,
                lambda: list(range(insertions)),
                list(range(insertions)),
            )[0]
            for time in range(times)
        ]
    )
    partial = partial.reshape(times, insertions, nmode, 2, nmode).transpose(0, 1, 3, 4, 2)
    meson = lax.psum_scatter(partial * scale, axes, scatter_dimension=3, tiled=True)
    rows = lax.all_gather(meson, "tm", axis=0, tiled=True)
    whole = lax.all_gather(rows, axes, axis=3, tiled=True)
    left, right = rows[time_pairs[:, 0]], whole[time_pairs[:, 1]]

    def multiply(a, b):
        return jnp.einsum("qgik,qgkj->qgij", a, b, precision=highest)

    real = multiply(left[:, :, 0], right[:, :, 0]) - multiply(left[:, :, 1], right[:, :, 1])
    imag = multiply(left[:, :, 0], right[:, :, 1]) + multiply(left[:, :, 1], right[:, :, 0])
    return meson, jnp.stack([real, imag], axis=2) / math.sqrt(nmode)


def local(sink_modes, source_modes, gamma_index, momenta, pattern, time_pairs):
    times, nmode, _, comps, sites = sink_modes.shape
    spaces, subs, tms = (lax.axis_size(name) for name in ("space", "sub", "tm"))

    def as_rows(modes):
        return modes.transpose(0, 1, 3, 2, 4).reshape(times, nmode * comps * 2, sites)

    owners = (
        (spaces, subs, tms, times) == (4, 2, 2, 2)
        and gamma_index.shape[0] == spaces * subs
        and time_pairs.shape[0] == times
    )
    plan = by_owner if owners else by_rows
    arrays = (as_rows(sink_modes), as_rows(source_modes), gamma_index, momenta.T, pattern)
    scale = 1.0 / math.sqrt(3 * sites * spaces * subs)
    return plan(*arrays, time_pairs, nmode, times, scale)


def solution(mesh):
    rows = P(("grp", "tm"), None, None, None, ("space", "sub"))
    in_specs = (rows, rows, P(), P(), P("tm", ("space", "sub")), P("tm", None))
    out_specs = (P(("grp", "tm"), None, None, ("space", "sub"), None),) * 2
    return jax.shard_map(local, mesh=mesh, in_specs=in_specs, out_specs=out_specs, check_vma=False)
```

```python
import functools
import math

import jax
import jax.numpy as jnp
import numpy as np
from jax import lax
from jax.experimental import pallas as pl
from jax.experimental.pallas import tpu as pltpu
from jax.sharding import PartitionSpec as P

LAT = 96
CLASSES = 4
F32 = jnp.float32
BF16 = jnp.bfloat16
VMEM_LIMIT = 16 * 2**20
SMALL_LIMIT = 4 * 2**20
ROUND = ((3, 1, 2), (2, 1, 3))
LARGE = 10**11


def build_gammas():
    sigmas = [
        np.array([[0, 1], [1, 0]], dtype=complex),
        np.array([[0, -1j], [1j, 0]], dtype=complex),
        np.array([[1, 0], [0, -1]], dtype=complex),
    ]
    zero, one = np.zeros((2, 2), dtype=complex), np.eye(2, dtype=complex)
    gammas = [np.block([[zero, 1j * s], [-1j * s, zero]]) for s in sigmas]
    gammas.append(np.block([[zero, one], [one, zero]]))
    tables = []
    for subset in range(16):
        product = np.eye(4, dtype=complex)
        for factor in range(4):
            if subset >> factor & 1:
                product = product @ gammas[factor]
        tables.append(product)
    return tables


def gamma_codes():
    words = [0, 0, 0, 0]
    for index, table in enumerate(build_gammas()):
        flip = gamma_flip(index)
        for row in range(4):
            entry = table[row, row ^ flip]
            power = [k for k in range(4) if abs(entry - 1j**k) < 1e-6]
            assert len(power) == 1 and np.count_nonzero(table[row]) == 1
            words[index // 4] |= power[0] << (8 * (index % 4) + 2 * row)
    return [word - 2**32 if word >= 2**31 else word for word in words]


def gamma_flip(index):
    b1, b2, b3, b4 = (index & 1, (index >> 1) & 1, (index >> 2) & 1, (index >> 3) & 1)
    return (b1 ^ b2) | ((b1 ^ b2 ^ b3 ^ b4) << 1)


def site_coords(site):
    coords = []
    for axis in range(3):
        total = jnp.zeros_like(site)
        for level in range(6):
            total = total + (((site >> (3 * level + axis)) & 1) << level)
        coords.append(total)
    return coords


def wave_phases(insertions, momenta_ref, pattern_row):
    sites = pattern_row.shape[1]
    fours = insertions // CLASSES
    first_site = (
        lax.axis_index("space") * lax.axis_size("sub") + lax.axis_index("sub")
    ) * sites
    site = lax.broadcasted_iota(jnp.int32, (1, sites), 1) + first_site
    coords = site_coords(site)
    rows = []
    for four in range(fours):
        wave = jnp.zeros_like(site)
        for axis in range(3):
            chosen = jnp.zeros_like(site)
            for kind in range(CLASSES):
                chosen = jnp.where(
                    pattern_row == kind, momenta_ref[axis, four * CLASSES + kind], chosen
                )
            wave = wave + coords[axis] * chosen
        laps = jnp.floor((wave.astype(F32) + 0.5) * (1.0 / LAT)).astype(jnp.int32)
        rows.append((wave - LAT * laps).astype(F32) * (2.0 * math.pi / LAT))
    angle = jnp.concatenate(rows, axis=0)
    return jnp.cos(angle), jnp.sin(angle)


def multiply_slots(
    insertions, slots, gamma_ref, pattern_row, sink_mat, turned, buffers, out
):
    _, comps, _, nmode, sites = turned.shape
    colours = comps // 4
    words = gamma_codes()
    parts = len(buffers)
    per_part = comps // parts
    plan = []
    for slot in slots:
        g = insertions[slot]
        index = gamma_ref[g]
        word = jnp.int32(words[3])
        for step in (2, 1, 0):
            word = jnp.where(index < 4 * (step + 1), jnp.int32(words[step]), word)
        code = word >> (8 * (index & 3))
        mask = jnp.where(pattern_row == lax.rem(g, CLASSES), 1.0, 0.0)
        rows = []
        for spin in range(4):
            power = (code >> (2 * spin)) & 3
            real_sign = jnp.where((power == 0) | (power == 3), 1.0, -1.0)
            imag_sign = jnp.where(power < 2, 1.0, -1.0)
            rows.append(
                (
                    power & 1,
                    (gamma_flip(index) ^ spin) * colours,
                    (mask * real_sign).astype(BF16),
                    (mask * imag_sign).astype(BF16),
                )
            )
        plan.append((g // CLASSES, rows))
    for part in range(parts):
        buffer = buffers[part]
        for k, (four, rows) in enumerate(plan):
            base = k * nmode
            for step in range(per_part):
                comp = part * per_part + step
                odd, taken, real_row, imag_row = rows[comp // colours]
                source = taken + comp % colours
                at = step * 2 * sites
                buffer[base : base + nmode, at : at + sites] = (
                    turned[four, source, odd] * real_row
                )
                buffer[base : base + nmode, at + sites : at + 2 * sites] = (
                    turned[four, source, 1 - odd] * imag_row
                )
        width = per_part * 2 * sites
        block = lax.dot_general(
            buffer[...],
            sink_mat[:, part * width : (part + 1) * width],
            (((1,), (1,)), ((), ())),
            preferred_element_type=F32,
        ).reshape(out.shape)
        out[...] = block if part == 0 else out[...] + block


def first_kernel(order, time, slots, chunks, ahead, loaded, waits, *refs):
    sink_src, source_src, gamma_hbm, momenta_hbm, pattern_hbm, *refs = refs
    out, sink_mat, turned, *refs = refs[waits:]
    nexts, refs = (refs[:2], refs[2:]) if ahead else ([], refs)
    sink_stage, source_stage, gamma_ref, momenta_ref, pattern_ref, *refs = refs
    small_sems, big_sems, next_sems, *refs = refs
    raws, buffers = ([sink_src, source_src], refs) if loaded else (refs[:2], refs[2:])
    rows, sites = sink_stage.shape
    fours, _, _, nmode, _ = turned.shape
    per_mode = rows // nmode
    comps = per_mode // 2
    insertions = order()
    height = rows // chunks

    small = [
        pltpu.make_async_copy(src, dst, small_sems.at[k])
        for k, (src, dst) in enumerate(
            [(momenta_hbm, momenta_ref), (pattern_hbm, pattern_ref), (gamma_hbm, gamma_ref)]
        )
    ]
    big, later = [], []
    if not loaded:
        for which, (src, dst) in enumerate(zip((sink_src, source_src), raws)):
            for k in range(chunks):
                part = pl.ds(k * height, height)
                sem = big_sems.at[which * chunks + k]
                big.append(pltpu.make_async_copy(src.at[time, part], dst.at[part], sem))
    for k, (src, dst) in enumerate(zip((sink_src, source_src), nexts)):
        later.append(pltpu.make_async_copy(src.at[time + 1], dst, next_sems.at[k]))
    for copy in small + big + later:
        copy.start()

    def stage(which, dst):
        for k in range(chunks):
            part = slice(k * height, (k + 1) * height)
            if not loaded:
                big[which * chunks + k].wait()
            dst[part] = raws[which][part].astype(F32)

    stage(0, sink_stage)
    for comp in range(comps):
        at = comp * 2 * sites
        real = sink_stage[pl.ds(2 * comp, nmode, stride=per_mode), :].astype(BF16)
        imag = sink_stage[pl.ds(2 * comp + 1, nmode, stride=per_mode), :].astype(BF16)
        sink_mat[0:nmode, at : at + sites] = real
        sink_mat[0:nmode, at + sites : at + 2 * sites] = imag
        sink_mat[nmode:, at : at + sites] = -imag
        sink_mat[nmode:, at + sites : at + 2 * sites] = real
    for copy in small:
        copy.wait()
    pattern_row = pattern_ref[time : time + 1, :]
    cosine, sine = wave_phases(fours * CLASSES, momenta_ref, pattern_row)
    stage(1, source_stage)
    for comp in range(comps):
        real = source_stage[pl.ds(2 * comp, nmode, stride=per_mode), :]
        imag = source_stage[pl.ds(2 * comp + 1, nmode, stride=per_mode), :]
        for four in range(fours):
            cos_row, sin_row = cosine[four : four + 1], sine[four : four + 1]
            turned[four, comp, 0] = (real * cos_row - imag * sin_row).astype(BF16)
            turned[four, comp, 1] = (real * sin_row + imag * cos_row).astype(BF16)
    multiply_slots(insertions, slots, gamma_ref, pattern_row, sink_mat, turned, buffers, out)
    for copy in later:
        copy.wait()


def block_cost(slots, nmode, depth):
    return pl.CostEstimate(
        flops=100 * slots * nmode * nmode * depth,
        bytes_accessed=8 * nmode * depth,
        transcendentals=0,
    )


def product_buffers(slots, nmode, depth):
    parts = 2
    return [pltpu.VMEM((slots * nmode, depth // parts), BF16)] * parts


def first_blocks(modes, small, time, nmode, order, slots, ahead=False, after=()):
    rows, sites = modes[0].shape[-2:]
    loaded = modes[0].ndim == 2
    comps = rows // nmode // 2
    depth = comps * 2 * sites
    chunks = 4 if rows % 64 == 0 else 1
    gamma_index, momenta, pattern = small
    fours = gamma_index.shape[0] // CLASSES
    raw = [pltpu.VMEM((rows, sites), BF16)] * 2
    where = pltpu.VMEM if loaded else pltpu.HBM
    if not loaded:
        modes = in_hbm(modes)
    return pl.pallas_call(
        functools.partial(first_kernel, order, time, slots, chunks, ahead, loaded, len(after)),
        in_specs=[pl.BlockSpec(memory_space=where)] * 2
        + [pl.BlockSpec(memory_space=pltpu.HBM)] * 3
        + [pl.BlockSpec(memory_space=pl.ANY)] * len(after),
        out_shape=[
            pltpu.VMEM((len(slots), nmode, 2 * nmode), F32),
            pltpu.VMEM((2 * nmode, depth), BF16),
            pltpu.VMEM((fours, comps, 2, nmode, sites), BF16),
        ]
        + (raw if ahead else []),
        scratch_shapes=[
            pltpu.VMEM((rows, sites), F32),
            pltpu.VMEM((rows, sites), F32),
            pltpu.SMEM(gamma_index.shape, jnp.int32),
            pltpu.SMEM(momenta.shape, jnp.int32),
            pltpu.VMEM(pattern.shape, jnp.int32),
            pltpu.SemaphoreType.DMA((3,)),
            pltpu.SemaphoreType.DMA((2 * chunks,)),
            pltpu.SemaphoreType.DMA((2,)),
        ]
        + ([] if loaded else raw)
        + product_buffers(len(slots), nmode, depth),
        compiler_params=pltpu.CompilerParams(vmem_limit_bytes=VMEM_LIMIT),
        cost_estimate=block_cost(len(slots), nmode, depth),
        name="first_blocks",
    )(*modes, *in_hbm(small), *after)


def in_hbm(arrays):
    return [pltpu.with_memory_space_constraint(a, pltpu.HBM) for a in arrays]


def later_kernel(order, time, slots, gamma_ref, pattern_ref, sink_mat, turned, out, *buffers):
    pattern_row = pattern_ref[time : time + 1, :]
    multiply_slots(order(), slots, gamma_ref, pattern_row, sink_mat, turned, buffers, out)


def later_blocks(gamma_index, pattern, sink_mat, turned, time, order, slots):
    nmode, depth = turned.shape[3], sink_mat.shape[1]
    return pl.pallas_call(
        functools.partial(later_kernel, order, time, slots),
        in_specs=[pl.BlockSpec(memory_space=pltpu.SMEM)]
        + [pl.BlockSpec(memory_space=pltpu.VMEM)] * 3,
        out_shape=pltpu.VMEM((len(slots), nmode, 2 * nmode), F32),
        scratch_shapes=product_buffers(len(slots), nmode, depth),
        compiler_params=pltpu.CompilerParams(vmem_limit_bytes=VMEM_LIMIT),
        cost_estimate=block_cost(len(slots), nmode, depth),
        name="later_blocks",
    )(gamma_index, pattern, sink_mat, turned)


def small_call(kernel, outs, name, *args, flops=1, after=(), scratch=()):
    return pl.pallas_call(
        kernel,
        in_specs=[pl.BlockSpec(memory_space=pltpu.VMEM)] * len(args)
        + [pl.BlockSpec(memory_space=pl.ANY)] * len(after),
        out_shape=outs,
        scratch_shapes=scratch,
        compiler_params=pltpu.CompilerParams(vmem_limit_bytes=SMALL_LIMIT),
        cost_estimate=pl.CostEstimate(flops=flops, bytes_accessed=1, transcendentals=0),
        name=name,
    )(*args, *after)


def add_units(keep, got):
    def kernel(keep_ref, got_ref, *outs):
        for slot, out in enumerate(outs):
            out[...] = keep_ref[slot] + got_ref[slot]

    units, rows, columns = keep.shape
    outs = [pltpu.VMEM((rows, columns), F32)] * units
    return small_call(kernel, outs, "add_cores", keep, got)


def sum_units(terms, scale, after=()):
    def kernel(*refs):
        total = refs[0][...]
        for ref in refs[1 : len(terms)]:
            total = total + ref[...]
        refs[-1][...] = total * scale

    out = pltpu.VMEM(terms[0].shape, F32)
    return small_call(kernel, out, "sum_chips", *terms, after=after)


def write_rows(whole, lane, spaces, subs, cores, outs):
    row_count = outs[0].shape[3]
    z, core = lax.axis_index("space"), lax.axis_index("sub")
    for c, out in zip(cores, outs, strict=True):
        for s in range(spaces):
            start = pl.multiple_of(((z ^ s) * subs + (core ^ c)) * row_count, row_count)
            for part in range(2):
                out[s, lane, part] = whole[part, pl.ds(start, row_count), :]


def turn(matrix, whole):
    nmode = matrix.shape[1] // 2
    for part in range(2):
        whole[part] = matrix[:, part * nmode : (part + 1) * nmode].T


def turn_field(field, after):
    def kernel(field_ref, *refs):
        turn(field_ref[...], refs[-1])

    nmode = field.shape[0]
    out = pltpu.VMEM((2, nmode, nmode), F32)
    return small_call(kernel, out, "turn_field", field, flops=LARGE, after=after)


def split_rows(whole, field, spaces, subs):
    nmode = whole.shape[1]

    def kernel(whole_ref, field_ref, away, keep, staging):
        turn(field_ref[...], staging)
        for lane, source in enumerate((whole_ref, staging)):
            write_rows(source, lane, spaces, subs, [1, 0], [away, keep])

    outs = [pltpu.VMEM((spaces, 2, 2, nmode // (spaces * subs), nmode), F32)] * 2
    scratch = [pltpu.VMEM((2, nmode, nmode), F32)]
    return small_call(kernel, outs, "split_rows", whole, field, scratch=scratch, flops=LARGE)


def product_kernel(spaces, subs, tms, pairs_ref, *refs):
    fields, (away, whole, held) = refs[:-3], refs[-3:]
    nmode = fields[0].shape[0]
    times = len(fields) // tms
    mine = lax.axis_index("tm")
    for other in range(tms):
        for time in range(times):
            held[(mine ^ other) * times + time] = fields[other * times + time][...]
    for pair in range(pairs_ref.shape[0]):
        left, right = held[pairs_ref[pair, 0]], held[pairs_ref[pair, 1]]
        swapped = jnp.concatenate([-left[:, nmode:], left[:, :nmode]], axis=1)
        result = lax.dot_general(
            right,
            jnp.concatenate([left, swapped], axis=0),
            (((1,), (0,)), ((), ())),
            preferred_element_type=F32,
            precision=lax.Precision.HIGHEST,
        ) * (1.0 / math.sqrt(nmode))
        turn(result, whole.at[pair])
        write_rows(whole.at[pair], pair, spaces, subs, [1], [away])


def product_rows(time_pairs, fields, spaces, subs, tms):
    nmode, pairs = fields[0].shape[0], time_pairs.shape[0]
    shape = (spaces, pairs, 2, nmode // (spaces * subs), nmode)
    return pl.pallas_call(
        functools.partial(product_kernel, spaces, subs, tms),
        in_specs=[pl.BlockSpec(memory_space=pltpu.SMEM)]
        + [pl.BlockSpec(memory_space=pltpu.VMEM)] * len(fields),
        out_shape=[pltpu.VMEM(shape, F32), pltpu.VMEM((pairs, 2, nmode, nmode), F32)],
        scratch_shapes=[pltpu.VMEM((len(fields), nmode, 2 * nmode), F32)],
        compiler_params=pltpu.CompilerParams(vmem_limit_bytes=SMALL_LIMIT),
        cost_estimate=pl.CostEstimate(
            flops=8 * pairs * nmode**3, bytes_accessed=64 * nmode * nmode, transcendentals=0
        ),
        name="products",
    )(time_pairs, *fields)


def keep_rows(whole, spaces, subs):
    lanes, _, nmode, _ = whole.shape

    def kernel(whole_ref, out):
        for lane in range(lanes):
            write_rows(whole_ref.at[lane], lane, spaces, subs, [0], [out])

    out = pltpu.VMEM((spaces, lanes, 2, nmode // (spaces * subs), nmode), F32)
    return small_call(kernel, out, "keep_rows", whole, flops=LARGE)


def pair_cores(keep, got):
    shape = keep.shape

    def kernel(keep_ref, got_ref, *outs):
        for s, out in enumerate(outs):
            out[0] = keep_ref[s]
            out[1] = got_ref[s]

    outs = [pltpu.VMEM((2,) + shape[1:], F32)] * shape[0]
    return small_call(kernel, outs, "pair_cores", keep, got)


def put_blocks(args, places, arrays, spaces, subs, name, flops):
    lanes, _, row_count, nmode = args[0].shape[-4:]
    count = len(arrays)

    def kernel(*refs):
        outs, sems = refs[-1 - count : -1], refs[-1]
        refs = refs[len(given) :]
        z, core = lax.axis_index("space"), lax.axis_index("sub")
        copies = []
        for out, group in zip(outs, places, strict=True):
            for s, operand, index in group:
                block = refs[operand] if index is None else refs[operand].at[index]
                for c in range(subs):
                    copy = pltpu.make_async_copy(
                        block.at[c],
                        out.at[:, (z ^ s) * subs + (core ^ c)],
                        sems.at[len(copies)],
                    )
                    copy.start()
                    copies.append(copy)
        for copy in copies:
            copy.wait()

    out = jax.ShapeDtypeStruct((lanes, spaces * subs, 2, row_count, nmode), F32)
    given = [(k, array) for k, array in enumerate(arrays) if array is not None]
    return pl.pallas_call(
        kernel,
        in_specs=[pl.BlockSpec(memory_space=pltpu.HBM)] * len(given)
        + [pl.BlockSpec(memory_space=pltpu.VMEM)] * len(args),
        out_specs=[pl.BlockSpec(memory_space=pltpu.HBM)] * count,
        out_shape=[out] * count,
        input_output_aliases={n: k for n, (k, _) in enumerate(given)},
        scratch_shapes=[pltpu.SemaphoreType.DMA((sum(map(len, places)) * subs,))],
        compiler_params=pltpu.CompilerParams(vmem_limit_bytes=SMALL_LIMIT),
        cost_estimate=pl.CostEstimate(flops=flops, bytes_accessed=1, transcendentals=0),
        name=name,
    )(*(array for _, array in given), *args)


def swap(value, axis, distance):
    size = lax.axis_size(axis)
    return lax.ppermute(value, axis, [(i, i ^ distance) for i in range(size)])


def own_insertions(spaces, subs):
    z, core = lax.axis_index("space"), lax.axis_index("sub")
    return [(z ^ s) * subs + (core ^ c) for c in range(subs) for s in range(spaces)]


def by_owner(sink, source, gamma_index, momenta, pattern, time_pairs, nmode, times, scale):
    spaces, subs, tms = (lax.axis_size(name) for name in ("space", "sub", "tm"))
    order = functools.partial(own_insertions, spaces, subs)
    mine, other = list(range(spaces)), list(range(spaces, 2 * spaces))
    small = (gamma_index, momenta, pattern)

    def send(away, laid, time):
        got = swap(away, "sub", 1)
        keep = later_blocks(gamma_index, pattern, *laid, time, order, mine)
        parts = add_units(keep, got)
        return [parts[0]] + [swap(parts[s], "space", s) for s in ROUND[time]]

    away, sink_mat, turned, *modes = first_blocks(
        (sink, source), small, 0, nmode, order, other, ahead=True
    )
    first = send(away, (sink_mat, turned), 0)
    away, sink_mat, turned = first_blocks(modes, small, 1, nmode, order, other, after=first[:1])
    second = send(away, (sink_mat, turned), 1)
    first = sum_units(first, scale)
    first_other = swap(first, "tm", 1)
    whole = turn_field(first, second[1:])
    second = sum_units(second, scale, [first_other, whole])
    second_other = swap(second, "tm", 1)

    away, keep = split_rows(whole, second, spaces, subs)
    meson = pair_cores(keep, swap(away, "sub", 1))
    own, near, two, three = meson
    two, three, near = (swap(v, "space", s) for v, s in ((two, 2), (three, 3), (near, 1)))
    fields = [first, second, first_other, second_other]
    away, whole = product_rows(time_pairs, fields, spaces, subs, tms)
    got = swap(away, "sub", 1)
    products = pair_cores(keep_rows(whole, spaces, subs), got)
    places = [
        [(0, 0, None), (1, 3, None), (2, 2, None), (3, 1, None)],
        [(0, 4, None)],
    ]
    meson_parts = [own, three, two, near]
    own, near, two, three = products
    two, three, near = (swap(v, "space", s) for v, s in ((two, 2), (three, 3), (near, 1)))
    meson, products = put_blocks(
        meson_parts + [own], places, [None, None], spaces, subs, "put_early", LARGE
    )
    places = [[(1, 1, None), (2, 0, None), (3, 2, None)]]
    (products,) = put_blocks([two, near, three], places, [products], spaces, subs, "put_late", 1)
    return meson, products


def by_rows(sink, source, gamma_index, momenta, pattern, time_pairs, nmode, times, scale):
    axes = ("space", "sub")
    highest = lax.Precision.HIGHEST
    insertions = gamma_index.shape[0]
    partial = jnp.stack(
        [
            first_blocks(
                (sink, source),
                (gamma_index, momenta, pattern),
                time,
                nmode,
                lambda: list(range(insertions)),
                list(range(insertions)),
            )[0]
            for time in range(times)
        ]
    )
    partial = partial.reshape(times, insertions, nmode, 2, nmode).transpose(0, 1, 3, 4, 2)
    meson = lax.psum_scatter(partial * scale, axes, scatter_dimension=3, tiled=True)
    rows = lax.all_gather(meson, "tm", axis=0, tiled=True)
    whole = lax.all_gather(rows, axes, axis=3, tiled=True)
    left, right = rows[time_pairs[:, 0]], whole[time_pairs[:, 1]]

    def multiply(a, b):
        return jnp.einsum("qgik,qgkj->qgij", a, b, precision=highest)

    real = multiply(left[:, :, 0], right[:, :, 0]) - multiply(left[:, :, 1], right[:, :, 1])
    imag = multiply(left[:, :, 0], right[:, :, 1]) + multiply(left[:, :, 1], right[:, :, 0])
    return meson, jnp.stack([real, imag], axis=2) / math.sqrt(nmode)


def local(sink_modes, source_modes, gamma_index, momenta, pattern, time_pairs):
    times, nmode, _, comps, sites = sink_modes.shape
    spaces, subs, tms = (lax.axis_size(name) for name in ("space", "sub", "tm"))

    def as_rows(modes):
        return modes.transpose(0, 1, 3, 2, 4).reshape(times, nmode * comps * 2, sites)

    owners = (
        (spaces, subs, tms, times) == (4, 2, 2, 2)
        and gamma_index.shape[0] == spaces * subs
        and time_pairs.shape[0] == times
    )
    plan = by_owner if owners else by_rows
    arrays = (as_rows(sink_modes), as_rows(source_modes), gamma_index, momenta.T, pattern)
    scale = 1.0 / math.sqrt(3 * sites * spaces * subs)
    return plan(*arrays, time_pairs, nmode, times, scale)


def solution(mesh):
    rows = P(("grp", "tm"), None, None, None, ("space", "sub"))
    in_specs = (rows, rows, P(), P(), P("tm", ("space", "sub")), P("tm", None))
    out_specs = (P(("grp", "tm"), None, None, ("space", "sub"), None),) * 2
    return jax.shard_map(local, mesh=mesh, in_specs=in_specs, out_specs=out_specs, check_vma=False)
```

```python
import functools
import math

import jax
import jax.numpy as jnp
import numpy as np
from jax import lax
from jax.experimental import pallas as pl
from jax.experimental.pallas import tpu as pltpu
from jax.sharding import PartitionSpec as P

LAT = 96
CLASSES = 4
F32 = jnp.float32
BF16 = jnp.bfloat16
VMEM_LIMIT = 16 * 2**20
SMALL_LIMIT = 4 * 2**20
ROUND = ((3, 1, 2), (2, 1, 3))
LARGE = 10**11


def build_gammas():
    sigmas = [
        np.array([[0, 1], [1, 0]], dtype=complex),
        np.array([[0, -1j], [1j, 0]], dtype=complex),
        np.array([[1, 0], [0, -1]], dtype=complex),
    ]
    zero, one = np.zeros((2, 2), dtype=complex), np.eye(2, dtype=complex)
    gammas = [np.block([[zero, 1j * s], [-1j * s, zero]]) for s in sigmas]
    gammas.append(np.block([[zero, one], [one, zero]]))
    tables = []
    for subset in range(16):
        product = np.eye(4, dtype=complex)
        for factor in range(4):
            if subset >> factor & 1:
                product = product @ gammas[factor]
        tables.append(product)
    return tables


def gamma_codes():
    words = [0, 0, 0, 0]
    for index, table in enumerate(build_gammas()):
        flip = gamma_flip(index)
        for row in range(4):
            entry = table[row, row ^ flip]
            power = [k for k in range(4) if abs(entry - 1j**k) < 1e-6]
            assert len(power) == 1 and np.count_nonzero(table[row]) == 1
            words[index // 4] |= power[0] << (8 * (index % 4) + 2 * row)
    return [word - 2**32 if word >= 2**31 else word for word in words]


def gamma_flip(index):
    b1, b2, b3, b4 = (index & 1, (index >> 1) & 1, (index >> 2) & 1, (index >> 3) & 1)
    return (b1 ^ b2) | ((b1 ^ b2 ^ b3 ^ b4) << 1)


def site_coords(site):
    coords = []
    for axis in range(3):
        total = jnp.zeros_like(site)
        for level in range(6):
            total = total + (((site >> (3 * level + axis)) & 1) << level)
        coords.append(total)
    return coords


def wave_phases(insertions, momenta_ref, pattern_row):
    sites = pattern_row.shape[1]
    fours = insertions // CLASSES
    first_site = (
        lax.axis_index("space") * lax.axis_size("sub") + lax.axis_index("sub")
    ) * sites
    site = lax.broadcasted_iota(jnp.int32, (1, sites), 1) + first_site
    coords = site_coords(site)
    rows = []
    for four in range(fours):
        wave = jnp.zeros_like(site)
        for axis in range(3):
            chosen = jnp.zeros_like(site)
            for kind in range(CLASSES):
                chosen = jnp.where(
                    pattern_row == kind, momenta_ref[axis, four * CLASSES + kind], chosen
                )
            wave = wave + coords[axis] * chosen
        laps = jnp.floor((wave.astype(F32) + 0.5) * (1.0 / LAT)).astype(jnp.int32)
        rows.append((wave - LAT * laps).astype(F32) * (2.0 * math.pi / LAT))
    angle = jnp.concatenate(rows, axis=0)
    return jnp.cos(angle), jnp.sin(angle)


def multiply_slots(
    insertions, slots, gamma_ref, pattern_row, sink_mat, turned, buffers, out
):
    _, comps, _, nmode, sites = turned.shape
    colours = comps // 4
    words = gamma_codes()
    parts = len(buffers)
    per_part = comps // parts
    plan = []
    for slot in slots:
        g = insertions[slot]
        index = gamma_ref[g]
        word = jnp.int32(words[3])
        for step in (2, 1, 0):
            word = jnp.where(index < 4 * (step + 1), jnp.int32(words[step]), word)
        code = word >> (8 * (index & 3))
        mask = jnp.where(pattern_row == lax.rem(g, CLASSES), 1.0, 0.0)
        rows = []
        for spin in range(4):
            power = (code >> (2 * spin)) & 3
            real_sign = jnp.where((power == 0) | (power == 3), 1.0, -1.0)
            imag_sign = jnp.where(power < 2, 1.0, -1.0)
            rows.append(
                (
                    power & 1,
                    (gamma_flip(index) ^ spin) * colours,
                    (mask * real_sign).astype(BF16),
                    (mask * imag_sign).astype(BF16),
                )
            )
        plan.append((g // CLASSES, rows))
    for part in range(parts):
        buffer = buffers[part]
        for k, (four, rows) in enumerate(plan):
            base = k * nmode
            for step in range(per_part):
                comp = part * per_part + step
                odd, taken, real_row, imag_row = rows[comp // colours]
                source = taken + comp % colours
                at = step * 2 * sites
                buffer[base : base + nmode, at : at + sites] = (
                    turned[four, source, odd] * real_row
                )
                buffer[base : base + nmode, at + sites : at + 2 * sites] = (
                    turned[four, source, 1 - odd] * imag_row
                )
        width = per_part * 2 * sites
        block = lax.dot_general(
            buffer[...],
            sink_mat[:, part * width : (part + 1) * width],
            (((1,), (1,)), ((), ())),
            preferred_element_type=F32,
        ).reshape(out.shape)
        out[...] = block if part == 0 else out[...] + block


def first_kernel(order, time, slots, chunks, ahead, loaded, waits, *refs):
    sink_src, source_src, gamma_hbm, momenta_hbm, pattern_hbm, *refs = refs
    out, sink_mat, turned, *refs = refs[waits:]
    nexts, refs = (refs[:2], refs[2:]) if ahead else ([], refs)
    sink_stage, source_stage, gamma_ref, momenta_ref, pattern_ref, *refs = refs
    small_sems, big_sems, next_sems, *refs = refs
    raws, buffers = ([sink_src, source_src], refs) if loaded else (refs[:2], refs[2:])
    rows, sites = sink_stage.shape
    fours, _, _, nmode, _ = turned.shape
    per_mode = rows // nmode
    comps = per_mode // 2
    insertions = order()
    height = rows // chunks

    small = [
        pltpu.make_async_copy(src, dst, small_sems.at[k])
        for k, (src, dst) in enumerate(
            [(momenta_hbm, momenta_ref), (pattern_hbm, pattern_ref), (gamma_hbm, gamma_ref)]
        )
    ]
    big, later = [], []
    if not loaded:
        for which, (src, dst) in enumerate(zip((sink_src, source_src), raws)):
            for k in range(chunks):
                part = pl.ds(k * height, height)
                sem = big_sems.at[which * chunks + k]
                big.append(pltpu.make_async_copy(src.at[time, part], dst.at[part], sem))
    for k, (src, dst) in enumerate(zip((sink_src, source_src), nexts)):
        later.append(pltpu.make_async_copy(src.at[time + 1], dst, next_sems.at[k]))
    for copy in small + big + later:
        copy.start()

    def stage(which, dst):
        for k in range(chunks):
            part = slice(k * height, (k + 1) * height)
            if not loaded:
                big[which * chunks + k].wait()
            dst[part] = raws[which][part].astype(F32)

    stage(0, sink_stage)
    for comp in range(comps):
        at = comp * 2 * sites
        real = sink_stage[pl.ds(2 * comp, nmode, stride=per_mode), :].astype(BF16)
        imag = sink_stage[pl.ds(2 * comp + 1, nmode, stride=per_mode), :].astype(BF16)
        sink_mat[0:nmode, at : at + sites] = real
        sink_mat[0:nmode, at + sites : at + 2 * sites] = imag
        sink_mat[nmode:, at : at + sites] = -imag
        sink_mat[nmode:, at + sites : at + 2 * sites] = real
    for copy in small:
        copy.wait()
    pattern_row = pattern_ref[time : time + 1, :]
    cosine, sine = wave_phases(fours * CLASSES, momenta_ref, pattern_row)
    stage(1, source_stage)
    for comp in range(comps):
        real = source_stage[pl.ds(2 * comp, nmode, stride=per_mode), :]
        imag = source_stage[pl.ds(2 * comp + 1, nmode, stride=per_mode), :]
        for four in range(fours):
            cos_row, sin_row = cosine[four : four + 1], sine[four : four + 1]
            turned[four, comp, 0] = (real * cos_row - imag * sin_row).astype(BF16)
            turned[four, comp, 1] = (real * sin_row + imag * cos_row).astype(BF16)
    multiply_slots(insertions, slots, gamma_ref, pattern_row, sink_mat, turned, buffers, out)
    for copy in later:
        copy.wait()


def block_cost(slots, nmode, depth):
    return pl.CostEstimate(
        flops=100 * slots * nmode * nmode * depth,
        bytes_accessed=8 * nmode * depth,
        transcendentals=0,
    )


def product_buffers(slots, nmode, depth):
    parts = 2
    return [pltpu.VMEM((slots * nmode, depth // parts), BF16)] * parts


def first_blocks(modes, small, time, nmode, order, slots, ahead=False, after=()):
    rows, sites = modes[0].shape[-2:]
    loaded = modes[0].ndim == 2
    comps = rows // nmode // 2
    depth = comps * 2 * sites
    chunks = 4 if rows % 64 == 0 else 1
    gamma_index, momenta, pattern = small
    fours = gamma_index.shape[0] // CLASSES
    raw = [pltpu.VMEM((rows, sites), BF16)] * 2
    where = pltpu.VMEM if loaded else pltpu.HBM
    if not loaded:
        modes = in_hbm(modes)
    return pl.pallas_call(
        functools.partial(first_kernel, order, time, slots, chunks, ahead, loaded, len(after)),
        in_specs=[pl.BlockSpec(memory_space=where)] * 2
        + [pl.BlockSpec(memory_space=pltpu.HBM)] * 3
        + [pl.BlockSpec(memory_space=pl.ANY)] * len(after),
        out_shape=[
            pltpu.VMEM((len(slots), nmode, 2 * nmode), F32),
            pltpu.VMEM((2 * nmode, depth), BF16),
            pltpu.VMEM((fours, comps, 2, nmode, sites), BF16),
        ]
        + (raw if ahead else []),
        scratch_shapes=[
            pltpu.VMEM((rows, sites), F32),
            pltpu.VMEM((rows, sites), F32),
            pltpu.SMEM(gamma_index.shape, jnp.int32),
            pltpu.SMEM(momenta.shape, jnp.int32),
            pltpu.VMEM(pattern.shape, jnp.int32),
            pltpu.SemaphoreType.DMA((3,)),
            pltpu.SemaphoreType.DMA((2 * chunks,)),
            pltpu.SemaphoreType.DMA((2,)),
        ]
        + ([] if loaded else raw)
        + product_buffers(len(slots), nmode, depth),
        compiler_params=pltpu.CompilerParams(vmem_limit_bytes=VMEM_LIMIT),
        cost_estimate=block_cost(len(slots), nmode, depth),
        name="first_blocks",
    )(*modes, *in_hbm(small), *after)


def in_hbm(arrays):
    return [pltpu.with_memory_space_constraint(a, pltpu.HBM) for a in arrays]


def later_kernel(order, time, slots, gamma_ref, pattern_ref, sink_mat, turned, out, *buffers):
    pattern_row = pattern_ref[time : time + 1, :]
    multiply_slots(order(), slots, gamma_ref, pattern_row, sink_mat, turned, buffers, out)


def later_blocks(gamma_index, pattern, sink_mat, turned, time, order, slots):
    nmode, depth = turned.shape[3], sink_mat.shape[1]
    return pl.pallas_call(
        functools.partial(later_kernel, order, time, slots),
        in_specs=[pl.BlockSpec(memory_space=pltpu.SMEM)]
        + [pl.BlockSpec(memory_space=pltpu.VMEM)] * 3,
        out_shape=pltpu.VMEM((len(slots), nmode, 2 * nmode), F32),
        scratch_shapes=product_buffers(len(slots), nmode, depth),
        compiler_params=pltpu.CompilerParams(vmem_limit_bytes=VMEM_LIMIT),
        cost_estimate=block_cost(len(slots), nmode, depth),
        name="later_blocks",
    )(gamma_index, pattern, sink_mat, turned)


def small_call(kernel, outs, name, *args, flops=1, after=(), scratch=()):
    return pl.pallas_call(
        kernel,
        in_specs=[pl.BlockSpec(memory_space=pltpu.VMEM)] * len(args)
        + [pl.BlockSpec(memory_space=pl.ANY)] * len(after),
        out_shape=outs,
        scratch_shapes=scratch,
        compiler_params=pltpu.CompilerParams(vmem_limit_bytes=SMALL_LIMIT),
        cost_estimate=pl.CostEstimate(flops=flops, bytes_accessed=1, transcendentals=0),
        name=name,
    )(*args, *after)


def add_units(keep, got):
    def kernel(keep_ref, got_ref, *outs):
        for slot, out in enumerate(outs):
            out[...] = keep_ref[slot] + got_ref[slot]

    units, rows, columns = keep.shape
    outs = [pltpu.VMEM((rows, columns), F32)] * units
    return small_call(kernel, outs, "add_cores", keep, got)


def sum_units(terms, scale, after=()):
    def kernel(*refs):
        total = refs[0][...]
        for ref in refs[1 : len(terms)]:
            total = total + ref[...]
        refs[-1][...] = total * scale

    out = pltpu.VMEM(terms[0].shape, F32)
    return small_call(kernel, out, "sum_chips", *terms, after=after)


def write_rows(whole, lane, spaces, subs, cores, outs):
    row_count = outs[0].shape[3]
    z, core = lax.axis_index("space"), lax.axis_index("sub")
    for c, out in zip(cores, outs, strict=True):
        for s in range(spaces):
            start = pl.multiple_of(((z ^ s) * subs + (core ^ c)) * row_count, row_count)
            for part in range(2):
                out[s, lane, part] = whole[part, pl.ds(start, row_count), :]


def turn(matrix, whole):
    nmode = matrix.shape[1] // 2
    for part in range(2):
        whole[part] = matrix[:, part * nmode : (part + 1) * nmode].T


def turn_field(field, after):
    def kernel(field_ref, *refs):
        turn(field_ref[...], refs[-1])

    nmode = field.shape[0]
    out = pltpu.VMEM((2, nmode, nmode), F32)
    return small_call(kernel, out, "turn_field", field, flops=LARGE, after=after)


def split_rows(whole, field, spaces, subs):
    nmode = whole.shape[1]

    def kernel(whole_ref, field_ref, away, keep, staging):
        turn(field_ref[...], staging)
        for lane, source in enumerate((whole_ref, staging)):
            write_rows(source, lane, spaces, subs, [1, 0], [away, keep])

    outs = [pltpu.VMEM((spaces, 2, 2, nmode // (spaces * subs), nmode), F32)] * 2
    scratch = [pltpu.VMEM((2, nmode, nmode), F32)]
    return small_call(kernel, outs, "split_rows", whole, field, scratch=scratch, flops=LARGE)


def split_dot(a, b):
    a_high, b_high = a.astype(BF16), b.astype(BF16)
    a_low = (a - a_high.astype(F32)).astype(BF16)
    b_low = (b - b_high.astype(F32)).astype(BF16)

    def dot(x, y):
        return lax.dot_general(x, y, (((1,), (0,)), ((), ())), preferred_element_type=F32)

    small = dot(a_low, b_low) + dot(a_low, b_high) + dot(a_high, b_low)
    return small + dot(a_high, b_high)


def product_kernel(spaces, subs, tms, pairs_ref, *refs):
    fields, (away, whole, held) = refs[:-3], refs[-3:]
    nmode = fields[0].shape[0]
    times = len(fields) // tms
    mine = lax.axis_index("tm")
    for other in range(tms):
        for time in range(times):
            held[(mine ^ other) * times + time] = fields[other * times + time][...]
    for pair in range(pairs_ref.shape[0]):
        left, right = held[pairs_ref[pair, 0]], held[pairs_ref[pair, 1]]
        swapped = jnp.concatenate([-left[:, nmode:], left[:, :nmode]], axis=1)
        result = split_dot(right, jnp.concatenate([left, swapped], axis=0)) * (
            1.0 / math.sqrt(nmode)
        )
        turn(result, whole.at[pair])
        write_rows(whole.at[pair], pair, spaces, subs, [1], [away])


def product_rows(time_pairs, fields, spaces, subs, tms):
    nmode, pairs = fields[0].shape[0], time_pairs.shape[0]
    shape = (spaces, pairs, 2, nmode // (spaces * subs), nmode)
    return pl.pallas_call(
        functools.partial(product_kernel, spaces, subs, tms),
        in_specs=[pl.BlockSpec(memory_space=pltpu.SMEM)]
        + [pl.BlockSpec(memory_space=pltpu.VMEM)] * len(fields),
        out_shape=[pltpu.VMEM(shape, F32), pltpu.VMEM((pairs, 2, nmode, nmode), F32)],
        scratch_shapes=[pltpu.VMEM((len(fields), nmode, 2 * nmode), F32)],
        compiler_params=pltpu.CompilerParams(vmem_limit_bytes=SMALL_LIMIT),
        cost_estimate=pl.CostEstimate(
            flops=8 * pairs * nmode**3, bytes_accessed=64 * nmode * nmode, transcendentals=0
        ),
        name="products",
    )(time_pairs, *fields)


def keep_rows(whole, spaces, subs):
    lanes, _, nmode, _ = whole.shape

    def kernel(whole_ref, out):
        for lane in range(lanes):
            write_rows(whole_ref.at[lane], lane, spaces, subs, [0], [out])

    out = pltpu.VMEM((spaces, lanes, 2, nmode // (spaces * subs), nmode), F32)
    return small_call(kernel, out, "keep_rows", whole, flops=LARGE)


def pair_cores(keep, got):
    shape = keep.shape

    def kernel(keep_ref, got_ref, *outs):
        for s, out in enumerate(outs):
            out[0] = keep_ref[s]
            out[1] = got_ref[s]

    outs = [pltpu.VMEM((2,) + shape[1:], F32)] * shape[0]
    return small_call(kernel, outs, "pair_cores", keep, got)


def put_blocks(args, places, arrays, spaces, subs, name, flops):
    lanes, _, row_count, nmode = args[0].shape[-4:]
    count = len(arrays)

    def kernel(*refs):
        outs, sems = refs[-1 - count : -1], refs[-1]
        refs = refs[len(given) :]
        z, core = lax.axis_index("space"), lax.axis_index("sub")
        copies = []
        for out, group in zip(outs, places, strict=True):
            for s, operand, index in group:
                block = refs[operand] if index is None else refs[operand].at[index]
                for c in range(subs):
                    copy = pltpu.make_async_copy(
                        block.at[c],
                        out.at[:, (z ^ s) * subs + (core ^ c)],
                        sems.at[len(copies)],
                    )
                    copy.start()
                    copies.append(copy)
        for copy in copies:
            copy.wait()

    out = jax.ShapeDtypeStruct((lanes, spaces * subs, 2, row_count, nmode), F32)
    given = [(k, array) for k, array in enumerate(arrays) if array is not None]
    return pl.pallas_call(
        kernel,
        in_specs=[pl.BlockSpec(memory_space=pltpu.HBM)] * len(given)
        + [pl.BlockSpec(memory_space=pltpu.VMEM)] * len(args),
        out_specs=[pl.BlockSpec(memory_space=pltpu.HBM)] * count,
        out_shape=[out] * count,
        input_output_aliases={n: k for n, (k, _) in enumerate(given)},
        scratch_shapes=[pltpu.SemaphoreType.DMA((sum(map(len, places)) * subs,))],
        compiler_params=pltpu.CompilerParams(vmem_limit_bytes=SMALL_LIMIT),
        cost_estimate=pl.CostEstimate(flops=flops, bytes_accessed=1, transcendentals=0),
        name=name,
    )(*(array for _, array in given), *args)


def swap(value, axis, distance):
    size = lax.axis_size(axis)
    return lax.ppermute(value, axis, [(i, i ^ distance) for i in range(size)])


def own_insertions(spaces, subs):
    z, core = lax.axis_index("space"), lax.axis_index("sub")
    return [(z ^ s) * subs + (core ^ c) for c in range(subs) for s in range(spaces)]


def by_owner(sink, source, gamma_index, momenta, pattern, time_pairs, nmode, times, scale):
    spaces, subs, tms = (lax.axis_size(name) for name in ("space", "sub", "tm"))
    order = functools.partial(own_insertions, spaces, subs)
    mine, other = list(range(spaces)), list(range(spaces, 2 * spaces))
    small = (gamma_index, momenta, pattern)

    def send(away, laid, time):
        got = swap(away, "sub", 1)
        keep = later_blocks(gamma_index, pattern, *laid, time, order, mine)
        parts = add_units(keep, got)
        return [parts[0]] + [swap(parts[s], "space", s) for s in ROUND[time]]

    away, sink_mat, turned, *modes = first_blocks(
        (sink, source), small, 0, nmode, order, other, ahead=True
    )
    first = send(away, (sink_mat, turned), 0)
    away, sink_mat, turned = first_blocks(modes, small, 1, nmode, order, other, after=first[:1])
    second = send(away, (sink_mat, turned), 1)
    first = sum_units(first, scale)
    first_other = swap(first, "tm", 1)
    whole = turn_field(first, second[1:])
    second = sum_units(second, scale, [first_other, whole])
    second_other = swap(second, "tm", 1)

    away, keep = split_rows(whole, second, spaces, subs)
    meson = pair_cores(keep, swap(away, "sub", 1))
    own, near, two, three = meson
    two, three, near = (swap(v, "space", s) for v, s in ((two, 2), (three, 3), (near, 1)))
    fields = [first, second, first_other, second_other]
    away, whole = product_rows(time_pairs, fields, spaces, subs, tms)
    got = swap(away, "sub", 1)
    products = pair_cores(keep_rows(whole, spaces, subs), got)
    places = [
        [(0, 0, None), (1, 3, None), (2, 2, None), (3, 1, None)],
        [(0, 4, None)],
    ]
    meson_parts = [own, three, two, near]
    own, near, two, three = products
    two, three, near = (swap(v, "space", s) for v, s in ((two, 2), (three, 3), (near, 1)))
    meson, products = put_blocks(
        meson_parts + [own], places, [None, None], spaces, subs, "put_early", LARGE
    )
    places = [[(1, 1, None), (2, 0, None), (3, 2, None)]]
    (products,) = put_blocks([two, near, three], places, [products], spaces, subs, "put_late", 1)
    return meson, products


def by_rows(sink, source, gamma_index, momenta, pattern, time_pairs, nmode, times, scale):
    axes = ("space", "sub")
    highest = lax.Precision.HIGHEST
    insertions = gamma_index.shape[0]
    partial = jnp.stack(
        [
            first_blocks(
                (sink, source),
                (gamma_index, momenta, pattern),
                time,
                nmode,
                lambda: list(range(insertions)),
                list(range(insertions)),
            )[0]
            for time in range(times)
        ]
    )
    partial = partial.reshape(times, insertions, nmode, 2, nmode).transpose(0, 1, 3, 4, 2)
    meson = lax.psum_scatter(partial * scale, axes, scatter_dimension=3, tiled=True)
    rows = lax.all_gather(meson, "tm", axis=0, tiled=True)
    whole = lax.all_gather(rows, axes, axis=3, tiled=True)
    left, right = rows[time_pairs[:, 0]], whole[time_pairs[:, 1]]

    def multiply(a, b):
        return jnp.einsum("qgik,qgkj->qgij", a, b, precision=highest)

    real = multiply(left[:, :, 0], right[:, :, 0]) - multiply(left[:, :, 1], right[:, :, 1])
    imag = multiply(left[:, :, 0], right[:, :, 1]) + multiply(left[:, :, 1], right[:, :, 0])
    return meson, jnp.stack([real, imag], axis=2) / math.sqrt(nmode)


def local(sink_modes, source_modes, gamma_index, momenta, pattern, time_pairs):
    times, nmode, _, comps, sites = sink_modes.shape
    spaces, subs, tms = (lax.axis_size(name) for name in ("space", "sub", "tm"))

    def as_rows(modes):
        return modes.transpose(0, 1, 3, 2, 4).reshape(times, nmode * comps * 2, sites)

    owners = (
        (spaces, subs, tms, times) == (4, 2, 2, 2)
        and gamma_index.shape[0] == spaces * subs
        and time_pairs.shape[0] == times
    )
    plan = by_owner if owners else by_rows
    arrays = (as_rows(sink_modes), as_rows(source_modes), gamma_index, momenta.T, pattern)
    scale = 1.0 / math.sqrt(3 * sites * spaces * subs)
    return plan(*arrays, time_pairs, nmode, times, scale)


def solution(mesh):
    rows = P(("grp", "tm"), None, None, None, ("space", "sub"))
    in_specs = (rows, rows, P(), P(), P("tm", ("space", "sub")), P("tm", None))
    out_specs = (P(("grp", "tm"), None, None, ("space", "sub"), None),) * 2
    return jax.shard_map(local, mesh=mesh, in_specs=in_specs, out_specs=out_specs, check_vma=False)
```

```python
import functools
import math

import jax
import jax.numpy as jnp
import numpy as np
from jax import lax
from jax.experimental import pallas as pl
from jax.experimental.pallas import tpu as pltpu
from jax.sharding import PartitionSpec as P

LAT = 96
CLASSES = 4
F32 = jnp.float32
BF16 = jnp.bfloat16
VMEM_LIMIT = 16 * 2**20
SMALL_LIMIT = 4 * 2**20
ROUND = ((3, 1, 2), (1, 2, 3))
LARGE = 10**11


def build_gammas():
    sigmas = [
        np.array([[0, 1], [1, 0]], dtype=complex),
        np.array([[0, -1j], [1j, 0]], dtype=complex),
        np.array([[1, 0], [0, -1]], dtype=complex),
    ]
    zero, one = np.zeros((2, 2), dtype=complex), np.eye(2, dtype=complex)
    gammas = [np.block([[zero, 1j * s], [-1j * s, zero]]) for s in sigmas]
    gammas.append(np.block([[zero, one], [one, zero]]))
    tables = []
    for subset in range(16):
        product = np.eye(4, dtype=complex)
        for factor in range(4):
            if subset >> factor & 1:
                product = product @ gammas[factor]
        tables.append(product)
    return tables


def gamma_codes():
    words = [0, 0, 0, 0]
    for index, table in enumerate(build_gammas()):
        flip = gamma_flip(index)
        for row in range(4):
            entry = table[row, row ^ flip]
            power = [k for k in range(4) if abs(entry - 1j**k) < 1e-6]
            assert len(power) == 1 and np.count_nonzero(table[row]) == 1
            words[index // 4] |= power[0] << (8 * (index % 4) + 2 * row)
    return [word - 2**32 if word >= 2**31 else word for word in words]


def gamma_flip(index):
    b1, b2, b3, b4 = (index & 1, (index >> 1) & 1, (index >> 2) & 1, (index >> 3) & 1)
    return (b1 ^ b2) | ((b1 ^ b2 ^ b3 ^ b4) << 1)


def site_coords(site):
    coords = []
    for axis in range(3):
        total = jnp.zeros_like(site)
        for level in range(6):
            total = total + (((site >> (3 * level + axis)) & 1) << level)
        coords.append(total)
    return coords


def wave_phases(insertions, momenta_ref, pattern_row):
    sites = pattern_row.shape[1]
    fours = insertions // CLASSES
    first_site = (
        lax.axis_index("space") * lax.axis_size("sub") + lax.axis_index("sub")
    ) * sites
    site = lax.broadcasted_iota(jnp.int32, (1, sites), 1) + first_site
    coords = site_coords(site)
    rows = []
    for four in range(fours):
        wave = jnp.zeros_like(site)
        for axis in range(3):
            chosen = jnp.zeros_like(site)
            for kind in range(CLASSES):
                chosen = jnp.where(
                    pattern_row == kind, momenta_ref[axis, four * CLASSES + kind], chosen
                )
            wave = wave + coords[axis] * chosen
        laps = jnp.floor((wave.astype(F32) + 0.5) * (1.0 / LAT)).astype(jnp.int32)
        rows.append((wave - LAT * laps).astype(F32) * (2.0 * math.pi / LAT))
    angle = jnp.concatenate(rows, axis=0)
    return jnp.cos(angle), jnp.sin(angle)


def multiply_slots(
    insertions, slots, gamma_ref, pattern_row, sink_mat, turned, buffers, out
):
    _, comps, _, nmode, sites = turned.shape
    colours = comps // 4
    words = gamma_codes()
    parts = len(buffers)
    per_part = comps // parts
    plan = []
    for slot in slots:
        g = insertions[slot]
        index = gamma_ref[g]
        word = jnp.int32(words[3])
        for step in (2, 1, 0):
            word = jnp.where(index < 4 * (step + 1), jnp.int32(words[step]), word)
        code = word >> (8 * (index & 3))
        mask = jnp.where(pattern_row == lax.rem(g, CLASSES), 1.0, 0.0)
        rows = []
        for spin in range(4):
            power = (code >> (2 * spin)) & 3
            real_sign = jnp.where((power == 0) | (power == 3), 1.0, -1.0)
            imag_sign = jnp.where(power < 2, 1.0, -1.0)
            rows.append(
                (
                    power & 1,
                    (gamma_flip(index) ^ spin) * colours,
                    (mask * real_sign).astype(BF16),
                    (mask * imag_sign).astype(BF16),
                )
            )
        plan.append((g // CLASSES, rows))
    for part in range(parts):
        buffer = buffers[part]
        for k, (four, rows) in enumerate(plan):
            base = k * nmode
            for step in range(per_part):
                comp = part * per_part + step
                odd, taken, real_row, imag_row = rows[comp // colours]
                source = taken + comp % colours
                at = step * 2 * sites
                buffer[base : base + nmode, at : at + sites] = (
                    turned[four, source, odd] * real_row
                )
                buffer[base : base + nmode, at + sites : at + 2 * sites] = (
                    turned[four, source, 1 - odd] * imag_row
                )
        width = per_part * 2 * sites
        block = lax.dot_general(
            buffer[...],
            sink_mat[:, part * width : (part + 1) * width],
            (((1,), (1,)), ((), ())),
            preferred_element_type=F32,
        ).reshape(out.shape)
        out[...] = block if part == 0 else out[...] + block


def first_kernel(order, time, slots, chunks, ahead, loaded, waits, *refs):
    sink_src, source_src, gamma_hbm, momenta_hbm, pattern_hbm, *refs = refs
    out, sink_mat, turned, *refs = refs[waits:]
    nexts, refs = (refs[:2], refs[2:]) if ahead else ([], refs)
    sink_stage, source_stage, gamma_ref, momenta_ref, pattern_ref, *refs = refs
    small_sems, big_sems, next_sems, *refs = refs
    raws, buffers = ([sink_src, source_src], refs) if loaded else (refs[:2], refs[2:])
    rows, sites = sink_stage.shape
    fours, _, _, nmode, _ = turned.shape
    per_mode = rows // nmode
    comps = per_mode // 2
    insertions = order()
    height = rows // chunks

    small = [
        pltpu.make_async_copy(src, dst, small_sems.at[k])
        for k, (src, dst) in enumerate(
            [(momenta_hbm, momenta_ref), (pattern_hbm, pattern_ref), (gamma_hbm, gamma_ref)]
        )
    ]
    big, later = [], []
    if not loaded:
        for which, (src, dst) in enumerate(zip((sink_src, source_src), raws)):
            for k in range(chunks):
                part = pl.ds(k * height, height)
                sem = big_sems.at[which * chunks + k]
                big.append(pltpu.make_async_copy(src.at[time, part], dst.at[part], sem))
    for k, (src, dst) in enumerate(zip((sink_src, source_src), nexts)):
        later.append(pltpu.make_async_copy(src.at[time + 1], dst, next_sems.at[k]))
    for copy in small + big + later:
        copy.start()

    def stage(which, dst):
        for k in range(chunks):
            part = slice(k * height, (k + 1) * height)
            if not loaded:
                big[which * chunks + k].wait()
            dst[part] = raws[which][part].astype(F32)

    stage(0, sink_stage)
    for comp in range(comps):
        at = comp * 2 * sites
        real = sink_stage[pl.ds(2 * comp, nmode, stride=per_mode), :].astype(BF16)
        imag = sink_stage[pl.ds(2 * comp + 1, nmode, stride=per_mode), :].astype(BF16)
        sink_mat[0:nmode, at : at + sites] = real
        sink_mat[0:nmode, at + sites : at + 2 * sites] = imag
        sink_mat[nmode:, at : at + sites] = -imag
        sink_mat[nmode:, at + sites : at + 2 * sites] = real
    for copy in small:
        copy.wait()
    pattern_row = pattern_ref[time : time + 1, :]
    cosine, sine = wave_phases(fours * CLASSES, momenta_ref, pattern_row)
    stage(1, source_stage)
    for comp in range(comps):
        real = source_stage[pl.ds(2 * comp, nmode, stride=per_mode), :]
        imag = source_stage[pl.ds(2 * comp + 1, nmode, stride=per_mode), :]
        for four in range(fours):
            cos_row, sin_row = cosine[four : four + 1], sine[four : four + 1]
            turned[four, comp, 0] = (real * cos_row - imag * sin_row).astype(BF16)
            turned[four, comp, 1] = (real * sin_row + imag * cos_row).astype(BF16)
    multiply_slots(insertions, slots, gamma_ref, pattern_row, sink_mat, turned, buffers, out)
    for copy in later:
        copy.wait()


def block_cost(slots, nmode, depth):
    return pl.CostEstimate(
        flops=100 * slots * nmode * nmode * depth,
        bytes_accessed=8 * nmode * depth,
        transcendentals=0,
    )


def product_buffers(slots, nmode, depth):
    parts = 2
    return [pltpu.VMEM((slots * nmode, depth // parts), BF16)] * parts


def first_blocks(modes, small, time, nmode, order, slots, ahead=False, after=()):
    rows, sites = modes[0].shape[-2:]
    loaded = modes[0].ndim == 2
    comps = rows // nmode // 2
    depth = comps * 2 * sites
    chunks = 4 if rows % 64 == 0 else 1
    gamma_index, momenta, pattern = small
    fours = gamma_index.shape[0] // CLASSES
    raw = [pltpu.VMEM((rows, sites), BF16)] * 2
    where = pltpu.VMEM if loaded else pltpu.HBM
    if not loaded:
        modes = in_hbm(modes)
    return pl.pallas_call(
        functools.partial(first_kernel, order, time, slots, chunks, ahead, loaded, len(after)),
        in_specs=[pl.BlockSpec(memory_space=where)] * 2
        + [pl.BlockSpec(memory_space=pltpu.HBM)] * 3
        + [pl.BlockSpec(memory_space=pl.ANY)] * len(after),
        out_shape=[
            pltpu.VMEM((len(slots), nmode, 2 * nmode), F32),
            pltpu.VMEM((2 * nmode, depth), BF16),
            pltpu.VMEM((fours, comps, 2, nmode, sites), BF16),
        ]
        + (raw if ahead else []),
        scratch_shapes=[
            pltpu.VMEM((rows, sites), F32),
            pltpu.VMEM((rows, sites), F32),
            pltpu.SMEM(gamma_index.shape, jnp.int32),
            pltpu.SMEM(momenta.shape, jnp.int32),
            pltpu.VMEM(pattern.shape, jnp.int32),
            pltpu.SemaphoreType.DMA((3,)),
            pltpu.SemaphoreType.DMA((2 * chunks,)),
            pltpu.SemaphoreType.DMA((2,)),
        ]
        + ([] if loaded else raw)
        + product_buffers(len(slots), nmode, depth),
        compiler_params=pltpu.CompilerParams(vmem_limit_bytes=VMEM_LIMIT),
        cost_estimate=block_cost(len(slots), nmode, depth),
        name="first_blocks",
    )(*modes, *in_hbm(small), *after)


def in_hbm(arrays):
    return [pltpu.with_memory_space_constraint(a, pltpu.HBM) for a in arrays]


def later_kernel(order, time, slots, gamma_ref, pattern_ref, sink_mat, turned, out, *buffers):
    pattern_row = pattern_ref[time : time + 1, :]
    multiply_slots(order(), slots, gamma_ref, pattern_row, sink_mat, turned, buffers, out)


def later_blocks(gamma_index, pattern, sink_mat, turned, time, order, slots):
    nmode, depth = turned.shape[3], sink_mat.shape[1]
    return pl.pallas_call(
        functools.partial(later_kernel, order, time, slots),
        in_specs=[pl.BlockSpec(memory_space=pltpu.SMEM)]
        + [pl.BlockSpec(memory_space=pltpu.VMEM)] * 3,
        out_shape=pltpu.VMEM((len(slots), nmode, 2 * nmode), F32),
        scratch_shapes=product_buffers(len(slots), nmode, depth),
        compiler_params=pltpu.CompilerParams(vmem_limit_bytes=VMEM_LIMIT),
        cost_estimate=block_cost(len(slots), nmode, depth),
        name="later_blocks",
    )(gamma_index, pattern, sink_mat, turned)


def small_call(kernel, outs, name, *args, flops=1, after=(), scratch=()):
    return pl.pallas_call(
        kernel,
        in_specs=[pl.BlockSpec(memory_space=pltpu.VMEM)] * len(args)
        + [pl.BlockSpec(memory_space=pl.ANY)] * len(after),
        out_shape=outs,
        scratch_shapes=scratch,
        compiler_params=pltpu.CompilerParams(vmem_limit_bytes=SMALL_LIMIT),
        cost_estimate=pl.CostEstimate(flops=flops, bytes_accessed=1, transcendentals=0),
        name=name,
    )(*args, *after)


def add_units(keep, got):
    def kernel(keep_ref, got_ref, *outs):
        for slot, out in enumerate(outs):
            out[...] = keep_ref[slot] + got_ref[slot]

    units, rows, columns = keep.shape
    outs = [pltpu.VMEM((rows, columns), F32)] * units
    return small_call(kernel, outs, "add_cores", keep, got)


def sum_units(terms, scale, after=()):
    def kernel(*refs):
        total = refs[0][...]
        for ref in refs[1 : len(terms)]:
            total = total + ref[...]
        refs[-1][...] = total * scale

    out = pltpu.VMEM(terms[0].shape, F32)
    return small_call(kernel, out, "sum_chips", *terms, after=after)


def write_rows(whole, lane, spaces, subs, cores, outs):
    row_count = outs[0].shape[3]
    z, core = lax.axis_index("space"), lax.axis_index("sub")
    for c, out in zip(cores, outs, strict=True):
        for s in range(spaces):
            start = pl.multiple_of(((z ^ s) * subs + (core ^ c)) * row_count, row_count)
            for part in range(2):
                out[s, lane, part] = whole[part, pl.ds(start, row_count), :]


def turn(matrix, whole):
    nmode = matrix.shape[1] // 2
    for part in range(2):
        whole[part] = matrix[:, part * nmode : (part + 1) * nmode].T


def turn_field(field, after):
    def kernel(field_ref, *refs):
        turn(field_ref[...], refs[-1])

    nmode = field.shape[0]
    out = pltpu.VMEM((2, nmode, nmode), F32)
    return small_call(kernel, out, "turn_field", field, flops=LARGE, after=after)


def split_rows(whole, field, spaces, subs):
    nmode = whole.shape[1]

    def kernel(whole_ref, field_ref, away, keep, staging):
        turn(field_ref[...], staging)
        for lane, source in enumerate((whole_ref, staging)):
            write_rows(source, lane, spaces, subs, [1, 0], [away, keep])

    outs = [pltpu.VMEM((spaces, 2, 2, nmode // (spaces * subs), nmode), F32)] * 2
    scratch = [pltpu.VMEM((2, nmode, nmode), F32)]
    return small_call(kernel, outs, "split_rows", whole, field, scratch=scratch, flops=LARGE)


def split_dot(a, b):
    a_high, b_high = a.astype(BF16), b.astype(BF16)
    a_low = (a - a_high.astype(F32)).astype(BF16)
    b_low = (b - b_high.astype(F32)).astype(BF16)

    def dot(x, y):
        return lax.dot_general(x, y, (((1,), (0,)), ((), ())), preferred_element_type=F32)

    small = dot(a_low, b_low) + dot(a_low, b_high) + dot(a_high, b_low)
    return small + dot(a_high, b_high)


def product_kernel(spaces, subs, tms, pairs_ref, *refs):
    fields, (away, whole, held) = refs[:-3], refs[-3:]
    nmode = fields[0].shape[0]
    times = len(fields) // tms
    mine = lax.axis_index("tm")
    for other in range(tms):
        for time in range(times):
            held[(mine ^ other) * times + time] = fields[other * times + time][...]
    for pair in range(pairs_ref.shape[0]):
        left, right = held[pairs_ref[pair, 0]], held[pairs_ref[pair, 1]]
        swapped = jnp.concatenate([-left[:, nmode:], left[:, :nmode]], axis=1)
        result = split_dot(right, jnp.concatenate([left, swapped], axis=0)) * (
            1.0 / math.sqrt(nmode)
        )
        turn(result, whole.at[pair])
        write_rows(whole.at[pair], pair, spaces, subs, [1], [away])


def product_rows(time_pairs, fields, spaces, subs, tms):
    nmode, pairs = fields[0].shape[0], time_pairs.shape[0]
    shape = (spaces, pairs, 2, nmode // (spaces * subs), nmode)
    return pl.pallas_call(
        functools.partial(product_kernel, spaces, subs, tms),
        in_specs=[pl.BlockSpec(memory_space=pltpu.SMEM)]
        + [pl.BlockSpec(memory_space=pltpu.VMEM)] * len(fields),
        out_shape=[pltpu.VMEM(shape, F32), pltpu.VMEM((pairs, 2, nmode, nmode), F32)],
        scratch_shapes=[pltpu.VMEM((len(fields), nmode, 2 * nmode), F32)],
        compiler_params=pltpu.CompilerParams(vmem_limit_bytes=SMALL_LIMIT),
        cost_estimate=pl.CostEstimate(
            flops=8 * pairs * nmode**3, bytes_accessed=64 * nmode * nmode, transcendentals=0
        ),
        name="products",
    )(time_pairs, *fields)


def keep_rows(whole, spaces, subs):
    lanes, _, nmode, _ = whole.shape

    def kernel(whole_ref, out):
        for lane in range(lanes):
            write_rows(whole_ref.at[lane], lane, spaces, subs, [0], [out])

    out = pltpu.VMEM((spaces, lanes, 2, nmode // (spaces * subs), nmode), F32)
    return small_call(kernel, out, "keep_rows", whole, flops=LARGE)


def pair_cores(keep, got):
    shape = keep.shape

    def kernel(keep_ref, got_ref, *outs):
        for s, out in enumerate(outs):
            out[0] = keep_ref[s]
            out[1] = got_ref[s]

    outs = [pltpu.VMEM((2,) + shape[1:], F32)] * shape[0]
    return small_call(kernel, outs, "pair_cores", keep, got)


def put_blocks(args, places, arrays, spaces, subs, name, flops):
    lanes, _, row_count, nmode = args[0].shape[-4:]
    count = len(arrays)

    def kernel(*refs):
        outs, sems = refs[-1 - count : -1], refs[-1]
        refs = refs[len(given) :]
        z, core = lax.axis_index("space"), lax.axis_index("sub")
        copies = []
        for out, group in zip(outs, places, strict=True):
            for s, operand, index in group:
                block = refs[operand] if index is None else refs[operand].at[index]
                for c in range(subs):
                    copy = pltpu.make_async_copy(
                        block.at[c],
                        out.at[:, (z ^ s) * subs + (core ^ c)],
                        sems.at[len(copies)],
                    )
                    copy.start()
                    copies.append(copy)
        for copy in copies:
            copy.wait()

    out = jax.ShapeDtypeStruct((lanes, spaces * subs, 2, row_count, nmode), F32)
    given = [(k, array) for k, array in enumerate(arrays) if array is not None]
    return pl.pallas_call(
        kernel,
        in_specs=[pl.BlockSpec(memory_space=pltpu.HBM)] * len(given)
        + [pl.BlockSpec(memory_space=pltpu.VMEM)] * len(args),
        out_specs=[pl.BlockSpec(memory_space=pltpu.HBM)] * count,
        out_shape=[out] * count,
        input_output_aliases={n: k for n, (k, _) in enumerate(given)},
        scratch_shapes=[pltpu.SemaphoreType.DMA((sum(map(len, places)) * subs,))],
        compiler_params=pltpu.CompilerParams(vmem_limit_bytes=SMALL_LIMIT),
        cost_estimate=pl.CostEstimate(flops=flops, bytes_accessed=1, transcendentals=0),
        name=name,
    )(*(array for _, array in given), *args)


def swap(value, axis, distance):
    size = lax.axis_size(axis)
    return lax.ppermute(value, axis, [(i, i ^ distance) for i in range(size)])


def own_insertions(spaces, subs):
    z, core = lax.axis_index("space"), lax.axis_index("sub")
    return [(z ^ s) * subs + (core ^ c) for c in range(subs) for s in range(spaces)]


def by_owner(sink, source, gamma_index, momenta, pattern, time_pairs, nmode, times, scale):
    spaces, subs, tms = (lax.axis_size(name) for name in ("space", "sub", "tm"))
    order = functools.partial(own_insertions, spaces, subs)
    mine, other = list(range(spaces)), list(range(spaces, 2 * spaces))
    small = (gamma_index, momenta, pattern)

    def send(away, laid, time):
        got = swap(away, "sub", 1)
        keep = later_blocks(gamma_index, pattern, *laid, time, order, mine)
        parts = add_units(keep, got)
        return [parts[0]] + [swap(parts[s], "space", s) for s in ROUND[time]]

    away, sink_mat, turned, *modes = first_blocks(
        (sink, source), small, 0, nmode, order, other, ahead=True
    )
    first = send(away, (sink_mat, turned), 0)
    away, sink_mat, turned = first_blocks(modes, small, 1, nmode, order, other, after=first[:1])
    second = send(away, (sink_mat, turned), 1)
    first = sum_units(first, scale)
    first_other = swap(first, "tm", 1)
    whole = turn_field(first, second[1:])
    second = sum_units(second, scale, [first_other, whole])
    second_other = swap(second, "tm", 1)

    away, keep = split_rows(whole, second, spaces, subs)
    meson = pair_cores(keep, swap(away, "sub", 1))
    own, near, two, three = meson
    two, three, near = (swap(v, "space", s) for v, s in ((two, 2), (three, 3), (near, 1)))
    fields = [first, second, first_other, second_other]
    away, whole = product_rows(time_pairs, fields, spaces, subs, tms)
    got = swap(away, "sub", 1)
    products = pair_cores(keep_rows(whole, spaces, subs), got)
    places = [
        [(0, 0, None), (1, 3, None), (2, 2, None), (3, 1, None)],
        [(0, 4, None)],
    ]
    meson_parts = [own, three, two, near]
    own, near, two, three = products
    two, three, near = (swap(v, "space", s) for v, s in ((two, 2), (three, 3), (near, 1)))
    meson, products = put_blocks(
        meson_parts + [own], places, [None, None], spaces, subs, "put_early", LARGE
    )
    places = [[(1, 1, None), (2, 0, None), (3, 2, None)]]
    (products,) = put_blocks([two, near, three], places, [products], spaces, subs, "put_late", 1)
    return meson, products


def by_rows(sink, source, gamma_index, momenta, pattern, time_pairs, nmode, times, scale):
    axes = ("space", "sub")
    highest = lax.Precision.HIGHEST
    insertions = gamma_index.shape[0]
    partial = jnp.stack(
        [
            first_blocks(
                (sink, source),
                (gamma_index, momenta, pattern),
                time,
                nmode,
                lambda: list(range(insertions)),
                list(range(insertions)),
            )[0]
            for time in range(times)
        ]
    )
    partial = partial.reshape(times, insertions, nmode, 2, nmode).transpose(0, 1, 3, 4, 2)
    meson = lax.psum_scatter(partial * scale, axes, scatter_dimension=3, tiled=True)
    rows = lax.all_gather(meson, "tm", axis=0, tiled=True)
    whole = lax.all_gather(rows, axes, axis=3, tiled=True)
    left, right = rows[time_pairs[:, 0]], whole[time_pairs[:, 1]]

    def multiply(a, b):
        return jnp.einsum("qgik,qgkj->qgij", a, b, precision=highest)

    real = multiply(left[:, :, 0], right[:, :, 0]) - multiply(left[:, :, 1], right[:, :, 1])
    imag = multiply(left[:, :, 0], right[:, :, 1]) + multiply(left[:, :, 1], right[:, :, 0])
    return meson, jnp.stack([real, imag], axis=2) / math.sqrt(nmode)


def local(sink_modes, source_modes, gamma_index, momenta, pattern, time_pairs):
    times, nmode, _, comps, sites = sink_modes.shape
    spaces, subs, tms = (lax.axis_size(name) for name in ("space", "sub", "tm"))

    def as_rows(modes):
        return modes.transpose(0, 1, 3, 2, 4).reshape(times, nmode * comps * 2, sites)

    owners = (
        (spaces, subs, tms, times) == (4, 2, 2, 2)
        and gamma_index.shape[0] == spaces * subs
        and time_pairs.shape[0] == times
    )
    plan = by_owner if owners else by_rows
    arrays = (as_rows(sink_modes), as_rows(source_modes), gamma_index, momenta.T, pattern)
    scale = 1.0 / math.sqrt(3 * sites * spaces * subs)
    return plan(*arrays, time_pairs, nmode, times, scale)


def solution(mesh):
    rows = P(("grp", "tm"), None, None, None, ("space", "sub"))
    in_specs = (rows, rows, P(), P(), P("tm", ("space", "sub")), P("tm", None))
    out_specs = (P(("grp", "tm"), None, None, ("space", "sub"), None),) * 2
    return jax.shard_map(local, mesh=mesh, in_specs=in_specs, out_specs=out_specs, check_vma=False)
```
